32 devices in a mesh: scan: 4 (over x, core), obj: 8 (over z, y).
Axes of the slice: x: 2, y: 2, z: 4, core: 2. Of those that a mesh axis runs over, the one named last changes fastest.
Arguments:
- object_slices: float32 [2, 2, 2048, 2048], P(None, None, 'obj'), may hold values from -4 to 4
- probe: float32 [2, 2, 256, 256], replicated, may hold values from -6 to 6
- measured: bfloat16 [4, 8, 2, 256, 256], P('scan', 'obj'), may hold values from 0 to 4
- positions: int32 [4, 8, 2, 2], P('scan', 'obj'), may hold values from 0 to 1792, as said below
- counts: int32 [4, 8], P('scan', 'obj'), may hold values from 0 to 2, as said below
Outputs:
- object_grad: float32 [2, 2, 2048, 2048], P(None, None, 'obj', 'scan')
- probe_grad: float32 [2, 2, 256, 256], P(None, None, 'obj', 'scan')
The draws below stay inside these ranges and needn't reach their ends.
Inputs may be any that keep to these rules, and one draw needn't show every extreme that they name: In every tile o the counts over the 4 batches sum to exactly 4, and some batch of every tile has 2 live patterns. `positions`: the row offset is below 256, the column at most 1792.
All inputs are finite; a program needn't handle non-finite values.
Results may differ from the reference program's by a relative error of at most 0.013.
Values may be sent and summed in bfloat16 or wider, within the bound.
No kernel may reach another device: no remote copies, remote signals or barrier semaphores. Data moves between devices by JAX's collectives and lax.ppermute only.
A program may use at most 128 MiB of HBM per device.

```python
import math
import jax
import jax.numpy as jnp
from jax import lax

N = 256
M = 2
L = 2
R = 256
W = 2048
P_DEV = 2
H = 2048
LIVE = 32
N_SCAN = 4
N_OBJ = 8


def draw_positions(key, part):
    key_rows, key_cols = jax.random.split(jax.random.fold_in(key, 11))
    grid_shape = (N_SCAN, N_OBJ, P_DEV)
    row_vals = jax.random.randint(key_rows, grid_shape, 0, R)
    col_vals = jax.random.randint(key_cols, grid_shape, 0, W - N + 1)
    row_vals = row_vals.at[0, 0, 0].set(R - 1).at[0, 0, 1].set(0)
    col_vals = col_vals.at[0, 0, 0].set(W - N).at[0, 0, 1].set(0)
    return jnp.stack([row_vals, col_vals], axis=-1).astype(jnp.int32)


def draw_counts(key, part):
    key_pairs, key_perm = jax.random.split(jax.random.fold_in(key, 23))
    pair_count = N_SCAN // 2
    lower = jax.random.randint(key_pairs, (pair_count, N_OBJ), 0, P_DEV + 1)
    lower = lower.at[0].set(0)
    paired = jnp.stack([lower, P_DEV - lower], axis=1).reshape(N_SCAN, N_OBJ)
    perm_keys = jax.random.split(key_perm, N_OBJ)
    orders = jax.vmap(lambda one_key: jax.random.permutation(one_key, N_SCAN))(perm_keys)
    shuffled = jnp.take_along_axis(paired, orders.T.astype(jnp.int32), axis=0)
    return shuffled.astype(jnp.int32)


def shard_levels(rng, extent, pieces, smallest, largest):
    loudness, own = 1.0, jax.random.fold_in(rng, 6)
    for dim, blocks in pieces:
        steps = jnp.exp(jax.random.uniform(jax.random.fold_in(own, dim), (blocks,), jnp.float32, smallest / len(pieces), largest / len(pieces)))
        loudness = loudness * jnp.repeat(steps, extent[dim] // blocks).reshape([-1 if axis == dim else 1 for axis in range(len(extent))])
    return loudness


def bell_draw(key, shape, scale, most, cuts=(), kind=jnp.bfloat16):
    level = shard_levels(key, shape, cuts, -0.22, 0.18) if cuts else 1.0
    drawn = jax.random.normal(key, shape, jnp.float32) * scale * level
    return jnp.minimum(jnp.maximum(drawn, -most), most).astype(kind)


def setup_inputs(seed: int = 0) -> dict:
    key_list = jax.random.split(jax.random.key(seed), 6)
    object_slices = bell_draw(key_list[0], (L, 2, H, W), 0.7, 4.0, ((2, 8),), jnp.float32)
    probe = bell_draw(key_list[1], (M, 2, N, N), 1.0, 6.0, (), jnp.float32)
    measured = jnp.clip(4.0 * jax.random.uniform(key_list[2], (N_SCAN, N_OBJ, P_DEV, N, N), jnp.float32) ** shard_levels(key_list[2], (N_SCAN, N_OBJ, P_DEV, N, N), ((0, 4), (1, 8)), -0.2, 0.2), 0.0, 4.0).astype(jnp.bfloat16)
    positions = draw_positions(jax.random.fold_in(key_list[5], 71), 0)
    counts = draw_counts(jax.random.fold_in(key_list[5], 71), 0)
    return {"object_slices": object_slices, "probe": probe, "measured": measured, "positions": positions, "counts": counts}


HIGHEST_MODE = lax.Precision.HIGHEST

def dft_matrix(length, sign):
    index_row = jnp.arange(length, dtype=jnp.int32)
    product = index_row[:, None] * index_row[None, :] % length
    angles = product.astype(jnp.float32) * (2.0 * math.pi / length)
    factor = 1.0 / math.sqrt(length)
    real_part = jnp.cos(angles) * factor
    imag_part = sign * jnp.sin(angles) * factor
    stacked = jnp.stack([jnp.stack([real_part, -imag_part]), jnp.stack([imag_part, real_part])])
    return stacked.astype(jnp.bfloat16)

def fresnel_kernel(length):
    index_row = jnp.arange(length, dtype=jnp.int32)
    freqs = jnp.where(index_row < length // 2, index_row, index_row - length)
    squares = freqs * freqs
    summed = (squares[:, None] + squares[None, :]) % (4 * length)
    phases = summed.astype(jnp.float32) * (2.0 * math.pi / (4 * length))
    return jnp.stack([jnp.cos(phases), -jnp.sin(phases)])

def rounded(values):
    return lax.optimization_barrier(values.astype(jnp.bfloat16)).astype(jnp.float32)

def transform(field_in, matrix):
    weights = matrix.astype(jnp.float32)
    partial_out = jnp.einsum('pqab,qbc->pac', weights, rounded(field_in), precision=HIGHEST_MODE)
    return jnp.einsum('qab,pqbc->pac', rounded(partial_out), weights, precision=HIGHEST_MODE)

def complex_mul(first_op, second_op):
    return jnp.stack([first_op[0] * second_op[0] - first_op[1] * second_op[1], first_op[0] * second_op[1] + first_op[1] * second_op[0]])

def conj_mul(first_op, second_op):
    return jnp.stack([first_op[0] * second_op[0] + first_op[1] * second_op[1], first_op[0] * second_op[1] - first_op[1] * second_op[0]])

def pattern_terms(patches, probe, pattern_data, weight, forward, inverse, kernel):
    layers = patches.shape[0]

    def forward_mode(mode_probe):
        arrivals = [mode_probe]
        field_now = complex_mul(mode_probe, patches[0])
        for layer_idx in range(1, layers):
            spectrum = transform(field_now, forward)
            field_now = transform(complex_mul(kernel, spectrum), inverse)
            arrivals.append(field_now)
            field_now = complex_mul(field_now, patches[layer_idx])
        return (transform(field_now, forward), jnp.stack(arrivals))
    far_field, arrivals = jax.vmap(forward_mode)(probe)
    intensity = lax.optimization_barrier(jnp.sum(far_field[:, 0] ** 2 + far_field[:, 1] ** 2, axis=0))
    misfit = (intensity - pattern_data.astype(jnp.float32)) * weight

    def back_mode(mode_far, mode_arrivals):
        adjoint = transform(misfit[None] * mode_far, inverse)
        layer_grads = [None] * layers
        for layer_idx in reversed(range(layers)):
            layer_grads[layer_idx] = conj_mul(mode_arrivals[layer_idx], adjoint)
            adjoint = conj_mul(patches[layer_idx], adjoint)
            if layer_idx > 0:
                spectrum = transform(adjoint, forward)
                adjoint = transform(conj_mul(kernel, spectrum), inverse)
        return (jnp.stack(layer_grads), adjoint)
    patch_grads, probe_grads = jax.vmap(back_mode)(far_field, arrivals)
    return (lax.optimization_barrier(jnp.sum(patch_grads, axis=0)), probe_grads)

def reference(object_slices, probe, measured, positions, counts):
    forward = dft_matrix(N, -1.0)
    inverse = dft_matrix(N, 1.0)
    kernel = fresnel_kernel(N)
    extended = jnp.concatenate([object_slices, object_slices[:, :, :N]], axis=2)
    count_all = N_SCAN * N_OBJ * P_DEV
    flat_measured = measured.reshape(count_all, N, N)
    flat_positions = positions.reshape(count_all, 2)
    flat_counts = counts.reshape(N_SCAN * N_OBJ)
    zero_index = jnp.zeros((), jnp.int32)

    def step_fn(state_in, inputs):
        grad_ext, probe_sum = state_in
        pattern_id, pattern_data, pattern_pos = inputs
        group_id = pattern_id // P_DEV
        tile_id = group_id % N_OBJ
        slot_id = pattern_id % P_DEV
        weight = (slot_id < flat_counts[group_id]).astype(jnp.float32)
        row_start = (tile_id * R + pattern_pos[0]).astype(jnp.int32)
        col_start = pattern_pos[1].astype(jnp.int32)
        corner = (zero_index, zero_index, row_start, col_start)
        patches = lax.dynamic_slice(extended, corner, (L, 2, N, N))
        patch_grad, probe_grad = pattern_terms(patches, probe, pattern_data, weight, forward, inverse, kernel)
        current = lax.dynamic_slice(grad_ext, corner, (L, 2, N, N))
        grad_ext = lax.dynamic_update_slice(grad_ext, current + patch_grad, corner)
        return ((grad_ext, probe_sum + probe_grad), None)
    initial = (jnp.zeros((L, 2, H + N, W), jnp.float32), jnp.zeros(probe.shape, jnp.float32))
    pattern_ids = jnp.arange(count_all, dtype=jnp.int32)
    (grad_ext, probe_sum), leftover = lax.scan(step_fn, initial, (pattern_ids, flat_measured, flat_positions))
    object_grad = grad_ext[:, :, :H].at[:, :, :N].add(grad_ext[:, :, H:])
    return (object_grad, probe_sum * (1.0 / math.sqrt(LIVE)))
```

```python
import functools
import math

import jax
import jax.numpy as jnp
import ml_dtypes
import numpy as np
from jax import lax
from jax.experimental import pallas as pl
from jax.experimental.pallas import tpu as pltpu
from jax.sharding import PartitionSpec as P

AXES = ("scan", "obj")
CORES = 2
MIB = 1 << 20


def dft_tables(length):
    index = np.arange(length)
    angles = (index[:, None] * index[None, :] % length) * (2.0 * math.pi / length)
    parts = np.stack([np.cos(angles), -np.sin(angles)]) / math.sqrt(length)
    return parts.astype(np.float32).astype(ml_dtypes.bfloat16).astype(np.float32)


def fresnel_tables(length):
    index = np.arange(length)
    freqs = np.where(index < length // 2, index, index - length)
    squares = freqs * freqs
    phases = ((squares[:, None] + squares[None, :]) % (4 * length)) * (2.0 * math.pi / (4 * length))
    return np.stack([np.cos(phases), -np.sin(phases)]).astype(np.float32)


def send(block, scan_of, obj_step):
    n_scan, n_obj = lax.axis_size("scan"), lax.axis_size("obj")
    route = []
    for s in range(n_scan):
        for o in range(n_obj):
            route.append((s * n_obj + o, scan_of(s) % n_scan * n_obj + (o + obj_step) % n_obj))
    return lax.ppermute(block, AXES, route)


def fill_table(table, infos, me, n_scan):
    for k, info in enumerate(infos):
        row = lax.rem(me - k + n_scan, n_scan)
        for j in range(5):
            table[row, j] = info[j]


def assigned(table, target, n_scan):
    idle = table[target, 0] == 0
    rank = jnp.int32(0)
    for a in range(n_scan):
        rank += jnp.where((table[a, 0] == 0) & (a < target), 1, 0)
    source = jnp.int32(target)
    seen = jnp.int32(0)
    for a in range(n_scan):
        full = table[a, 0] == 2
        source = jnp.where(idle & full & (seen == rank), a, source)
        seen += jnp.where(full, 1, 0)
    slot = jnp.where(idle, 1, 0)
    row = jnp.where(idle, table[source, 3], table[source, 1])
    col = jnp.where(idle, table[source, 4], table[source, 2])
    return source, slot, row, col


def column_block(col, length, tile_cols):
    base = jnp.minimum(lax.div(col, length), tile_cols // length - 2)
    return base, col - base * length


def cut_kernel(n_scan, *refs):
    infos = refs[:n_scan]
    object_ref, out_ref, table, wide, sem = refs[n_scan:]
    layers, _, rows, length = out_ref.shape
    me = lax.axis_index("scan")
    fill_table(table, infos, me, n_scan)
    _, _, _, col = assigned(table, me, n_scan)
    base, off = column_block(col, length, object_ref.shape[3])
    start = pl.multiple_of(base * length, length)
    copy = pltpu.make_async_copy(object_ref.at[:, :, :, pl.ds(start, 2 * length)], wide, sem)
    copy.start()
    copy.wait()
    step = 32
    lane = lax.broadcasted_iota(jnp.int32, (step, length), 1)
    keep = lane >= off
    for l in range(layers):
        for q in range(2):
            for i in range(0, rows, step):
                at = pl.ds(i, step)
                picked = jnp.where(keep, wide[l, q, at, :length], wide[l, q, at, length:])
                out_ref[l, q, at, :] = picked.astype(out_ref.dtype)


def pattern_kernel(n_scan, *refs):
    infos = refs[:n_scan]
    object_ref, piece_ref, probe_ref, own_ref = refs[n_scan : n_scan + 4]
    others = refs[n_scan + 4 : 2 * n_scan + 3]
    dft_ref, fresnel_ref = refs[2 * n_scan + 3 : 2 * n_scan + 5]
    grad_ref, egrad_ref = refs[2 * n_scan + 5 : 2 * n_scan + 7]
    (table, wide, x_ref, p_ref, a_ref, v_ref, u_ref, s_ref, far_ref, meas_ref,
     lf, li, rf, ri, sem) = refs[2 * n_scan + 7 :]
    modes, _, length, _ = probe_ref.shape
    me = lax.axis_index("scan")
    fill_table(table, infos, me, n_scan)
    source, slot, row, col = assigned(table, me, n_scan)
    base, off = column_block(col, length, object_ref.shape[3])
    start = pl.multiple_of(base * length, length)
    copy = pltpu.make_async_copy(object_ref.at[:, :, :, pl.ds(start, 2 * length)], wide, sem)
    copy.start()
    turn = lax.rem(off, length)

    @pl.when(slot == 0)
    def _():
        meas_ref[...] = own_ref[0]

    for k in range(1, n_scan):
        @pl.when((slot == 1) & (source == lax.rem(me - k + n_scan, n_scan)))
        def _():
            meas_ref[...] = others[k - 1][...]

    def put(matrix, real, imag):
        matrix[:length, :length] = real.astype(jnp.bfloat16)
        matrix[length:, length:] = real.astype(jnp.bfloat16)
        matrix[:length, length:] = imag.astype(jnp.bfloat16)
        matrix[length:, :length] = (-imag).astype(jnp.bfloat16)

    real, imag = dft_ref[0], dft_ref[1]
    put(lf, pltpu.roll(real, row, 1), -pltpu.roll(imag, row, 1))
    put(li, pltpu.roll(real, row, 0), pltpu.roll(imag, row, 0))
    put(rf, pltpu.roll(real, turn, 0), pltpu.roll(imag, turn, 0))
    put(ri, pltpu.roll(real, turn, 1), -pltpu.roll(imag, turn, 1))
    for m in range(modes):
        for q in range(2):
            p_ref[m, q] = pltpu.roll(pltpu.roll(probe_ref[m, q], row, 0), turn, 1)

    step = 32
    chunks = range(0, length, step)
    lane = lax.broadcasted_iota(jnp.int32, (step, length), 1)
    line = lax.broadcasted_iota(jnp.int32, (step, length), 0)
    keep = lane >= off

    def load_x(l):
        for q in range(2):
            for i in chunks:
                at = pl.ds(i, step)
                own = jnp.where(keep, wide[l, q, at, :length], wide[l, q, at, length:])
                x_ref[l, q, at, :] = jnp.where(line >= row - i, own, piece_ref[l, q, at, :].astype(jnp.float32))

    def put_v(m, i, real, imag):
        at = m * length
        v_ref[pl.ds(i, step), at : at + length] = real.astype(jnp.bfloat16)
        v_ref[pl.ds(length + i, step), at : at + length] = imag.astype(jnp.bfloat16)

    def transform(left, right):
        mid = jnp.dot(left[...], v_ref[...], preferred_element_type=jnp.float32).astype(jnp.bfloat16)
        for m in range(modes):
            for q in range(2):
                u_ref[m * length : (m + 1) * length, q * length : (q + 1) * length] = mid[
                    q * length : (q + 1) * length, m * length : (m + 1) * length
                ]
        s_ref[...] = jnp.dot(u_ref[...], right[...], preferred_element_type=jnp.float32)

    def get_s(ref, m, i):
        at = pl.ds(m * length + i, step)
        return ref[at, :length], ref[at, length:]

    def mul(ar, ai, br, bi):
        return ar * br - ai * bi, ar * bi + ai * br

    def cmul(ar, ai, br, bi):
        return ar * br + ai * bi, ar * bi - ai * br

    def propagate(conj):
        transform(lf, rf)
        for i in chunks:
            at = pl.ds(i, step)
            kr, ki = fresnel_ref[0, at, :], fresnel_ref[1, at, :]
            for m in range(modes):
                sr, si = get_s(s_ref, m, i)
                put_v(m, i, *(cmul if conj else mul)(kr, ki, sr, si))
        transform(li, ri)

    copy.wait()
    for l in range(2):
        load_x(l)
    for i in chunks:
        at = pl.ds(i, step)
        xr, xi = x_ref[0, 0, at, :], x_ref[0, 1, at, :]
        for m in range(modes):
            put_v(m, i, *mul(p_ref[m, 0, at, :], p_ref[m, 1, at, :], xr, xi))
    propagate(False)
    for i in chunks:
        at = pl.ds(i, step)
        xr, xi = x_ref[1, 0, at, :], x_ref[1, 1, at, :]
        for m in range(modes):
            ar, ai = get_s(s_ref, m, i)
            a_ref[m, 0, at, :] = ar
            a_ref[m, 1, at, :] = ai
            put_v(m, i, *mul(ar, ai, xr, xi))
    transform(lf, rf)
    for i in chunks:
        at = pl.ds(i, step)
        misfit = -meas_ref[at, :].astype(jnp.float32)
        for m in range(modes):
            fr, fi = get_s(s_ref, m, i)
            misfit += fr * fr + fi * fi
        for m in range(modes):
            fr, fi = get_s(s_ref, m, i)
            put_v(m, i, misfit * fr, misfit * fi)
    transform(li, ri)
    for i in chunks:
        at = pl.ds(i, step)
        xr, xi = x_ref[1, 0, at, :], x_ref[1, 1, at, :]
        gr = gi = 0.0
        for m in range(modes):
            cr, ci = get_s(s_ref, m, i)
            dr, di = cmul(a_ref[m, 0, at, :], a_ref[m, 1, at, :], cr, ci)
            gr, gi = gr + dr, gi + di
            put_v(m, i, *cmul(xr, xi, cr, ci))
        grad_ref[1, 0, at, :] = gr.astype(jnp.bfloat16)
        grad_ref[1, 1, at, :] = gi.astype(jnp.bfloat16)
    propagate(True)
    for i in chunks:
        at = pl.ds(i, step)
        xr, xi = x_ref[0, 0, at, :], x_ref[0, 1, at, :]
        gr = gi = 0.0
        for m in range(modes):
            cr, ci = get_s(s_ref, m, i)
            dr, di = cmul(p_ref[m, 0, at, :], p_ref[m, 1, at, :], cr, ci)
            gr, gi = gr + dr, gi + di
            er, ei = cmul(xr, xi, cr, ci)
            a_ref[m, 0, at, :] = er
            a_ref[m, 1, at, :] = ei
        grad_ref[0, 0, at, :] = gr.astype(jnp.bfloat16)
        grad_ref[0, 1, at, :] = gi.astype(jnp.bfloat16)
    row_back = lax.rem(length - row, length)
    turn_back = lax.rem(length - turn, length)
    for m in range(modes):
        for q in range(2):
            egrad_ref[m, q] = pltpu.roll(pltpu.roll(a_ref[m, q], row_back, 0), turn_back, 1)


def place_kernel(n_scan, steps, *refs):
    own_infos, prev_infos = refs[:n_scan], refs[n_scan : 2 * n_scan]
    patches = refs[2 * n_scan : 4 * n_scan]
    out_ref, own_table, prev_table = refs[4 * n_scan :]
    layers, _, rows, width = out_ref.shape
    length = patches[0].shape[3]
    tile_cols = width * n_scan
    me = lax.axis_index("scan")
    fill_table(own_table, own_infos, me, n_scan)
    fill_table(prev_table, prev_infos, me, n_scan)
    step = 32
    out_ref[...] = jnp.zeros(out_ref.shape, jnp.float32)
    lane = lax.broadcasted_iota(jnp.int32, (step, length), 1)
    line = lax.broadcasted_iota(jnp.int32, (step, length), 0)
    for index, patch in enumerate(patches):
        flip, jump = steps[index % n_scan]
        source = lax.rem((me ^ flip) - jump + n_scan, n_scan)
        table = own_table if index < n_scan else prev_table
        _, _, row, col = assigned(table, source, n_scan)
        base, off = column_block(col, length, tile_cols)
        top, bottom = (row, rows) if index < n_scan else (0, row)
        for block in range(width // length):
            here = me * (width // length) + block
            first, second = base == here, base + 1 == here
            left = jnp.where(first, off, 0)
            right = jnp.where(first, length, off)

            @pl.when(first | second)
            def _():
                cols = (lane >= left) & (lane < right)
                spot = slice(block * length, (block + 1) * length)
                for i in range(0, rows, step):
                    mask = cols & (line >= top - i) & (line < bottom - i)
                    at = pl.ds(i, step)
                    for l in range(layers):
                        for q in range(2):
                            value = patch[l, q, at, :].astype(jnp.float32)
                            out_ref[l, q, at, spot] += jnp.where(mask, value, 0.0)


def body(object_slices, probe, measured, positions, counts):
    layers, _, tile_rows, tile_cols = object_slices.shape
    modes, _, length, _ = probe.shape
    slots = measured.shape[2]
    n_scan, n_obj = lax.axis_size("scan"), lax.axis_size("obj")
    smem = pl.BlockSpec(memory_space=pltpu.SMEM)
    vmem = pl.BlockSpec(memory_space=pltpu.VMEM)
    hbm = pl.BlockSpec(memory_space=pl.ANY)
    info = jnp.concatenate([counts[0], positions[0, 0].reshape(-1)])
    prev_infos = [send(info, lambda s, k=k: s + k, 1) for k in range(n_scan)]
    own_infos = [info] + [send(info, lambda s, k=k: s + k, 0) for k in range(1, n_scan)]
    second = measured[0, 0, 1]
    others = [send(second, lambda s, k=k: s + k, 0) for k in range(1, n_scan)]

    piece_shape = (layers, 2, length, length)
    table = pltpu.SMEM((n_scan, 8), jnp.int32)
    wide = pltpu.VMEM((layers, 2, tile_rows, 2 * length), jnp.float32)
    piece = pl.pallas_call(
        functools.partial(cut_kernel, n_scan),
        out_shape=jax.ShapeDtypeStruct(piece_shape, jnp.bfloat16),
        in_specs=[smem] * n_scan + [hbm],
        out_specs=vmem,
        scratch_shapes=[table, wide, pltpu.SemaphoreType.DMA],
        compiler_params=pltpu.CompilerParams(vmem_limit_bytes=16 * MIB),
        name="cut",
    )(*prev_infos, object_slices)
    got = send(piece, lambda s: s, -1)

    wide_mat = pltpu.VMEM((2 * length, 2 * length), jnp.bfloat16)
    stack_mat = pltpu.VMEM((modes * length, 2 * length), jnp.float32)
    flops = 3 * 2 * 2 * modes * 8 * length**3
    grad, egrad = pl.pallas_call(
        functools.partial(pattern_kernel, n_scan),
        out_shape=[
            jax.ShapeDtypeStruct(piece_shape, jnp.bfloat16),
            jax.ShapeDtypeStruct(probe.shape, jnp.float32),
        ],
        in_specs=[smem] * n_scan + [hbm] + [vmem] * (n_scan + 4),
        out_specs=[vmem, vmem],
        scratch_shapes=[
            table,
            wide,
            pltpu.VMEM(piece_shape, jnp.float32),
            pltpu.VMEM(probe.shape, jnp.float32),
            pltpu.VMEM(probe.shape, jnp.float32),
            pltpu.VMEM((2 * length, modes * length), jnp.bfloat16),
            pltpu.VMEM((modes * length, 2 * length), jnp.bfloat16),
            stack_mat,
            stack_mat,
            pltpu.VMEM((length, length), measured.dtype),
            wide_mat,
            wide_mat,
            wide_mat,
            wide_mat,
            pltpu.SemaphoreType.DMA,
        ],
        compiler_params=pltpu.CompilerParams(vmem_limit_bytes=32 * MIB),
        cost_estimate=pl.CostEstimate(flops=flops, bytes_accessed=8 * MIB, transcendentals=0),
        name="pattern",
    )(*own_infos, object_slices, got, probe, measured[0, 0], *others, dft_tables(length), fresnel_tables(length))

    jumps = [CORES * k for k in range(n_scan // CORES)]
    own_patches = [grad] + [send(grad, lambda s, j=j: s + j, 0) for j in jumps[1:]]
    prev_patches = [send(grad, lambda s, j=j: s + j, 1) for j in jumps]
    own_other = [send(p, lambda s: s ^ 1, 0) for p in own_patches]
    prev_other = [send(p, lambda s: s ^ 1, 0) for p in prev_patches]
    steps = [(0, j) for j in jumps] + [(1, j) for j in jumps]
    object_grad = pl.pallas_call(
        functools.partial(place_kernel, n_scan, steps),
        out_shape=jax.ShapeDtypeStruct((layers, 2, tile_rows, tile_cols // n_scan), jnp.float32),
        in_specs=[smem] * (2 * n_scan) + [vmem] * (2 * n_scan),
        out_specs=vmem,
        scratch_shapes=[table, table],
        compiler_params=pltpu.CompilerParams(vmem_limit_bytes=32 * MIB),
        name="place",
    )(*own_infos, *prev_infos, *own_patches, *own_other, *prev_patches, *prev_other)

    factor = 1.0 / math.sqrt(n_scan * n_obj * slots // 2)
    partial_probe = lax.psum_scatter(egrad, "scan", scatter_dimension=3, tiled=True)
    probe_total = lax.psum_scatter(partial_probe, "obj", scatter_dimension=2, tiled=True)
    return (object_grad, probe_total * factor)


def solution(mesh):
    return jax.shard_map(
        body,
        mesh=mesh,
        in_specs=(
            P(None, None, "obj", None),
            P(),
            P("scan", "obj", None, None, None),
            P("scan", "obj", None, None),
            P("scan", "obj"),
        ),
        out_specs=(P(None, None, "obj", "scan"), P(None, None, "obj", "scan")),
        check_vma=False,
    )
```

```python
import functools
import math

import jax
import jax.numpy as jnp
import ml_dtypes
import numpy as np
from jax import lax
from jax.experimental import pallas as pl
from jax.experimental.pallas import tpu as pltpu
from jax.sharding import PartitionSpec as P

AXES = ("scan", "obj")
CORES = 2
MIB = 1 << 20


def dft_tables(length):
    index = np.arange(length)
    angles = (index[:, None] * index[None, :] % length) * (2.0 * math.pi / length)
    parts = np.stack([np.cos(angles), -np.sin(angles)]) / math.sqrt(length)
    return parts.astype(np.float32).astype(ml_dtypes.bfloat16).astype(np.float32)


def fresnel_tables(length):
    index = np.arange(length)
    freqs = np.where(index < length // 2, index, index - length)
    squares = freqs * freqs
    phases = ((squares[:, None] + squares[None, :]) % (4 * length)) * (2.0 * math.pi / (4 * length))
    return np.stack([np.cos(phases), -np.sin(phases)]).astype(np.float32)


def send(block, scan_of, obj_step):
    n_scan, n_obj = lax.axis_size("scan"), lax.axis_size("obj")
    route = []
    for s in range(n_scan):
        for o in range(n_obj):
            route.append((s * n_obj + o, scan_of(s) % n_scan * n_obj + (o + obj_step) % n_obj))
    return lax.ppermute(block, AXES, route)


def assigned(info, tile, target, n_scan, n_obj):
    def entry(a, j):
        return info[a * n_obj + tile, 0, j]

    idle = entry(target, 0) == 0
    counts = [entry(a, 0) for a in range(n_scan)]
    rank = jnp.int32(0)
    for a in range(n_scan):
        rank += jnp.where((counts[a] == 0) & (a < target), 1, 0)
    source = jnp.int32(target)
    seen = jnp.int32(0)
    for a in range(n_scan):
        full = counts[a] == 2
        source = jnp.where(idle & full & (seen == rank), a, source)
        seen += jnp.where(full, 1, 0)
    slot = jnp.where(idle, 1, 0)
    return source, slot, entry(source, 1 + 2 * slot), entry(source, 2 + 2 * slot)


def column_block(col, length, tile_cols):
    base = jnp.minimum(lax.div(col, length), tile_cols // length - 2)
    return base, col - base * length


STEP = 32


def lanes(length):
    return lax.broadcasted_iota(jnp.int32, (STEP, length), 1)


def lines(length):
    return lax.broadcasted_iota(jnp.int32, (STEP, length), 0)


def mul(ar, ai, br, bi):
    return ar * br - ai * bi, ar * bi + ai * br


def cmul(ar, ai, br, bi):
    return ar * br + ai * bi, ar * bi - ai * br


def fetch_columns(object_ref, wide, sem, base, length):
    start = pl.multiple_of(base * length, length)
    copy = pltpu.make_async_copy(object_ref.at[:, :, :, pl.ds(start, 2 * length)], wide, sem)
    copy.start()
    return copy


def pick_columns(wide, l, q, at, off, length):
    return jnp.where(lanes(length) >= off, wide[l, q, at, :length], wide[l, q, at, length:])


def cut_kernel(sizes, info, object_ref, piece0, piece1, wide, sem):
    n_scan, n_obj, tile_cols = sizes
    _, rows, length = piece0.shape
    tile = lax.rem(lax.axis_index("obj") + n_obj - 1, n_obj)
    _, _, _, col = assigned(info, tile, lax.axis_index("scan"), n_scan, n_obj)
    base, off = column_block(col, length, tile_cols)
    fetch_columns(object_ref, wide, sem, base, length).wait()
    for l, piece in enumerate((piece0, piece1)):
        for q in range(2):
            for i in range(0, rows, STEP):
                at = pl.ds(i, STEP)
                piece[q, at, :] = pick_columns(wide, l, q, at, off, length).astype(piece.dtype)


def prep_kernel(sizes, info, object_ref, probe_ref, dft_ref, mats, p_ref, xo_ref, wide, sem):
    n_scan, n_obj, tile_cols = sizes
    modes, _, length, _ = probe_ref.shape
    _, _, row, col = assigned(info, lax.axis_index("obj"), lax.axis_index("scan"), n_scan, n_obj)
    base, off = column_block(col, length, tile_cols)
    copy = fetch_columns(object_ref, wide, sem, base, length)
    turn = lax.rem(off, length)

    def put(k, real, imag):
        mats[k, :length, :length] = real.astype(jnp.bfloat16)
        mats[k, length:, length:] = real.astype(jnp.bfloat16)
        mats[k, :length, length:] = imag.astype(jnp.bfloat16)
        mats[k, length:, :length] = (-imag).astype(jnp.bfloat16)

    real, imag = dft_ref[0], dft_ref[1]
    put(0, pltpu.roll(real, row, 1), -pltpu.roll(imag, row, 1))
    put(1, pltpu.roll(real, turn, 0), pltpu.roll(imag, turn, 0))
    put(2, pltpu.roll(real, row, 0), pltpu.roll(imag, row, 0))
    put(3, pltpu.roll(real, turn, 1), -pltpu.roll(imag, turn, 1))
    for m in range(modes):
        for q in range(2):
            p_ref[m, q] = pltpu.roll(pltpu.roll(probe_ref[m, q], row, 0), turn, 1)
    copy.wait()
    for l in range(xo_ref.shape[0]):
        for q in range(2):
            for i in range(0, length, STEP):
                at = pl.ds(i, STEP)
                xo_ref[l, q, at, :] = pick_columns(wide, l, q, at, off, length)


def put_v(v_ref, length, m, i, real, imag):
    spot = slice(m * length, (m + 1) * length)
    v_ref[pl.ds(i, STEP), spot] = real.astype(jnp.bfloat16)
    v_ref[pl.ds(length + i, STEP), spot] = imag.astype(jnp.bfloat16)


def get_s(s_ref, length, m, i):
    at = pl.ds(m * length + i, STEP)
    return s_ref[at, :length], s_ref[at, length:]


def transform(mats, inverse, v_ref, u_ref, s_ref):
    length = mats.shape[1] // 2
    mid = jnp.dot(mats[2 * inverse], v_ref[...], preferred_element_type=jnp.float32).astype(jnp.bfloat16)
    for m in range(v_ref.shape[1] // length):
        for q in range(2):
            u_ref[m * length : (m + 1) * length, q * length : (q + 1) * length] = mid[
                q * length : (q + 1) * length, m * length : (m + 1) * length
            ]
    s_ref[...] = jnp.dot(u_ref[...], mats[2 * inverse + 1], preferred_element_type=jnp.float32)


def propagate(product, mats, fresnel_ref, v_in, v_ref, u_ref, s_ref):
    length = mats.shape[1] // 2
    transform(mats, 0, v_in, u_ref, s_ref)
    for i in range(0, length, STEP):
        at = pl.ds(i, STEP)
        kr, ki = fresnel_ref[0, at, :], fresnel_ref[1, at, :]
        for m in range(v_ref.shape[1] // length):
            put_v(v_ref, length, m, i, *product(kr, ki, *get_s(s_ref, length, m, i)))
    transform(mats, 1, v_ref, u_ref, s_ref)


def join(own, piece_ref, q, i, row, length):
    piece = piece_ref[q, pl.ds(i, STEP), :].astype(jnp.float32)
    return jnp.where(lines(length) >= row - i, own, piece)


def first_kernel(sizes, info, mats, fresnel_ref, p_ref, xo_ref, piece, a_ref, x_ref, v_ref, u_ref, s_ref):
    n_scan, n_obj, tile_cols = sizes
    modes, _, length, _ = p_ref.shape
    _, _, row, _ = assigned(info, lax.axis_index("obj"), lax.axis_index("scan"), n_scan, n_obj)
    for i in range(0, length, STEP):
        at = pl.ds(i, STEP)
        xr = join(xo_ref[0, 0, at, :], piece, 0, i, row, length)
        xi = join(xo_ref[0, 1, at, :], piece, 1, i, row, length)
        x_ref[0, at, :] = xr
        x_ref[1, at, :] = xi
        for m in range(modes):
            put_v(v_ref, length, m, i, *mul(p_ref[m, 0, at, :], p_ref[m, 1, at, :], xr, xi))
    propagate(mul, mats, fresnel_ref, v_ref, v_ref, u_ref, s_ref)
    for i in range(0, length, STEP):
        at = pl.ds(i, STEP)
        for m in range(modes):
            a_ref[m, 0, at, :], a_ref[m, 1, at, :] = get_s(s_ref, length, m, i)


def second_kernel(sizes, *refs):
    n_scan, n_obj, tile_cols = sizes
    info, mats, a_ref, xo_ref, piece, own_ref = refs[:6]
    others = refs[6 : 5 + n_scan]
    grad_ref, v_out, v_ref, u_ref, s_ref, x_ref, meas_ref = refs[5 + n_scan :]
    modes, _, length, _ = a_ref.shape
    me = lax.axis_index("scan")
    source, slot, row, _ = assigned(info, lax.axis_index("obj"), me, n_scan, n_obj)

    @pl.when(slot == 0)
    def _():
        meas_ref[...] = own_ref[0]

    for k in range(1, n_scan):
        @pl.when((slot == 1) & (source == lax.rem(me - k + n_scan, n_scan)))
        def _():
            meas_ref[...] = others[k - 1][...]

    for i in range(0, length, STEP):
        at = pl.ds(i, STEP)
        xr = join(xo_ref[1, 0, at, :], piece, 0, i, row, length)
        xi = join(xo_ref[1, 1, at, :], piece, 1, i, row, length)
        x_ref[0, at, :] = xr
        x_ref[1, at, :] = xi
        for m in range(modes):
            put_v(v_ref, length, m, i, *mul(a_ref[m, 0, at, :], a_ref[m, 1, at, :], xr, xi))
    transform(mats, 0, v_ref, u_ref, s_ref)
    for i in range(0, length, STEP):
        misfit = -meas_ref[pl.ds(i, STEP), :].astype(jnp.float32)
        for m in range(modes):
            fr, fi = get_s(s_ref, length, m, i)
            misfit += fr * fr + fi * fi
        for m in range(modes):
            fr, fi = get_s(s_ref, length, m, i)
            put_v(v_ref, length, m, i, misfit * fr, misfit * fi)
    transform(mats, 1, v_ref, u_ref, s_ref)
    for i in range(0, length, STEP):
        at = pl.ds(i, STEP)
        gr = gi = 0.0
        for m in range(modes):
            cr, ci = get_s(s_ref, length, m, i)
            dr, di = cmul(a_ref[m, 0, at, :], a_ref[m, 1, at, :], cr, ci)
            gr, gi = gr + dr, gi + di
            put_v(v_out, length, m, i, *cmul(x_ref[0, at, :], x_ref[1, at, :], cr, ci))
        grad_ref[0, at, :] = gr.astype(grad_ref.dtype)
        grad_ref[1, at, :] = gi.astype(grad_ref.dtype)


def third_kernel(sizes, info, mats, fresnel_ref, v_in, x_ref, p_ref, grad_ref, e_ref, v_ref, u_ref, s_ref, b_ref):
    n_scan, n_obj, tile_cols = sizes
    modes, _, length, _ = p_ref.shape
    _, _, row, col = assigned(info, lax.axis_index("obj"), lax.axis_index("scan"), n_scan, n_obj)
    _, off = column_block(col, length, tile_cols)
    propagate(cmul, mats, fresnel_ref, v_in, v_ref, u_ref, s_ref)
    for i in range(0, length, STEP):
        at = pl.ds(i, STEP)
        gr = gi = 0.0
        for m in range(modes):
            cr, ci = get_s(s_ref, length, m, i)
            dr, di = cmul(p_ref[m, 0, at, :], p_ref[m, 1, at, :], cr, ci)
            gr, gi = gr + dr, gi + di
            b_ref[m, 0, at, :], b_ref[m, 1, at, :] = cmul(x_ref[0, at, :], x_ref[1, at, :], cr, ci)
        grad_ref[0, at, :] = gr.astype(grad_ref.dtype)
        grad_ref[1, at, :] = gi.astype(grad_ref.dtype)
    row_back = lax.rem(length - row, length)
    col_back = lax.rem(2 * length - off, length)
    per_row, per_col = length // n_obj, length // n_scan
    lane = lax.broadcasted_iota(jnp.int32, (length, 128), 1)
    for m in range(modes):
        for q in range(2):
            b_ref[m, q] = pltpu.roll(pltpu.roll(b_ref[m, q], row_back, 0), col_back, 1)
        for s in range(n_scan):
            first, shift = s * per_col // 128 * 128, s * per_col % 128
            real = b_ref[m, 0, :, first : first + 128]
            imag = b_ref[m, 1, :, first : first + 128]
            real = pltpu.roll(real, (128 - shift) % 128, 1) if shift else real
            imag = pltpu.roll(imag, (per_col - shift) % 128, 1) if shift != per_col else imag
            both = jnp.where(lane < per_col, real, imag)[:, : 2 * per_col]
            for o in range(n_obj):
                e_ref[s * n_obj + o, m] = both[o * per_row : (o + 1) * per_row].astype(e_ref.dtype)


def place_kernel(sizes, steps, factor, *refs):
    n_scan, n_obj, tile_cols = sizes
    info, chunks = refs[:2]
    out_ref, probe_out = refs[-2:]
    patches = refs[2:-2]
    layers, _, rows, width = out_ref.shape
    length = patches[0].shape[2]
    me = lax.axis_index("scan")
    here = lax.axis_index("obj")
    out_ref[...] = jnp.zeros(out_ref.shape, jnp.float32)
    lane, line = lanes(length), lines(length)
    for index in range(2 * n_scan):
        previous, member = divmod(index, n_scan)
        flip, jump = steps[member]
        source = lax.rem((me ^ flip) - jump + n_scan, n_scan)
        tile = lax.rem(here + n_obj - previous, n_obj)
        _, _, row, col = assigned(info, tile, source, n_scan, n_obj)
        base, off = column_block(col, length, tile_cols)
        top, bottom = (0, row) if previous else (row, rows)
        for block in range(width // length):
            column = me * (width // length) + block
            first, second = base == column, base + 1 == column
            left = jnp.where(first, off, 0)
            right = jnp.where(first, length, off)

            @pl.when(first | second)
            def _():
                cols = (lane >= left) & (lane < right)
                spot = slice(block * length, (block + 1) * length)
                for i in range(0, rows, STEP):
                    mask = cols & (line >= top - i) & (line < bottom - i)
                    at = pl.ds(i, STEP)
                    for l in range(layers):
                        for q in range(2):
                            value = patches[index * layers + l][q, at, :].astype(jnp.float32)
                            out_ref[l, q, at, spot] += jnp.where(mask, value, 0.0)

    per_col = probe_out.shape[3]
    for m in range(probe_out.shape[0]):
        total = chunks[0, m].astype(jnp.float32)
        for d in range(1, n_scan * n_obj):
            total += chunks[d, m].astype(jnp.float32)
        total *= factor
        probe_out[m, 0] = total[:, :per_col]
        probe_out[m, 1] = total[:, per_col:]


def body(object_slices, probe, measured, positions, counts):
    layers, _, tile_rows, tile_cols = object_slices.shape
    modes, _, length, _ = probe.shape
    slots = measured.shape[2]
    n_scan, n_obj = lax.axis_size("scan"), lax.axis_size("obj")
    devices = n_scan * n_obj
    sizes = (n_scan, n_obj, tile_cols)
    smem = pl.BlockSpec(memory_space=pltpu.SMEM)
    vmem = pl.BlockSpec(memory_space=pltpu.VMEM)
    hbm = pl.BlockSpec(memory_space=pltpu.HBM)
    params = pltpu.CompilerParams(vmem_limit_bytes=20 * MIB)
    real, half = jnp.float32, jnp.bfloat16

    def call(kernel, outs, ins, scratch, name, flops, *args):
        return pl.pallas_call(
            kernel,
            out_shape=[jax.ShapeDtypeStruct(*o) for o in outs],
            in_specs=ins,
            out_specs=[vmem] * len(outs),
            scratch_shapes=scratch,
            compiler_params=params,
            cost_estimate=pl.CostEstimate(flops=flops, bytes_accessed=4 * MIB, transcendentals=0),
            name=name,
        )(*args)

    def kernel_of(function):
        return functools.partial(function, sizes)

    info = jnp.concatenate([counts[0], positions[0, 0].reshape(-1)])
    info = jnp.broadcast_to(jnp.pad(info, (0, 123)), (devices, 1, 128))
    info = lax.all_to_all(info, AXES, 0, 0, tiled=True)
    second = measured[0, 0, 1]
    others = [send(second, lambda s, k=k: s + k, 0) for k in range(1, n_scan)]

    piece_shape = (2, length, length)
    field_shape = (modes, 2, length, length)
    wide = [pltpu.VMEM((layers, 2, tile_rows, 2 * length), real), pltpu.SemaphoreType.DMA]
    vus = [
        pltpu.VMEM((2 * length, modes * length), half),
        pltpu.VMEM((modes * length, 2 * length), half),
        pltpu.VMEM((modes * length, 2 * length), real),
    ]
    pair_flops = 2 * 2 * modes * 8 * length**3
    pieces = call(
        kernel_of(cut_kernel), [(piece_shape, half)] * 2, [smem, hbm], wide, "cut", MIB, info, object_slices
    )
    pieces = [send(piece, lambda s: s, -1) for piece in pieces]
    mats, turned, own_part = call(
        kernel_of(prep_kernel),
        [((4, 2 * length, 2 * length), half), (field_shape, real), ((layers, *piece_shape), real)],
        [smem, hbm, vmem, vmem],
        wide,
        "prep",
        MIB,
        info,
        object_slices,
        probe,
        dft_tables(length),
    )
    fresnel = fresnel_tables(length)
    arrived, patch = call(
        kernel_of(first_kernel),
        [(field_shape, real), (piece_shape, real)],
        [smem] + [vmem] * 5,
        vus,
        "first",
        pair_flops,
        info,
        mats,
        fresnel,
        turned,
        own_part,
        pieces[0],
    )
    grad1, carried = call(
        kernel_of(second_kernel),
        [(piece_shape, half), ((2 * length, modes * length), half)],
        [smem] + [vmem] * (4 + n_scan),
        vus + [pltpu.VMEM(piece_shape, real), pltpu.VMEM((length, length), measured.dtype)],
        "second",
        pair_flops,
        info,
        mats,
        arrived,
        own_part,
        pieces[1],
        measured[0, 0],
        *others,
    )
    chunk_shape = (devices, modes, length // n_obj, 2 * (length // n_scan))
    grad0, chunks = call(
        kernel_of(third_kernel),
        [(piece_shape, half), (chunk_shape, half)],
        [smem] + [vmem] * 5,
        vus + [pltpu.VMEM(field_shape, real)],
        "third",
        pair_flops,
        info,
        mats,
        fresnel,
        carried,
        patch,
        turned,
    )

    jumps = [CORES * k for k in range(n_scan // CORES)]
    held = []
    for l, grad in enumerate((grad0, grad1)):
        own = [grad] + [send(grad, lambda s, j=j: s + j, 0) for j in jumps[1:]]
        passed = [send(grad, lambda s: s, 1)]
        if l == 0:
            passed += [send(passed[0], lambda s, j=j: s + j, 0) for j in jumps[1:]]
        else:
            passed += [send(patch_grad, lambda s: s, 1) for patch_grad in own[1:]]
        own += [send(p, lambda s: s ^ 1, 0) for p in own]
        passed += [send(p, lambda s: s ^ 1, 0) for p in passed]
        held.append(own + passed)
    chunks = lax.all_to_all(chunks, AXES, 0, 0, tiled=True)
    steps = [(0, j) for j in jumps] + [(1, j) for j in jumps]
    factor = 1.0 / math.sqrt(n_scan * n_obj * slots // 2)
    object_grad, probe_grad = call(
        functools.partial(place_kernel, sizes, steps, factor),
        [
            ((layers, 2, tile_rows, tile_cols // n_scan), real),
            ((modes, 2, length // n_obj, length // n_scan), real),
        ],
        [smem, vmem] + [vmem] * (2 * n_scan * layers),
        [],
        "place",
        MIB,
        info,
        chunks,
        *[held[l][index] for index in range(2 * n_scan) for l in range(layers)],
    )
    return (object_grad, probe_grad)


def solution(mesh):
    return jax.shard_map(
        body,
        mesh=mesh,
        in_specs=(
            P(None, None, "obj", None),
            P(),
            P("scan", "obj", None, None, None),
            P("scan", "obj", None, None),
            P("scan", "obj"),
        ),
        out_specs=(P(None, None, "obj", "scan"), P(None, None, "obj", "scan")),
        check_vma=False,
    )
```

```python
import functools
import math

import jax
import jax.numpy as jnp
import ml_dtypes
import numpy as np
from jax import lax
from jax.experimental import pallas as pl
from jax.experimental.pallas import tpu as pltpu
from jax.sharding import PartitionSpec as P

AXES = ("scan", "obj")
CORES = 2
MIB = 1 << 20
SMALL, LARGE = 20, 58


def dft_tables(length):
    index = np.arange(length)
    angles = (index[:, None] * index[None, :] % length) * (2.0 * math.pi / length)
    parts = np.stack([np.cos(angles), -np.sin(angles)]) / math.sqrt(length)
    return parts.astype(np.float32).astype(ml_dtypes.bfloat16).astype(np.float32)


def fresnel_tables(length):
    index = np.arange(length)
    freqs = np.where(index < length // 2, index, index - length)
    squares = freqs * freqs
    phases = ((squares[:, None] + squares[None, :]) % (4 * length)) * (2.0 * math.pi / (4 * length))
    return np.stack([np.cos(phases), -np.sin(phases)]).astype(np.float32)


def send(block, move):
    n_scan, n_obj = lax.axis_size("scan"), lax.axis_size("obj")
    route = []
    for s in range(n_scan):
        for o in range(n_obj):
            goal = move(s, o)
            if goal is not None:
                route.append((s * n_obj + o, goal[0] % n_scan * n_obj + goal[1] % n_obj))
    return lax.ppermute(block, AXES, route)


OWN, PREVIOUS = 0, 1


def live(info, tile, rank, n_scan):
    def entry(a, j):
        return info[a, 0, 8 * tile + j]

    source, slot = jnp.int32(0), jnp.int32(0)
    before = jnp.int32(0)
    for a in range(n_scan):
        count = entry(a, 0)
        here = (rank >= before) & (rank < before + count)
        source = jnp.where(here, a, source)
        slot = jnp.where(here, rank - before, slot)
        before += count
    return source, slot, entry(source, 1 + 2 * slot), entry(source, 2 + 2 * slot)


def place_of(n_scan):
    me = lax.axis_index("scan")
    core = lax.rem(me, CORES)
    chip = lax.div(me, CORES)
    return chip, core, chip + core * (n_scan // CORES)


def column_block(col, length, tile_cols):
    base = jnp.minimum(lax.div(col, length), tile_cols // length - 2)
    return base, col - base * length


STEP = 32


def lanes(length):
    return lax.broadcasted_iota(jnp.int32, (STEP, length), 1)


def lines(length):
    return lax.broadcasted_iota(jnp.int32, (STEP, length), 0)


def mul(ar, ai, br, bi):
    return ar * br - ai * bi, ar * bi + ai * br


def cmul(ar, ai, br, bi):
    return ar * br + ai * bi, ar * bi - ai * br


def fetch_columns(object_ref, wide, sem, base, length):
    start = pl.multiple_of(base * length, length)
    copy = pltpu.make_async_copy(object_ref.at[:, :, :, pl.ds(start, 2 * length)], wide, sem)
    copy.start()
    return copy


def pick_columns(wide, l, q, at, off, length):
    return jnp.where(lanes(length) >= off, wide[l, q, at, :length], wide[l, q, at, length:])


def cut_kernel(sizes, info, object_ref, piece0, piece1, wide, sem):
    n_scan, _, tile_cols = sizes
    _, rows, length = piece0.shape
    _, core, rank = place_of(n_scan)
    _, _, _, col = live(info, 1 - core, rank, n_scan)
    base, off = column_block(col, length, tile_cols)
    fetch_columns(object_ref, wide, sem, base, length).wait()
    for l, piece in enumerate((piece0, piece1)):
        for q in range(2):
            for i in range(0, rows, STEP):
                at = pl.ds(i, STEP)
                piece[q, at, :] = pick_columns(wide, l, q, at, off, length).astype(piece.dtype)


def choose_kernel(sizes, steps, info, *refs):
    n_scan, _, _ = sizes
    sources = refs[:n_scan]
    out_ref, sem = refs[n_scan:]
    me = lax.axis_index("scan")
    _, _, rank = place_of(n_scan)
    source, slot, _, _ = live(info, OWN, rank, n_scan)
    for (flip, jump), candidate in zip(steps, sources):
        @pl.when(source == lax.rem((me ^ flip) - jump + n_scan, n_scan))
        def _():
            copy = pltpu.make_async_copy(candidate.at[slot], out_ref, sem)
            copy.start()
            copy.wait()


def prep_kernel(sizes, info, object_ref, probe_ref, dft_ref, mats, p_ref, xo_ref, wide, sem):
    n_scan, _, tile_cols = sizes
    modes, _, length, _ = probe_ref.shape
    _, core, rank = place_of(n_scan)
    _, _, row, col = live(info, core, rank, n_scan)
    base, off = column_block(col, length, tile_cols)
    copy = fetch_columns(object_ref, wide, sem, base, length)
    turn = lax.rem(off, length)

    def put(k, real, imag):
        mats[k, :length, :length] = real.astype(jnp.bfloat16)
        mats[k, length:, length:] = real.astype(jnp.bfloat16)
        mats[k, :length, length:] = imag.astype(jnp.bfloat16)
        mats[k, length:, :length] = (-imag).astype(jnp.bfloat16)

    real, imag = dft_ref[0], dft_ref[1]
    put(0, pltpu.roll(real, row, 1), -pltpu.roll(imag, row, 1))
    put(1, pltpu.roll(real, turn, 0), pltpu.roll(imag, turn, 0))
    put(2, pltpu.roll(real, row, 0), pltpu.roll(imag, row, 0))
    put(3, pltpu.roll(real, turn, 1), -pltpu.roll(imag, turn, 1))
    for m in range(modes):
        for q in range(2):
            p_ref[m, q] = pltpu.roll(pltpu.roll(probe_ref[m, q], row, 0), turn, 1)
    copy.wait()
    for l in range(xo_ref.shape[0]):
        for q in range(2):
            for i in range(0, length, STEP):
                at = pl.ds(i, STEP)
                xo_ref[l, q, at, :] = pick_columns(wide, l, q, at, off, length)


def put_v(v_ref, length, m, i, real, imag):
    spot = slice(m * length, (m + 1) * length)
    v_ref[pl.ds(i, STEP), spot] = real.astype(jnp.bfloat16)
    v_ref[pl.ds(length + i, STEP), spot] = imag.astype(jnp.bfloat16)


def get_s(s_ref, length, m, i):
    at = pl.ds(m * length + i, STEP)
    return s_ref[at, :length], s_ref[at, length:]


def transform(mats, inverse, v_ref, u_ref, s_ref):
    length = mats.shape[1] // 2
    mid = jnp.dot(mats[2 * inverse], v_ref[...], preferred_element_type=jnp.float32).astype(jnp.bfloat16)
    for m in range(v_ref.shape[1] // length):
        for q in range(2):
            u_ref[m * length : (m + 1) * length, q * length : (q + 1) * length] = mid[
                q * length : (q + 1) * length, m * length : (m + 1) * length
            ]
    s_ref[...] = jnp.dot(u_ref[...], mats[2 * inverse + 1], preferred_element_type=jnp.float32)


def propagate(product, mats, fresnel_ref, v_in, v_ref, u_ref, s_ref):
    length = mats.shape[1] // 2
    transform(mats, 0, v_in, u_ref, s_ref)
    for i in range(0, length, STEP):
        at = pl.ds(i, STEP)
        kr, ki = fresnel_ref[0, at, :], fresnel_ref[1, at, :]
        for m in range(v_ref.shape[1] // length):
            put_v(v_ref, length, m, i, *product(kr, ki, *get_s(s_ref, length, m, i)))
    transform(mats, 1, v_ref, u_ref, s_ref)


def own_rows(sizes, info, length):
    n_scan, _, _ = sizes
    _, core, rank = place_of(n_scan)
    _, _, row, _ = live(info, core, rank, n_scan)
    return jnp.where(core == 0, row, 0), jnp.where(core == 0, length, row)


def join(own, piece_ref, q, i, bounds, length):
    piece = piece_ref[q, pl.ds(i, STEP), :].astype(jnp.float32)
    line = lines(length)
    return jnp.where((line >= bounds[0] - i) & (line < bounds[1] - i), own, piece)


def first_kernel(sizes, info, mats, fresnel_ref, p_ref, xo_ref, piece, a_ref, x_ref, v_ref, u_ref, s_ref):
    modes, _, length, _ = p_ref.shape
    bounds = own_rows(sizes, info, length)
    for i in range(0, length, STEP):
        at = pl.ds(i, STEP)
        xr = join(xo_ref[0, 0, at, :], piece, 0, i, bounds, length)
        xi = join(xo_ref[0, 1, at, :], piece, 1, i, bounds, length)
        x_ref[0, at, :] = xr
        x_ref[1, at, :] = xi
        for m in range(modes):
            put_v(v_ref, length, m, i, *mul(p_ref[m, 0, at, :], p_ref[m, 1, at, :], xr, xi))
    propagate(mul, mats, fresnel_ref, v_ref, v_ref, u_ref, s_ref)
    for i in range(0, length, STEP):
        at = pl.ds(i, STEP)
        for m in range(modes):
            a_ref[m, 0, at, :], a_ref[m, 1, at, :] = get_s(s_ref, length, m, i)


def second_kernel(sizes, info, mats, a_ref, xo_ref, piece, meas_here, meas_sent, grad_ref, v_out, v_ref, u_ref, s_ref, x_ref):
    modes, _, length, _ = a_ref.shape
    bounds = own_rows(sizes, info, length)
    _, core, _ = place_of(sizes[0])
    for i in range(0, length, STEP):
        at = pl.ds(i, STEP)
        xr = join(xo_ref[1, 0, at, :], piece, 0, i, bounds, length)
        xi = join(xo_ref[1, 1, at, :], piece, 1, i, bounds, length)
        x_ref[0, at, :] = xr
        x_ref[1, at, :] = xi
        for m in range(modes):
            put_v(v_ref, length, m, i, *mul(a_ref[m, 0, at, :], a_ref[m, 1, at, :], xr, xi))
    transform(mats, 0, v_ref, u_ref, s_ref)
    for i in range(0, length, STEP):
        at = pl.ds(i, STEP)
        here, sent = meas_here[at, :].astype(jnp.float32), meas_sent[at, :].astype(jnp.float32)
        misfit = -jnp.where(core == 0, here, sent)
        for m in range(modes):
            fr, fi = get_s(s_ref, length, m, i)
            misfit += fr * fr + fi * fi
        for m in range(modes):
            fr, fi = get_s(s_ref, length, m, i)
            put_v(v_ref, length, m, i, misfit * fr, misfit * fi)
    transform(mats, 1, v_ref, u_ref, s_ref)
    for i in range(0, length, STEP):
        at = pl.ds(i, STEP)
        gr = gi = 0.0
        for m in range(modes):
            cr, ci = get_s(s_ref, length, m, i)
            dr, di = cmul(a_ref[m, 0, at, :], a_ref[m, 1, at, :], cr, ci)
            gr, gi = gr + dr, gi + di
            put_v(v_out, length, m, i, *cmul(x_ref[0, at, :], x_ref[1, at, :], cr, ci))
        grad_ref[0, at, :] = gr.astype(grad_ref.dtype)
        grad_ref[1, at, :] = gi.astype(grad_ref.dtype)


def third_kernel(sizes, info, mats, fresnel_ref, v_in, x_ref, p_ref, grad_ref, keep_ref, give_ref, v_ref, u_ref, s_ref, b_ref):
    n_scan, n_obj, tile_cols = sizes
    modes, _, length, _ = p_ref.shape
    chip, core, rank = place_of(n_scan)
    chips = n_scan // CORES
    _, _, row, col = live(info, core, rank, n_scan)
    _, off = column_block(col, length, tile_cols)
    propagate(cmul, mats, fresnel_ref, v_in, v_ref, u_ref, s_ref)
    for i in range(0, length, STEP):
        at = pl.ds(i, STEP)
        gr = gi = 0.0
        for m in range(modes):
            cr, ci = get_s(s_ref, length, m, i)
            dr, di = cmul(p_ref[m, 0, at, :], p_ref[m, 1, at, :], cr, ci)
            gr, gi = gr + dr, gi + di
            b_ref[m, 0, at, :], b_ref[m, 1, at, :] = cmul(x_ref[0, at, :], x_ref[1, at, :], cr, ci)
        grad_ref[0, at, :] = gr.astype(grad_ref.dtype)
        grad_ref[1, at, :] = gi.astype(grad_ref.dtype)
    row_back = lax.rem(length - row, length)
    col_back = lax.rem(2 * length - off, length)
    per_row, per_col = length // n_obj, length // n_scan
    lane = lax.broadcasted_iota(jnp.int32, (length, 128), 1)
    for m in range(modes):
        for q in range(2):
            b_ref[m, q] = pltpu.roll(pltpu.roll(b_ref[m, q], row_back, 0), col_back, 1)
        for s in range(n_scan):
            first, shift = s * per_col // 128 * 128, s * per_col % 128
            real = b_ref[m, 0, :, first : first + 128]
            imag = b_ref[m, 1, :, first : first + 128]
            real = pltpu.roll(real, (128 - shift) % 128, 1) if shift else real
            imag = pltpu.roll(imag, (per_col - shift) % 128, 1) if shift != per_col else imag
            both = jnp.where(lane < per_col, real, imag)[:, : 2 * per_col]
            apart = lax.rem(s // CORES - chip + chips, chips)
            for mine, ref in ((core, keep_ref), (1 - core, give_ref)):
                @pl.when(mine == s % CORES)
                def _():
                    for o in range(n_obj):
                        ref[o, apart, m] = both[o * per_row : (o + 1) * per_row].astype(ref.dtype)


def place_kernel(sizes, kinds, factor, *refs):
    n_scan, _, tile_cols = sizes
    chips = n_scan // CORES
    layers = refs[-4].shape[0]
    info = refs[0]
    shares = refs[1 : 1 + chips]
    patches = refs[1 + chips : -4]
    out_ref, probe_out, held, sems = refs[-4:]
    _, _, rows, width = out_ref.shape
    length = patches[0].shape[2]
    me = lax.axis_index("scan")
    chip, core, _ = place_of(n_scan)
    blocks = width // length
    first_block = me * blocks
    spots = []
    for index, (kind, flip, jump) in enumerate(kinds):
        other = core ^ flip
        tile = other ^ kind
        rank = lax.rem(chip - jump + chips, chips) + other * chips
        _, _, row, col = live(info, tile, rank, n_scan)
        base, off = column_block(col, length, tile_cols)
        top, bottom = jnp.where(tile == OWN, row, 0), jnp.where(tile == OWN, rows, row)
        meets = (base + 1 >= first_block) & (base < first_block + blocks)
        copies = [
            pltpu.make_async_copy(patches[index * layers + l], held.at[index, l], sems.at[index, l])
            for l in range(layers)
        ]
        spots.append((base, off, top, bottom, meets, copies))

        @pl.when(meets)
        def _():
            for copy in copies:
                copy.start()

    out_ref[...] = jnp.zeros(out_ref.shape, jnp.float32)
    per_col = probe_out.shape[3]
    for m in range(probe_out.shape[0]):
        total = sum(share[m].astype(jnp.float32) for share in shares) * factor
        probe_out[m, 0] = total[:, :per_col]
        probe_out[m, 1] = total[:, per_col:]
    lane, line = lanes(length), lines(length)
    for index, (base, off, top, bottom, meets, copies) in enumerate(spots):
        @pl.when(meets)
        def _():
            for copy in copies:
                copy.wait()
        for block in range(blocks):
            first, second = base == first_block + block, base + 1 == first_block + block
            left = jnp.where(first, off, 0)
            right = jnp.where(first, length, off)

            @pl.when(first | second)
            def _():
                cols = (lane >= left) & (lane < right)
                spot = slice(block * length, (block + 1) * length)
                for i in range(0, rows, STEP):
                    mask = cols & (line >= top - i) & (line < bottom - i)
                    at = pl.ds(i, STEP)
                    for l in range(layers):
                        for q in range(2):
                            value = held[index, l, q, at, :].astype(jnp.float32)
                            out_ref[l, q, at, spot] += jnp.where(mask, value, 0.0)


def body(object_slices, probe, measured, positions, counts):
    layers, _, tile_rows, tile_cols = object_slices.shape
    modes, _, length, _ = probe.shape
    slots = measured.shape[2]
    n_scan, n_obj = lax.axis_size("scan"), lax.axis_size("obj")
    chips = n_scan // CORES
    sizes = (n_scan, n_obj, tile_cols)
    smem = pl.BlockSpec(memory_space=pltpu.SMEM)
    vmem = pl.BlockSpec(memory_space=pltpu.VMEM)
    hbm = pl.BlockSpec(memory_space=pltpu.HBM)
    real, half = jnp.float32, jnp.bfloat16

    def call(kernel, outs, ins, scratch, name, flops, limit, *args):
        return pl.pallas_call(
            functools.partial(kernel[0], sizes, *kernel[1:]),
            out_shape=[jax.ShapeDtypeStruct(*o) for o in outs],
            in_specs=ins,
            out_specs=[vmem] * len(outs),
            scratch_shapes=scratch,
            compiler_params=pltpu.CompilerParams(vmem_limit_bytes=limit * MIB),
            cost_estimate=pl.CostEstimate(flops=flops, bytes_accessed=4 * MIB, transcendentals=0),
            name=name,
        )(*args)

    def across(block):
        return send(block, lambda s, o: (s ^ 1, o))

    def along(block, jump):
        return send(block, lambda s, o: (s + CORES * jump, o)) if jump else block

    def outward(block, sign):
        return send(block, lambda s, o: (s, o + (sign if s % CORES == 0 else -sign)))

    info = jnp.concatenate([counts[0], positions[0, 0].reshape(-1), jnp.zeros((3,), jnp.int32)])
    both = jnp.concatenate([info, send(info, lambda s, o: (s, o + 1))])
    info = lax.all_to_all(jnp.broadcast_to(both, (n_scan, 1, 16)), "scan", 0, 0, tiled=True)

    steps = [(0, CORES * j) for j in range(chips)] + [(1, CORES * j) for j in range(chips)]
    gathered = [along(measured[0, 0], j) for j in range(chips)]
    gathered += [across(block) for block in gathered]

    piece_shape = (2, length, length)
    field_shape = (modes, 2, length, length)
    wide = [pltpu.VMEM((layers, 2, tile_rows, 2 * length), real), pltpu.SemaphoreType.DMA]
    vus = [
        pltpu.VMEM((2 * length, modes * length), half),
        pltpu.VMEM((modes * length, 2 * length), half),
        pltpu.VMEM((modes * length, 2 * length), real),
    ]
    pair_flops = 2 * 2 * modes * 8 * length**3
    pieces = call(
        (cut_kernel,), [(piece_shape, half)] * 2, [smem, hbm], wide, "cut", MIB, LARGE, info, object_slices
    )
    pieces = [outward(piece, -1) for piece in pieces]
    (chosen,) = call(
        (choose_kernel, steps),
        [((length, length), measured.dtype)],
        [smem] + [hbm] * n_scan,
        [pltpu.SemaphoreType.DMA],
        "choose",
        MIB,
        LARGE,
        info,
        *gathered,
    )
    passed = send(chosen, lambda s, o: (s, o + 1) if s % CORES else None)
    mats, turned, own_part = call(
        (prep_kernel,),
        [((4, 2 * length, 2 * length), half), (field_shape, real), ((layers, *piece_shape), real)],
        [smem, hbm, vmem, vmem],
        wide,
        "prep",
        MIB,
        LARGE,
        info,
        object_slices,
        probe,
        dft_tables(length),
    )
    fresnel = fresnel_tables(length)
    arrived, patch = call(
        (first_kernel,),
        [(field_shape, real), (piece_shape, real)],
        [smem] + [vmem] * 5,
        vus,
        "first",
        pair_flops,
        SMALL,
        info,
        mats,
        fresnel,
        turned,
        own_part,
        pieces[0],
    )
    grad1, carried = call(
        (second_kernel,),
        [(piece_shape, half), ((2 * length, modes * length), half)],
        [smem] + [vmem] * 6,
        vus + [pltpu.VMEM(piece_shape, real)],
        "second",
        pair_flops,
        SMALL,
        info,
        mats,
        arrived,
        own_part,
        pieces[1],
        chosen,
        passed,
    )
    chunk_shape = (n_obj, chips, modes, length // n_obj, 2 * (length // n_scan))
    grad0, keep, give = call(
        (third_kernel,),
        [(piece_shape, half), (chunk_shape, half), (chunk_shape, half)],
        [smem] + [vmem] * 5,
        vus + [pltpu.VMEM(field_shape, real)],
        "third",
        pair_flops,
        SMALL,
        info,
        mats,
        fresnel,
        carried,
        patch,
        turned,
    )

    held = []
    for grad in (grad0, grad1):
        here = [along(grad, j) for j in range(chips)]
        there = [outward(block, 1) for block in here]
        held.append(here + there + [across(block) for block in here + there])
    kinds = [(kind, flip, jump) for flip in range(2) for kind in range(2) for jump in range(chips)]
    chunks = (keep.astype(real) + across(give).astype(real)).astype(half)
    chunks = lax.all_to_all(chunks, "obj", 0, 0, tiled=True)
    chunks = jnp.sum(chunks.astype(real), axis=0).astype(half)
    shares = [along(chunks[j], j) for j in range(chips)]
    factor = 1.0 / math.sqrt(n_scan * n_obj * slots // 2)
    object_grad, probe_grad = call(
        (place_kernel, kinds, factor),
        [
            ((layers, 2, tile_rows, tile_cols // n_scan), real),
            ((modes, 2, length // n_obj, length // n_scan), real),
        ],
        [smem] + [vmem] * chips + [hbm] * (2 * n_scan * layers),
        [
            pltpu.VMEM((2 * n_scan, layers, *piece_shape), half),
            pltpu.SemaphoreType.DMA((2 * n_scan, layers)),
        ],
        "place",
        MIB,
        LARGE,
        info,
        *shares,
        *[held[l][index] for index in range(2 * n_scan) for l in range(layers)],
    )
    return (object_grad, probe_grad)


def solution(mesh):
    return jax.shard_map(
        body,
        mesh=mesh,
        in_specs=(
            P(None, None, "obj", None),
            P(),
            P("scan", "obj", None, None, None),
            P("scan", "obj", None, None),
            P("scan", "obj"),
        ),
        out_specs=(P(None, None, "obj", "scan"), P(None, None, "obj", "scan")),
        check_vma=False,
    )
```

```python
import functools
import math

import jax
import jax.numpy as jnp
import ml_dtypes
import numpy as np
from jax import lax
from jax.experimental import pallas as pl
from jax.experimental.pallas import tpu as pltpu
from jax.sharding import PartitionSpec as P

AXES = ("scan", "obj")
CORES = 2
MIB = 1 << 20
SMALL, LARGE = 20, 58


def dft_tables(length):
    index = np.arange(length)
    angles = (index[:, None] * index[None, :] % length) * (2.0 * math.pi / length)
    parts = np.stack([np.cos(angles), -np.sin(angles)]) / math.sqrt(length)
    return parts.astype(np.float32).astype(ml_dtypes.bfloat16).astype(np.float32)


def fresnel_tables(length):
    index = np.arange(length)
    freqs = np.where(index < length // 2, index, index - length)
    squares = freqs * freqs
    phases = ((squares[:, None] + squares[None, :]) % (4 * length)) * (2.0 * math.pi / (4 * length))
    return np.stack([np.cos(phases), -np.sin(phases)]).astype(np.float32)


def send(block, move):
    n_scan, n_obj = lax.axis_size("scan"), lax.axis_size("obj")
    route = []
    for s in range(n_scan):
        for o in range(n_obj):
            goal = move(s, o)
            if goal is not None:
                route.append((s * n_obj + o, goal[0] % n_scan * n_obj + goal[1] % n_obj))
    return lax.ppermute(block, AXES, route)


OWN, PREVIOUS = 0, 1


def live(info, tile, rank, n_scan):
    def entry(a, j):
        return info[a, 0, 8 * tile + j]

    source, slot = jnp.int32(0), jnp.int32(0)
    before = jnp.int32(0)
    for a in range(n_scan):
        count = entry(a, 0)
        here = (rank >= before) & (rank < before + count)
        source = jnp.where(here, a, source)
        slot = jnp.where(here, rank - before, slot)
        before += count
    return source, slot, entry(source, 1 + 2 * slot), entry(source, 2 + 2 * slot)


def place_of(n_scan):
    me = lax.axis_index("scan")
    core = lax.rem(me, CORES)
    chip = lax.div(me, CORES)
    return chip, core, chip + core * (n_scan // CORES)


def column_block(col, length, tile_cols):
    base = jnp.minimum(lax.div(col, length), tile_cols // length - 2)
    return base, col - base * length


STEP = 32


def lanes(length):
    return lax.broadcasted_iota(jnp.int32, (STEP, length), 1)


def lines(length):
    return lax.broadcasted_iota(jnp.int32, (STEP, length), 0)


def mul(ar, ai, br, bi):
    return ar * br - ai * bi, ar * bi + ai * br


def cmul(ar, ai, br, bi):
    return ar * br + ai * bi, ar * bi - ai * br


def fetch_columns(object_ref, wide, sems, base, length):
    layers, _, rows, _ = wide.shape
    start = pl.multiple_of(base * length, length)
    copies = []
    for l in range(layers):
        for q in range(2):
            for h in range(2):
                at = pl.ds(h * (rows // 2), rows // 2)
                copy = pltpu.make_async_copy(
                    object_ref.at[l, q, at, pl.ds(start, 2 * length)], wide.at[l, q, at], sems.at[l, q, h]
                )
                copy.start()
                copies.append(copy)
    return copies


def pick_columns(wide, l, q, at, off, length):
    return jnp.where(lanes(length) >= off, wide[l, q, at, :length], wide[l, q, at, length:])


def pick_kernel(sizes, own, info, object_ref, out_ref, wide, sems):
    n_scan, _, tile_cols = sizes
    layers, _, rows, length = out_ref.shape
    _, core, rank = place_of(n_scan)
    _, _, _, col = live(info, core if own else 1 - core, rank, n_scan)
    base, off = column_block(col, length, tile_cols)
    copies = fetch_columns(object_ref, wide, sems, base, length)
    for l in range(layers):
        for q in range(2):
            for i in range(0, rows, STEP):
                if i % (rows // 2) == 0:
                    copies.pop(0).wait()
                at = pl.ds(i, STEP)
                out_ref[l, q, at, :] = pick_columns(wide, l, q, at, off, length).astype(out_ref.dtype)


def choose_kernel(sizes, steps, info, *refs):
    n_scan, _, _ = sizes
    sources = refs[:n_scan]
    out_ref, sem = refs[n_scan:]
    me = lax.axis_index("scan")
    _, _, rank = place_of(n_scan)
    source, slot, _, _ = live(info, OWN, rank, n_scan)
    for (flip, jump), candidate in zip(steps, sources):
        @pl.when(source == lax.rem((me ^ flip) - jump + n_scan, n_scan))
        def _():
            copy = pltpu.make_async_copy(candidate.at[slot], out_ref, sem)
            copy.start()
            copy.wait()


def prep_kernel(sizes, info, probe_ref, dft_ref, mats, p_ref):
    n_scan, _, tile_cols = sizes
    modes, _, length, _ = probe_ref.shape
    _, core, rank = place_of(n_scan)
    _, _, row, col = live(info, core, rank, n_scan)
    _, off = column_block(col, length, tile_cols)
    turn = lax.rem(off, length)

    def put(k, real, imag):
        mats[k, :length, :length] = real.astype(jnp.bfloat16)
        mats[k, length:, length:] = real.astype(jnp.bfloat16)
        mats[k, :length, length:] = imag.astype(jnp.bfloat16)
        mats[k, length:, :length] = (-imag).astype(jnp.bfloat16)

    real, imag = dft_ref[0], dft_ref[1]
    put(0, pltpu.roll(real, row, 1), -pltpu.roll(imag, row, 1))
    put(1, pltpu.roll(real, turn, 0), pltpu.roll(imag, turn, 0))
    put(2, pltpu.roll(real, row, 0), pltpu.roll(imag, row, 0))
    put(3, pltpu.roll(real, turn, 1), -pltpu.roll(imag, turn, 1))
    for m in range(modes):
        for q in range(2):
            p_ref[m, q] = pltpu.roll(pltpu.roll(probe_ref[m, q], row, 0), turn, 1)


def put_v(v_ref, length, m, i, real, imag):
    spot = slice(m * length, (m + 1) * length)
    v_ref[pl.ds(i, STEP), spot] = real.astype(jnp.bfloat16)
    v_ref[pl.ds(length + i, STEP), spot] = imag.astype(jnp.bfloat16)


def get_s(s_ref, length, m, i):
    at = pl.ds(m * length + i, STEP)
    return s_ref[at, :length], s_ref[at, length:]


def transform(mats, inverse, v_ref, u_ref, s_ref):
    length = mats.shape[1] // 2
    mid = jnp.dot(mats[2 * inverse], v_ref[...], preferred_element_type=jnp.float32).astype(jnp.bfloat16)
    for m in range(v_ref.shape[1] // length):
        for q in range(2):
            u_ref[m * length : (m + 1) * length, q * length : (q + 1) * length] = mid[
                q * length : (q + 1) * length, m * length : (m + 1) * length
            ]
    s_ref[...] = jnp.dot(u_ref[...], mats[2 * inverse + 1], preferred_element_type=jnp.float32)


def propagate(product, mats, fresnel_ref, v_in, v_ref, u_ref, s_ref):
    length = mats.shape[1] // 2
    transform(mats, 0, v_in, u_ref, s_ref)
    for i in range(0, length, STEP):
        at = pl.ds(i, STEP)
        kr, ki = fresnel_ref[0, at, :], fresnel_ref[1, at, :]
        for m in range(v_ref.shape[1] // length):
            put_v(v_ref, length, m, i, *product(kr, ki, *get_s(s_ref, length, m, i)))
    transform(mats, 1, v_ref, u_ref, s_ref)


def own_rows(sizes, info, length):
    n_scan, _, _ = sizes
    _, core, rank = place_of(n_scan)
    _, _, row, _ = live(info, core, rank, n_scan)
    return jnp.where(core == 0, row, 0), jnp.where(core == 0, length, row)


def join(own, piece, i, bounds):
    line = lines(own.shape[1])
    return jnp.where((line >= bounds[0] - i) & (line < bounds[1] - i), own, piece.astype(jnp.float32))


def pattern_kernel(
    sizes, info, mats, fresnel_ref, p_ref, xo_ref, piece, meas_here, meas_sent,
    grad_ref, keep_ref, give_ref, v_ref, u_ref, s_ref, x_ref, a_ref,
):
    n_scan, n_obj, tile_cols = sizes
    modes, _, length, _ = p_ref.shape
    bounds = own_rows(sizes, info, length)
    chip, core, rank = place_of(n_scan)
    chips = n_scan // CORES
    _, _, row, col = live(info, core, rank, n_scan)
    _, off = column_block(col, length, tile_cols)
    for l in range(x_ref.shape[0]):
        for q in range(2):
            for i in range(0, length, STEP):
                at = pl.ds(i, STEP)
                x_ref[l, q, at, :] = join(xo_ref[l, q, at, :], piece[l, q, at, :], i, bounds)
    for i in range(0, length, STEP):
        at = pl.ds(i, STEP)
        xr, xi = x_ref[0, 0, at, :], x_ref[0, 1, at, :]
        for m in range(modes):
            put_v(v_ref, length, m, i, *mul(p_ref[m, 0, at, :], p_ref[m, 1, at, :], xr, xi))
    propagate(mul, mats, fresnel_ref, v_ref, v_ref, u_ref, s_ref)
    for i in range(0, length, STEP):
        at = pl.ds(i, STEP)
        xr, xi = x_ref[1, 0, at, :], x_ref[1, 1, at, :]
        for m in range(modes):
            ar, ai = get_s(s_ref, length, m, i)
            a_ref[m, 0, at, :] = ar
            a_ref[m, 1, at, :] = ai
            put_v(v_ref, length, m, i, *mul(ar, ai, xr, xi))
    transform(mats, 0, v_ref, u_ref, s_ref)
    for i in range(0, length, STEP):
        at = pl.ds(i, STEP)
        here, sent = meas_here[at, :].astype(jnp.float32), meas_sent[at, :].astype(jnp.float32)
        misfit = -jnp.where(core == 0, here, sent)
        for m in range(modes):
            fr, fi = get_s(s_ref, length, m, i)
            misfit += fr * fr + fi * fi
        for m in range(modes):
            fr, fi = get_s(s_ref, length, m, i)
            put_v(v_ref, length, m, i, misfit * fr, misfit * fi)
    transform(mats, 1, v_ref, u_ref, s_ref)
    for i in range(0, length, STEP):
        at = pl.ds(i, STEP)
        gr = gi = 0.0
        for m in range(modes):
            cr, ci = get_s(s_ref, length, m, i)
            dr, di = cmul(a_ref[m, 0, at, :], a_ref[m, 1, at, :], cr, ci)
            gr, gi = gr + dr, gi + di
            put_v(v_ref, length, m, i, *cmul(x_ref[1, 0, at, :], x_ref[1, 1, at, :], cr, ci))
        grad_ref[1, 0, at, :] = gr.astype(grad_ref.dtype)
        grad_ref[1, 1, at, :] = gi.astype(grad_ref.dtype)
    propagate(cmul, mats, fresnel_ref, v_ref, v_ref, u_ref, s_ref)
    for i in range(0, length, STEP):
        at = pl.ds(i, STEP)
        gr = gi = 0.0
        for m in range(modes):
            cr, ci = get_s(s_ref, length, m, i)
            dr, di = cmul(p_ref[m, 0, at, :], p_ref[m, 1, at, :], cr, ci)
            gr, gi = gr + dr, gi + di
            a_ref[m, 0, at, :], a_ref[m, 1, at, :] = cmul(x_ref[0, 0, at, :], x_ref[0, 1, at, :], cr, ci)
        grad_ref[0, 0, at, :] = gr.astype(grad_ref.dtype)
        grad_ref[0, 1, at, :] = gi.astype(grad_ref.dtype)
    row_back = lax.rem(length - row, length)
    col_back = lax.rem(2 * length - off, length)
    per_row, per_col = length // n_obj, length // n_scan
    lane = lax.broadcasted_iota(jnp.int32, (length, 128), 1)
    for m in range(modes):
        for q in range(2):
            a_ref[m, q] = pltpu.roll(pltpu.roll(a_ref[m, q], row_back, 0), col_back, 1)
        for s in range(n_scan):
            first, shift = s * per_col // 128 * 128, s * per_col % 128
            real = a_ref[m, 0, :, first : first + 128]
            imag = a_ref[m, 1, :, first : first + 128]
            real = pltpu.roll(real, (128 - shift) % 128, 1) if shift else real
            imag = pltpu.roll(imag, (per_col - shift) % 128, 1) if shift != per_col else imag
            both = jnp.where(lane < per_col, real, imag)[:, : 2 * per_col]
            apart = lax.rem(s // CORES - chip + chips, chips)
            for mine, ref in ((core, keep_ref), (1 - core, give_ref)):
                @pl.when(mine == s % CORES)
                def _():
                    for o in range(n_obj):
                        ref[o, apart, m] = both[o * per_row : (o + 1) * per_row].astype(ref.dtype)


def place_kernel(sizes, kinds, factor, *refs):
    n_scan, _, tile_cols = sizes
    chips = n_scan // CORES
    layers = refs[-4].shape[0]
    info = refs[0]
    shares = refs[1 : 1 + chips]
    patches = refs[1 + chips : -4]
    out_ref, probe_out, held, sems = refs[-4:]
    _, _, rows, width = out_ref.shape
    length = patches[0].shape[3]
    me = lax.axis_index("scan")
    chip, core, _ = place_of(n_scan)
    blocks = width // length
    first_block = me * blocks
    spots = []
    for index, (kind, flip, jump) in enumerate(kinds):
        other = core ^ flip
        tile = other ^ kind
        rank = lax.rem(chip - jump + chips, chips) + other * chips
        _, _, row, col = live(info, tile, rank, n_scan)
        base, off = column_block(col, length, tile_cols)
        top, bottom = jnp.where(tile == OWN, row, 0), jnp.where(tile == OWN, rows, row)
        meets = (base + 1 >= first_block) & (base < first_block + blocks)
        copies = [
            pltpu.make_async_copy(patches[index].at[l], held.at[index, l], sems.at[index, l])
            for l in range(layers)
        ]
        spots.append((base, off, top, bottom, meets, copies))

        @pl.when(meets)
        def _():
            for copy in copies:
                copy.start()

    out_ref[...] = jnp.zeros(out_ref.shape, jnp.float32)
    per_col = probe_out.shape[3]
    for m in range(probe_out.shape[0]):
        total = sum(share[m].astype(jnp.float32) for share in shares) * factor
        probe_out[m, 0] = total[:, :per_col]
        probe_out[m, 1] = total[:, per_col:]
    lane, line = lanes(length), lines(length)
    for index, (base, off, top, bottom, meets, copies) in enumerate(spots):
        @pl.when(meets)
        def _():
            for copy in copies:
                copy.wait()
        for block in range(blocks):
            first, second = base == first_block + block, base + 1 == first_block + block
            left = jnp.where(first, off, 0)
            right = jnp.where(first, length, off)

            @pl.when(first | second)
            def _():
                cols = (lane >= left) & (lane < right)
                spot = slice(block * length, (block + 1) * length)
                for i in range(0, rows, STEP):
                    mask = cols & (line >= top - i) & (line < bottom - i)
                    at = pl.ds(i, STEP)
                    for l in range(layers):
                        for q in range(2):
                            value = held[index, l, q, at, :].astype(jnp.float32)
                            out_ref[l, q, at, spot] += jnp.where(mask, value, 0.0)


def body(object_slices, probe, measured, positions, counts):
    layers, _, tile_rows, tile_cols = object_slices.shape
    modes, _, length, _ = probe.shape
    slots = measured.shape[2]
    n_scan, n_obj = lax.axis_size("scan"), lax.axis_size("obj")
    chips = n_scan // CORES
    sizes = (n_scan, n_obj, tile_cols)
    smem = pl.BlockSpec(memory_space=pltpu.SMEM)
    vmem = pl.BlockSpec(memory_space=pltpu.VMEM)
    hbm = pl.BlockSpec(memory_space=pltpu.HBM)
    real, half = jnp.float32, jnp.bfloat16

    def call(kernel, outs, ins, scratch, name, flops, limit, *args):
        return pl.pallas_call(
            functools.partial(kernel[0], sizes, *kernel[1:]),
            out_shape=[jax.ShapeDtypeStruct(*o) for o in outs],
            in_specs=ins,
            out_specs=[vmem] * len(outs),
            scratch_shapes=scratch,
            compiler_params=pltpu.CompilerParams(vmem_limit_bytes=limit * MIB),
            cost_estimate=pl.CostEstimate(flops=flops, bytes_accessed=4 * MIB, transcendentals=0),
            name=name,
        )(*args)

    def across(block):
        return send(block, lambda s, o: (s ^ 1, o))

    def along(block, jump):
        return send(block, lambda s, o: (s + CORES * jump, o)) if jump else block

    def outward(block, sign):
        return send(block, lambda s, o: (s, o + (sign if s % CORES == 0 else -sign)))

    info = jnp.concatenate([counts[0], positions[0, 0].reshape(-1), jnp.zeros((3,), jnp.int32)])
    both = jnp.concatenate([info, send(info, lambda s, o: (s, o + 1))])
    info = lax.all_to_all(jnp.broadcast_to(both, (n_scan, 1, 16)), "scan", 0, 0, tiled=True)

    measured, info = lax.optimization_barrier((measured, info))
    steps = [(0, CORES * j) for j in range(chips)] + [(1, CORES * j) for j in range(chips)]
    gathered = [along(measured[0, 0], j) for j in range(chips)]
    gathered += [across(block) for block in gathered]

    patch_shape = (layers, 2, length, length)
    field_shape = (modes, 2, length, length)
    wide = [pltpu.VMEM((layers, 2, tile_rows, 2 * length), real), pltpu.SemaphoreType.DMA((layers, 2, 2))]
    (piece,) = call(
        (pick_kernel, False), [(patch_shape, half)], [smem, hbm], wide, "cut", MIB, LARGE, info, object_slices
    )
    piece = outward(piece, -1)
    (own_part,) = call(
        (pick_kernel, True), [(patch_shape, real)], [smem, hbm], wide, "own", MIB, LARGE, info, object_slices
    )
    (chosen,) = call(
        (choose_kernel, steps),
        [((length, length), measured.dtype)],
        [smem] + [hbm] * n_scan,
        [pltpu.SemaphoreType.DMA],
        "choose",
        MIB,
        LARGE,
        info,
        *gathered,
    )
    passed = send(chosen, lambda s, o: (s, o + 1) if s % CORES else None)
    mats, turned = call(
        (prep_kernel,),
        [((4, 2 * length, 2 * length), half), (field_shape, real)],
        [smem, vmem, vmem],
        [],
        "prep",
        MIB,
        SMALL,
        info,
        probe,
        dft_tables(length),
    )
    chunk_shape = (n_obj, chips, modes, length // n_obj, 2 * (length // n_scan))
    grad, keep, give = call(
        (pattern_kernel,),
        [(patch_shape, half), (chunk_shape, half), (chunk_shape, half)],
        [smem] + [vmem] * 7,
        [
            pltpu.VMEM((2 * length, modes * length), half),
            pltpu.VMEM((modes * length, 2 * length), half),
            pltpu.VMEM((modes * length, 2 * length), real),
            pltpu.VMEM(patch_shape, real),
            pltpu.VMEM(field_shape, real),
        ],
        "pattern",
        3 * 2 * 2 * modes * 8 * length**3,
        SMALL,
        info,
        mats,
        fresnel_tables(length),
        turned,
        own_part,
        piece,
        chosen,
        passed,
    )

    here = [along(grad, j) for j in range(chips)]
    there = [outward(block, 1) for block in here]
    held = here + there + [across(block) for block in here + there]
    kinds = [(kind, flip, jump) for flip in range(2) for kind in range(2) for jump in range(chips)]
    chunks = (keep.astype(real) + across(give).astype(real)).astype(half)
    chunks = lax.all_to_all(chunks, "obj", 0, 0, tiled=True)
    chunks = jnp.sum(chunks.astype(real), axis=0).astype(half)
    shares = [along(chunks[j], j) for j in range(chips)]
    factor = 1.0 / math.sqrt(n_scan * n_obj * slots // 2)
    object_grad, probe_grad = call(
        (place_kernel, kinds, factor),
        [
            ((layers, 2, tile_rows, tile_cols // n_scan), real),
            ((modes, 2, length // n_obj, length // n_scan), real),
        ],
        [smem] + [vmem] * chips + [hbm] * (2 * n_scan),
        [
            pltpu.VMEM((2 * n_scan, layers, *patch_shape[1:]), half),
            pltpu.SemaphoreType.DMA((2 * n_scan, layers)),
        ],
        "place",
        MIB,
        LARGE,
        info,
        *shares,
        *held,
    )
    return (object_grad, probe_grad)


def solution(mesh):
    return jax.shard_map(
        body,
        mesh=mesh,
        in_specs=(
            P(None, None, "obj", None),
            P(),
            P("scan", "obj", None, None, None),
            P("scan", "obj", None, None),
            P("scan", "obj"),
        ),
        out_specs=(P(None, None, "obj", "scan"), P(None, None, "obj", "scan")),
        check_vma=False,
    )
```

```python
import functools
import math

import jax
import jax.numpy as jnp
import ml_dtypes
import numpy as np
from jax import lax
from jax.experimental import pallas as pl
from jax.experimental.pallas import tpu as pltpu
from jax.sharding import PartitionSpec as P

AXES = ("scan", "obj")
CORES = 2
MIB = 1 << 20
SMALL, LARGE = 20, 56


def dft_tables(length):
    index = np.arange(length)
    angles = (index[:, None] * index[None, :] % length) * (2.0 * math.pi / length)
    parts = np.stack([np.cos(angles), -np.sin(angles)]) / math.sqrt(length)
    return parts.astype(np.float32).astype(ml_dtypes.bfloat16).astype(np.float32)


def fresnel_tables(length):
    index = np.arange(length)
    freqs = np.where(index < length // 2, index, index - length)
    squares = freqs * freqs
    phases = ((squares[:, None] + squares[None, :]) % (4 * length)) * (2.0 * math.pi / (4 * length))
    return np.stack([np.cos(phases), -np.sin(phases)]).astype(np.float32)


def send(block, move):
    n_scan, n_obj = lax.axis_size("scan"), lax.axis_size("obj")
    route = []
    for s in range(n_scan):
        for o in range(n_obj):
            goal = move(s, o)
            if goal is not None:
                route.append((s * n_obj + o, goal[0] % n_scan * n_obj + goal[1] % n_obj))
    return lax.ppermute(block, AXES, route)


OWN, PREVIOUS = 0, 1


def live(info, tile, rank, n_scan):
    def entry(a, j):
        return info[a, 0, 8 * tile + j]

    source, slot = jnp.int32(0), jnp.int32(0)
    before = jnp.int32(0)
    for a in range(n_scan):
        count = entry(a, 0)
        here = (rank >= before) & (rank < before + count)
        source = jnp.where(here, a, source)
        slot = jnp.where(here, rank - before, slot)
        before += count
    return source, slot, entry(source, 1 + 2 * slot), entry(source, 2 + 2 * slot)


def place_of(n_scan):
    me = lax.axis_index("scan")
    core = lax.rem(me, CORES)
    chip = lax.div(me, CORES)
    return chip, core, chip + core * (n_scan // CORES)


def column_block(col, length, tile_cols):
    base = jnp.minimum(lax.div(col, length), tile_cols // length - 2)
    return base, col - base * length


STEP = 32


def lanes(length):
    return lax.broadcasted_iota(jnp.int32, (STEP, length), 1)


def lines(length):
    return lax.broadcasted_iota(jnp.int32, (STEP, length), 0)


def mul(ar, ai, br, bi):
    return ar * br - ai * bi, ar * bi + ai * br


def cmul(ar, ai, br, bi):
    return ar * br + ai * bi, ar * bi - ai * br


def fetch_columns(object_ref, wide, sems, base, length):
    layers, _, rows, _ = wide.shape
    start = pl.multiple_of(base * length, length)
    copies = []
    for l in range(layers):
        for q in range(2):
            for h in range(2):
                at = pl.ds(h * (rows // 2), rows // 2)
                copy = pltpu.make_async_copy(
                    object_ref.at[l, q, at, pl.ds(start, 2 * length)], wide.at[l, q, at], sems.at[l, q, h]
                )
                copy.start()
                copies.append(copy)
    return copies


def pick_columns(wide, l, q, at, off, length):
    return jnp.where(lanes(length) >= off, wide[l, q, at, :length], wide[l, q, at, length:])


def pick_kernel(sizes, own, info, object_ref, out_ref, wide, sems):
    n_scan, _, tile_cols = sizes
    layers, _, rows, length = out_ref.shape
    _, core, rank = place_of(n_scan)
    _, _, _, col = live(info, core if own else 1 - core, rank, n_scan)
    base, off = column_block(col, length, tile_cols)
    copies = fetch_columns(object_ref, wide, sems, base, length)
    for l in range(layers):
        for q in range(2):
            for i in range(0, rows, STEP):
                if i % (rows // 2) == 0:
                    copies.pop(0).wait()
                at = pl.ds(i, STEP)
                out_ref[l, q, at, :] = pick_columns(wide, l, q, at, off, length).astype(out_ref.dtype)


def choose_kernel(sizes, steps, info, *refs):
    n_scan, _, _ = sizes
    sources = refs[:n_scan]
    out_ref, sem = refs[n_scan:]
    me = lax.axis_index("scan")
    _, _, rank = place_of(n_scan)
    source, slot, _, _ = live(info, OWN, rank, n_scan)
    for (flip, jump), candidate in zip(steps, sources):
        @pl.when(source == lax.rem((me ^ flip) - jump + n_scan, n_scan))
        def _():
            copy = pltpu.make_async_copy(candidate.at[slot], out_ref, sem)
            copy.start()
            copy.wait()


def prep_kernel(sizes, info, probe_ref, dft_ref, mats, p_ref):
    n_scan, _, tile_cols = sizes
    modes, _, length, _ = probe_ref.shape
    _, core, rank = place_of(n_scan)
    _, _, row, col = live(info, core, rank, n_scan)
    _, off = column_block(col, length, tile_cols)
    turn = lax.rem(off, length)

    def put(k, real, imag):
        mats[k, :length, :length] = real.astype(jnp.bfloat16)
        mats[k, length:, length:] = real.astype(jnp.bfloat16)
        mats[k, :length, length:] = imag.astype(jnp.bfloat16)
        mats[k, length:, :length] = (-imag).astype(jnp.bfloat16)

    real, imag = dft_ref[0], dft_ref[1]
    put(0, pltpu.roll(real, row, 1), -pltpu.roll(imag, row, 1))
    put(1, pltpu.roll(real, turn, 0), pltpu.roll(imag, turn, 0))
    put(2, pltpu.roll(real, row, 0), pltpu.roll(imag, row, 0))
    put(3, pltpu.roll(real, turn, 1), -pltpu.roll(imag, turn, 1))
    for m in range(modes):
        for q in range(2):
            p_ref[m, q] = pltpu.roll(pltpu.roll(probe_ref[m, q], row, 0), turn, 1)


def put_v(v_ref, length, m, i, real, imag):
    spot = slice(m * length, (m + 1) * length)
    v_ref[pl.ds(i, STEP), spot] = real.astype(jnp.bfloat16)
    v_ref[pl.ds(length + i, STEP), spot] = imag.astype(jnp.bfloat16)


def get_s(s_ref, length, m, i):
    at = pl.ds(m * length + i, STEP)
    return s_ref[at, :length], s_ref[at, length:]


def transform(mats, inverse, v_ref, u_ref, s_ref):
    length = mats.shape[1] // 2
    mid = jnp.dot(mats[2 * inverse], v_ref[...], preferred_element_type=jnp.float32).astype(jnp.bfloat16)
    for m in range(v_ref.shape[1] // length):
        for q in range(2):
            u_ref[m * length : (m + 1) * length, q * length : (q + 1) * length] = mid[
                q * length : (q + 1) * length, m * length : (m + 1) * length
            ]
    s_ref[...] = jnp.dot(u_ref[...], mats[2 * inverse + 1], preferred_element_type=jnp.float32)


def propagate(product, mats, fresnel_ref, v_in, v_ref, u_ref, s_ref):
    length = mats.shape[1] // 2
    transform(mats, 0, v_in, u_ref, s_ref)
    for i in range(0, length, STEP):
        at = pl.ds(i, STEP)
        kr, ki = fresnel_ref[0, at, :], fresnel_ref[1, at, :]
        for m in range(v_ref.shape[1] // length):
            put_v(v_ref, length, m, i, *product(kr, ki, *get_s(s_ref, length, m, i)))
    transform(mats, 1, v_ref, u_ref, s_ref)


def own_rows(sizes, info, length):
    n_scan, _, _ = sizes
    _, core, rank = place_of(n_scan)
    _, _, row, _ = live(info, core, rank, n_scan)
    return jnp.where(core == 0, row, 0), jnp.where(core == 0, length, row)


def join(own, piece, i, bounds):
    line = lines(own.shape[1])
    return jnp.where((line >= bounds[0] - i) & (line < bounds[1] - i), own, piece.astype(jnp.float32))


def pattern_kernel(
    sizes, info, mats, fresnel_ref, p_ref, xo_ref, piece, meas_here, meas_sent,
    grad_ref, keep_ref, give_ref, v_ref, u_ref, s_ref, x_ref, a_ref,
):
    n_scan, n_obj, tile_cols = sizes
    modes, _, length, _ = p_ref.shape
    bounds = own_rows(sizes, info, length)
    chip, core, rank = place_of(n_scan)
    chips = n_scan // CORES
    _, _, row, col = live(info, core, rank, n_scan)
    _, off = column_block(col, length, tile_cols)
    for l in range(x_ref.shape[0]):
        for q in range(2):
            for i in range(0, length, STEP):
                at = pl.ds(i, STEP)
                x_ref[l, q, at, :] = join(xo_ref[l, q, at, :], piece[l, q, at, :], i, bounds)
    for i in range(0, length, STEP):
        at = pl.ds(i, STEP)
        xr, xi = x_ref[0, 0, at, :], x_ref[0, 1, at, :]
        for m in range(modes):
            put_v(v_ref, length, m, i, *mul(p_ref[m, 0, at, :], p_ref[m, 1, at, :], xr, xi))
    propagate(mul, mats, fresnel_ref, v_ref, v_ref, u_ref, s_ref)
    for i in range(0, length, STEP):
        at = pl.ds(i, STEP)
        xr, xi = x_ref[1, 0, at, :], x_ref[1, 1, at, :]
        for m in range(modes):
            ar, ai = get_s(s_ref, length, m, i)
            a_ref[m, 0, at, :] = ar
            a_ref[m, 1, at, :] = ai
            put_v(v_ref, length, m, i, *mul(ar, ai, xr, xi))
    transform(mats, 0, v_ref, u_ref, s_ref)
    for i in range(0, length, STEP):
        at = pl.ds(i, STEP)
        here, sent = meas_here[at, :].astype(jnp.float32), meas_sent[at, :].astype(jnp.float32)
        misfit = -jnp.where(core == 0, here, sent)
        for m in range(modes):
            fr, fi = get_s(s_ref, length, m, i)
            misfit += fr * fr + fi * fi
        for m in range(modes):
            fr, fi = get_s(s_ref, length, m, i)
            put_v(v_ref, length, m, i, misfit * fr, misfit * fi)
    transform(mats, 1, v_ref, u_ref, s_ref)
    for i in range(0, length, STEP):
        at = pl.ds(i, STEP)
        gr = gi = 0.0
        for m in range(modes):
            cr, ci = get_s(s_ref, length, m, i)
            dr, di = cmul(a_ref[m, 0, at, :], a_ref[m, 1, at, :], cr, ci)
            gr, gi = gr + dr, gi + di
            put_v(v_ref, length, m, i, *cmul(x_ref[1, 0, at, :], x_ref[1, 1, at, :], cr, ci))
        grad_ref[1, 0, at, :] = gr.astype(grad_ref.dtype)
        grad_ref[1, 1, at, :] = gi.astype(grad_ref.dtype)
    propagate(cmul, mats, fresnel_ref, v_ref, v_ref, u_ref, s_ref)
    for i in range(0, length, STEP):
        at = pl.ds(i, STEP)
        gr = gi = 0.0
        for m in range(modes):
            cr, ci = get_s(s_ref, length, m, i)
            dr, di = cmul(p_ref[m, 0, at, :], p_ref[m, 1, at, :], cr, ci)
            gr, gi = gr + dr, gi + di
            a_ref[m, 0, at, :], a_ref[m, 1, at, :] = cmul(x_ref[0, 0, at, :], x_ref[0, 1, at, :], cr, ci)
        grad_ref[0, 0, at, :] = gr.astype(grad_ref.dtype)
        grad_ref[0, 1, at, :] = gi.astype(grad_ref.dtype)
    row_back = lax.rem(length - row, length)
    col_back = lax.rem(2 * length - off, length)
    per_row, per_col = length // n_obj, length // n_scan
    lane = lax.broadcasted_iota(jnp.int32, (length, 128), 1)
    for m in range(modes):
        for q in range(2):
            a_ref[m, q] = pltpu.roll(pltpu.roll(a_ref[m, q], row_back, 0), col_back, 1)
        for s in range(n_scan):
            first, shift = s * per_col // 128 * 128, s * per_col % 128
            real = a_ref[m, 0, :, first : first + 128]
            imag = a_ref[m, 1, :, first : first + 128]
            real = pltpu.roll(real, (128 - shift) % 128, 1) if shift else real
            imag = pltpu.roll(imag, (per_col - shift) % 128, 1) if shift != per_col else imag
            both = jnp.where(lane < per_col, real, imag)[:, : 2 * per_col]
            apart = lax.rem(s // CORES - chip + chips, chips)
            for mine, ref in ((core, keep_ref), (1 - core, give_ref)):
                @pl.when(mine == s % CORES)
                def _():
                    for o in range(n_obj):
                        ref[o, apart, m] = both[o * per_row : (o + 1) * per_row].astype(ref.dtype)


def place_kernel(sizes, kinds, factor, *refs):
    n_scan, _, tile_cols = sizes
    chips = n_scan // CORES
    layers = refs[-4].shape[0]
    info = refs[0]
    shares = refs[1 : 1 + chips]
    patches = refs[1 + chips : -4]
    out_ref, probe_out, held, sems = refs[-4:]
    _, _, rows, width = out_ref.shape
    length = patches[0].shape[3]
    me = lax.axis_index("scan")
    chip, core, _ = place_of(n_scan)
    blocks = width // length
    first_block = me * blocks
    spots = []
    for index, (kind, flip, jump) in enumerate(kinds):
        other = core ^ flip
        tile = other ^ kind
        rank = lax.rem(chip - jump + chips, chips) + other * chips
        _, _, row, col = live(info, tile, rank, n_scan)
        base, off = column_block(col, length, tile_cols)
        top, bottom = jnp.where(tile == OWN, row, 0), jnp.where(tile == OWN, rows, row)
        meets = (base + 1 >= first_block) & (base < first_block + blocks)
        copies = [
            pltpu.make_async_copy(patches[index].at[l], held.at[index, l], sems.at[index, l])
            for l in range(layers)
        ]
        spots.append((base, off, top, bottom, meets, copies))

        @pl.when(meets)
        def _():
            for copy in copies:
                copy.start()

    out_ref[...] = jnp.zeros(out_ref.shape, jnp.float32)
    per_col = probe_out.shape[3]
    for m in range(probe_out.shape[0]):
        total = sum(share[m].astype(jnp.float32) for share in shares) * factor
        probe_out[m, 0] = total[:, :per_col]
        probe_out[m, 1] = total[:, per_col:]
    lane, line = lanes(length), lines(length)
    for index, (base, off, top, bottom, meets, copies) in enumerate(spots):
        @pl.when(meets)
        def _():
            for copy in copies:
                copy.wait()
        for block in range(blocks):
            first, second = base == first_block + block, base + 1 == first_block + block
            left = jnp.where(first, off, 0)
            right = jnp.where(first, length, off)

            @pl.when(first | second)
            def _():
                cols = (lane >= left) & (lane < right)
                spot = slice(block * length, (block + 1) * length)
                for i in range(0, rows, STEP):
                    mask = cols & (line >= top - i) & (line < bottom - i)
                    at = pl.ds(i, STEP)
                    for l in range(layers):
                        for q in range(2):
                            value = held[index, l, q, at, :].astype(jnp.float32)
                            out_ref[l, q, at, spot] += jnp.where(mask, value, 0.0)


def body(object_slices, probe, measured, positions, counts):
    layers, _, tile_rows, tile_cols = object_slices.shape
    modes, _, length, _ = probe.shape
    slots = measured.shape[2]
    n_scan, n_obj = lax.axis_size("scan"), lax.axis_size("obj")
    chips = n_scan // CORES
    sizes = (n_scan, n_obj, tile_cols)
    smem = pl.BlockSpec(memory_space=pltpu.SMEM)
    vmem = pl.BlockSpec(memory_space=pltpu.VMEM)
    hbm = pl.BlockSpec(memory_space=pltpu.HBM)
    real, half = jnp.float32, jnp.bfloat16

    def call(kernel, outs, ins, scratch, name, flops, limit, *args):
        return pl.pallas_call(
            functools.partial(kernel[0], sizes, *kernel[1:]),
            out_shape=[jax.ShapeDtypeStruct(*o) for o in outs],
            in_specs=ins,
            out_specs=[vmem] * len(outs),
            scratch_shapes=scratch,
            compiler_params=pltpu.CompilerParams(vmem_limit_bytes=limit * MIB),
            cost_estimate=pl.CostEstimate(flops=flops, bytes_accessed=4 * MIB, transcendentals=0),
            name=name,
        )(*args)

    def across(block):
        return send(block, lambda s, o: (s ^ 1, o))

    def along(block, jump):
        return send(block, lambda s, o: (s + CORES * jump, o)) if jump else block

    def outward(block, sign):
        return send(block, lambda s, o: (s, o + (sign if s % CORES == 0 else -sign)))

    info = jnp.concatenate([counts[0], positions[0, 0].reshape(-1), jnp.zeros((3,), jnp.int32)])
    both = jnp.concatenate([info, send(info, lambda s, o: (s, o + 1))])
    info = lax.all_to_all(jnp.broadcast_to(both, (n_scan, 1, 16)), "scan", 0, 0, tiled=True)

    measured, info = lax.optimization_barrier((measured, info))
    steps = [(0, CORES * j) for j in range(chips)] + [(1, CORES * j) for j in range(chips)]
    def shifted(block, flip, jump):
        return send(block, lambda s, o: ((s ^ flip) + jump, o)) if flip or jump else block

    gathered = [shifted(measured[0, 0], flip, jump) for flip, jump in steps]

    patch_shape = (layers, 2, length, length)
    field_shape = (modes, 2, length, length)
    wide = [pltpu.VMEM((layers, 2, tile_rows, 2 * length), real), pltpu.SemaphoreType.DMA((layers, 2, 2))]
    (piece,) = call(
        (pick_kernel, False), [(patch_shape, half)], [smem, hbm], wide, "cut", MIB, LARGE, info, object_slices
    )
    piece = outward(piece, -1)
    (own_part,) = call(
        (pick_kernel, True), [(patch_shape, real)], [smem, hbm], wide, "own", MIB, LARGE, info, object_slices
    )
    mats, turned = call(
        (prep_kernel,),
        [((4, 2 * length, 2 * length), half), (field_shape, real)],
        [smem, vmem, vmem],
        [],
        "prep",
        MIB,
        SMALL,
        info,
        probe,
        dft_tables(length),
    )
    gathered, mats, own_part = lax.optimization_barrier((gathered, mats, own_part))
    (chosen,) = call(
        (choose_kernel, steps),
        [((length, length), measured.dtype)],
        [smem] + [hbm] * n_scan,
        [pltpu.SemaphoreType.DMA],
        "choose",
        MIB,
        LARGE,
        info,
        *gathered,
    )
    passed = send(chosen, lambda s, o: (s, o + 1) if s % CORES else None)
    chunk_shape = (n_obj, chips, modes, length // n_obj, 2 * (length // n_scan))
    grad, keep, give = call(
        (pattern_kernel,),
        [(patch_shape, half), (chunk_shape, half), (chunk_shape, half)],
        [smem] + [vmem] * 7,
        [
            pltpu.VMEM((2 * length, modes * length), half),
            pltpu.VMEM((modes * length, 2 * length), half),
            pltpu.VMEM((modes * length, 2 * length), real),
            pltpu.VMEM(patch_shape, real),
            pltpu.VMEM(field_shape, real),
        ],
        "pattern",
        3 * 2 * 2 * modes * 8 * length**3,
        SMALL,
        info,
        mats,
        fresnel_tables(length),
        turned,
        own_part,
        piece,
        chosen,
        passed,
    )

    here = [grad] + [along(grad, j) for j in range(1, chips)]
    chunks = (keep.astype(real) + across(give).astype(real)).astype(half)
    chunks = lax.all_to_all(chunks, "obj", 0, 0, tiled=True)
    late, chunks = lax.optimization_barrier((here[1:], chunks))
    there = [outward(block, 1) for block in here[:1] + late]
    held = here + there + [across(block) for block in here + there]
    kinds = [(kind, flip, jump) for flip in range(2) for kind in range(2) for jump in range(chips)]
    chunks = jnp.sum(chunks.astype(real), axis=0).astype(half)
    shares = [along(chunks[j], j) for j in range(chips)]
    factor = 1.0 / math.sqrt(n_scan * n_obj * slots // 2)
    object_grad, probe_grad = call(
        (place_kernel, kinds, factor),
        [
            ((layers, 2, tile_rows, tile_cols // n_scan), real),
            ((modes, 2, length // n_obj, length // n_scan), real),
        ],
        [smem] + [vmem] * chips + [hbm] * (2 * n_scan),
        [
            pltpu.VMEM((2 * n_scan, layers, *patch_shape[1:]), half),
            pltpu.SemaphoreType.DMA((2 * n_scan, layers)),
        ],
        "place",
        MIB,
        LARGE,
        info,
        *shares,
        *held,
    )
    return (object_grad, probe_grad)


def solution(mesh):
    return jax.shard_map(
        body,
        mesh=mesh,
        in_specs=(
            P(None, None, "obj", None),
            P(),
            P("scan", "obj", None, None, None),
            P("scan", "obj", None, None),
            P("scan", "obj"),
        ),
        out_specs=(P(None, None, "obj", "scan"), P(None, None, "obj", "scan")),
        check_vma=False,
    )
```

```python
import functools
import math

import jax
import jax.numpy as jnp
import ml_dtypes
import numpy as np
from jax import lax
from jax.experimental import pallas as pl
from jax.experimental.pallas import tpu as pltpu
from jax.sharding import PartitionSpec as P

AXES = ("scan", "obj")
CORES = 2
MIB = 1 << 20
SMALL, LARGE = 20, 56


def dft_tables(length):
    index = np.arange(length)
    angles = (index[:, None] * index[None, :] % length) * (2.0 * math.pi / length)
    parts = np.stack([np.cos(angles), -np.sin(angles)]) / math.sqrt(length)
    return parts.astype(np.float32).astype(ml_dtypes.bfloat16).astype(np.float32)


def fresnel_tables(length):
    index = np.arange(length)
    freqs = np.where(index < length // 2, index, index - length)
    squares = freqs * freqs
    phases = ((squares[:, None] + squares[None, :]) % (4 * length)) * (2.0 * math.pi / (4 * length))
    return np.stack([np.cos(phases), -np.sin(phases)]).astype(np.float32)


def send(block, move):
    n_scan, n_obj = lax.axis_size("scan"), lax.axis_size("obj")
    route = []
    for s in range(n_scan):
        for o in range(n_obj):
            goal = move(s, o)
            if goal is not None:
                route.append((s * n_obj + o, goal[0] % n_scan * n_obj + goal[1] % n_obj))
    return lax.ppermute(block, AXES, route)


OWN, PREVIOUS = 0, 1


def assigned(info, tile, target, n_scan):
    def entry(a, j):
        return info[a, 0, 8 * tile + j]

    idle = entry(target, 0) == 0
    counts = [entry(a, 0) for a in range(n_scan)]
    rank = jnp.int32(0)
    for a in range(n_scan):
        rank += jnp.where((counts[a] == 0) & (a < target), 1, 0)
    source = jnp.int32(target)
    seen = jnp.int32(0)
    for a in range(n_scan):
        full = counts[a] == 2
        source = jnp.where(idle & full & (seen == rank), a, source)
        seen += jnp.where(full, 1, 0)
    slot = jnp.where(idle, 1, 0)
    return source, slot, entry(source, 1 + 2 * slot), entry(source, 2 + 2 * slot)


def column_block(col, length, tile_cols):
    base = jnp.minimum(lax.div(col, length), tile_cols // length - 2)
    return base, col - base * length


STEP = 32


def lanes(length):
    return lax.broadcasted_iota(jnp.int32, (STEP, length), 1)


def lines(length):
    return lax.broadcasted_iota(jnp.int32, (STEP, length), 0)


def mul(ar, ai, br, bi):
    return ar * br - ai * bi, ar * bi + ai * br


def cmul(ar, ai, br, bi):
    return ar * br + ai * bi, ar * bi - ai * br


def fetch_columns(object_ref, wide, sems, base, length):
    layers, _, rows, _ = wide.shape
    start = pl.multiple_of(base * length, length)
    copies = []
    for l in range(layers):
        for q in range(2):
            for h in range(2):
                at = pl.ds(h * (rows // 2), rows // 2)
                copy = pltpu.make_async_copy(
                    object_ref.at[l, q, at, pl.ds(start, 2 * length)], wide.at[l, q, at], sems.at[l, q, h]
                )
                copy.start()
                copies.append(copy)
    return copies


def pick_columns(wide, l, q, at, off, length):
    return jnp.where(lanes(length) >= off, wide[l, q, at, :length], wide[l, q, at, length:])


def pick_kernel(sizes, own, info, object_ref, out_ref, wide, sems):
    n_scan, _, tile_cols = sizes
    layers, _, rows, length = out_ref.shape
    _, _, _, col = assigned(info, OWN if own else PREVIOUS, lax.axis_index("scan"), n_scan)
    base, off = column_block(col, length, tile_cols)
    copies = fetch_columns(object_ref, wide, sems, base, length)
    for l in range(layers):
        for q in range(2):
            for i in range(0, rows, STEP):
                if i % (rows // 2) == 0:
                    copies.pop(0).wait()
                at = pl.ds(i, STEP)
                out_ref[l, q, at, :] = pick_columns(wide, l, q, at, off, length).astype(out_ref.dtype)


def prep_kernel(sizes, info, probe_ref, dft_ref, mats, p_ref):
    n_scan, _, tile_cols = sizes
    modes, _, length, _ = probe_ref.shape
    _, _, row, col = assigned(info, OWN, lax.axis_index("scan"), n_scan)
    _, off = column_block(col, length, tile_cols)
    turn = lax.rem(off, length)

    def put(k, real, imag):
        mats[k, :length, :length] = real.astype(jnp.bfloat16)
        mats[k, length:, length:] = real.astype(jnp.bfloat16)
        mats[k, :length, length:] = imag.astype(jnp.bfloat16)
        mats[k, length:, :length] = (-imag).astype(jnp.bfloat16)

    real, imag = dft_ref[0], dft_ref[1]
    put(0, pltpu.roll(real, row, 1), -pltpu.roll(imag, row, 1))
    put(1, pltpu.roll(real, turn, 0), pltpu.roll(imag, turn, 0))
    put(2, pltpu.roll(real, row, 0), pltpu.roll(imag, row, 0))
    put(3, pltpu.roll(real, turn, 1), -pltpu.roll(imag, turn, 1))
    for m in range(modes):
        for q in range(2):
            p_ref[m, q] = pltpu.roll(pltpu.roll(probe_ref[m, q], row, 0), turn, 1)


def put_v(v_ref, length, m, i, real, imag):
    spot = slice(m * length, (m + 1) * length)
    v_ref[pl.ds(i, STEP), spot] = real.astype(jnp.bfloat16)
    v_ref[pl.ds(length + i, STEP), spot] = imag.astype(jnp.bfloat16)


def get_s(s_ref, length, m, i):
    at = pl.ds(m * length + i, STEP)
    return s_ref[at, :length], s_ref[at, length:]


def transform(mats, inverse, v_ref, u_ref, s_ref):
    length = mats.shape[1] // 2
    mid = jnp.dot(mats[2 * inverse], v_ref[...], preferred_element_type=jnp.float32).astype(jnp.bfloat16)
    for m in range(v_ref.shape[1] // length):
        for q in range(2):
            u_ref[m * length : (m + 1) * length, q * length : (q + 1) * length] = mid[
                q * length : (q + 1) * length, m * length : (m + 1) * length
            ]
    s_ref[...] = jnp.dot(u_ref[...], mats[2 * inverse + 1], preferred_element_type=jnp.float32)


def propagate(product, mats, fresnel_ref, v_in, v_ref, u_ref, s_ref):
    length = mats.shape[1] // 2
    transform(mats, 0, v_in, u_ref, s_ref)
    for i in range(0, length, STEP):
        at = pl.ds(i, STEP)
        kr, ki = fresnel_ref[0, at, :], fresnel_ref[1, at, :]
        for m in range(v_ref.shape[1] // length):
            put_v(v_ref, length, m, i, *product(kr, ki, *get_s(s_ref, length, m, i)))
    transform(mats, 1, v_ref, u_ref, s_ref)


def join(own, piece, i, row):
    return jnp.where(lines(own.shape[1]) >= row - i, own, piece.astype(jnp.float32))


def pattern_kernel(sizes, *refs):
    n_scan, n_obj, tile_cols = sizes
    info, mats, fresnel_ref, p_ref, xo_ref, piece, own_ref = refs[:7]
    others = refs[7 : 6 + n_scan]
    grad_ref, keep_ref, give_ref, v_ref, u_ref, s_ref, x_ref, a_ref, meas_ref = refs[6 + n_scan :]
    modes, _, length, _ = p_ref.shape
    me = lax.axis_index("scan")
    core, chip, chips = lax.rem(me, CORES), lax.div(me, CORES), n_scan // CORES
    source, slot, row, col = assigned(info, OWN, me, n_scan)
    _, off = column_block(col, length, tile_cols)

    @pl.when(slot == 0)
    def _():
        meas_ref[...] = own_ref[0]

    for k in range(1, n_scan):
        @pl.when((slot == 1) & (source == lax.rem(me - k + n_scan, n_scan)))
        def _():
            meas_ref[...] = others[k - 1][...]

    for l in range(x_ref.shape[0]):
        for q in range(2):
            for i in range(0, length, STEP):
                at = pl.ds(i, STEP)
                x_ref[l, q, at, :] = join(xo_ref[l, q, at, :], piece[l, q, at, :], i, row)
    for i in range(0, length, STEP):
        at = pl.ds(i, STEP)
        xr, xi = x_ref[0, 0, at, :], x_ref[0, 1, at, :]
        for m in range(modes):
            put_v(v_ref, length, m, i, *mul(p_ref[m, 0, at, :], p_ref[m, 1, at, :], xr, xi))
    propagate(mul, mats, fresnel_ref, v_ref, v_ref, u_ref, s_ref)
    for i in range(0, length, STEP):
        at = pl.ds(i, STEP)
        xr, xi = x_ref[1, 0, at, :], x_ref[1, 1, at, :]
        for m in range(modes):
            ar, ai = get_s(s_ref, length, m, i)
            a_ref[m, 0, at, :] = ar
            a_ref[m, 1, at, :] = ai
            put_v(v_ref, length, m, i, *mul(ar, ai, xr, xi))
    transform(mats, 0, v_ref, u_ref, s_ref)
    for i in range(0, length, STEP):
        misfit = -meas_ref[pl.ds(i, STEP), :].astype(jnp.float32)
        for m in range(modes):
            fr, fi = get_s(s_ref, length, m, i)
            misfit += fr * fr + fi * fi
        for m in range(modes):
            fr, fi = get_s(s_ref, length, m, i)
            put_v(v_ref, length, m, i, misfit * fr, misfit * fi)
    transform(mats, 1, v_ref, u_ref, s_ref)
    for i in range(0, length, STEP):
        at = pl.ds(i, STEP)
        gr = gi = 0.0
        for m in range(modes):
            cr, ci = get_s(s_ref, length, m, i)
            dr, di = cmul(a_ref[m, 0, at, :], a_ref[m, 1, at, :], cr, ci)
            gr, gi = gr + dr, gi + di
            put_v(v_ref, length, m, i, *cmul(x_ref[1, 0, at, :], x_ref[1, 1, at, :], cr, ci))
        grad_ref[1, 0, at, :] = gr.astype(grad_ref.dtype)
        grad_ref[1, 1, at, :] = gi.astype(grad_ref.dtype)
    propagate(cmul, mats, fresnel_ref, v_ref, v_ref, u_ref, s_ref)
    for i in range(0, length, STEP):
        at = pl.ds(i, STEP)
        gr = gi = 0.0
        for m in range(modes):
            cr, ci = get_s(s_ref, length, m, i)
            dr, di = cmul(p_ref[m, 0, at, :], p_ref[m, 1, at, :], cr, ci)
            gr, gi = gr + dr, gi + di
            a_ref[m, 0, at, :], a_ref[m, 1, at, :] = cmul(x_ref[0, 0, at, :], x_ref[0, 1, at, :], cr, ci)
        grad_ref[0, 0, at, :] = gr.astype(grad_ref.dtype)
        grad_ref[0, 1, at, :] = gi.astype(grad_ref.dtype)
    row_back = lax.rem(length - row, length)
    col_back = lax.rem(2 * length - off, length)
    per_row, per_col = length // n_obj, length // n_scan
    lane = lax.broadcasted_iota(jnp.int32, (length, 128), 1)
    for m in range(modes):
        for q in range(2):
            a_ref[m, q] = pltpu.roll(pltpu.roll(a_ref[m, q], row_back, 0), col_back, 1)
        for s in range(n_scan):
            first, shift = s * per_col // 128 * 128, s * per_col % 128
            real = a_ref[m, 0, :, first : first + 128]
            imag = a_ref[m, 1, :, first : first + 128]
            real = pltpu.roll(real, (128 - shift) % 128, 1) if shift else real
            imag = pltpu.roll(imag, (per_col - shift) % 128, 1) if shift != per_col else imag
            both = jnp.where(lane < per_col, real, imag)[:, : 2 * per_col]
            apart = lax.rem(s // CORES - chip + chips, chips)
            for mine, ref in ((core, keep_ref), (1 - core, give_ref)):
                @pl.when(mine == s % CORES)
                def _():
                    for o in range(n_obj):
                        ref[o, apart, m] = both[o * per_row : (o + 1) * per_row].astype(ref.dtype)


def place_kernel(sizes, kinds, parts, factor, *refs):
    n_scan, _, tile_cols = sizes
    chips = n_scan // CORES
    layers = refs[-4].shape[0]
    info = refs[0]
    shares = refs[1 : 1 + chips]
    patches = refs[1 + chips : -4]
    out_ref, probe_out, held, sems = refs[-4:]
    _, _, rows, width = out_ref.shape
    length = patches[0].shape[-1]
    me = lax.axis_index("scan")
    blocks = width // length
    first_block = me * blocks
    spots = []
    for index, (tile, flip, jump) in enumerate(kinds):
        source = lax.rem((me ^ flip) - CORES * jump + n_scan, n_scan)
        _, _, row, col = assigned(info, tile, source, n_scan)
        base, off = column_block(col, length, tile_cols)
        top, bottom = (row, rows) if tile == OWN else (0, row)
        meets = (base + 1 >= first_block) & (base < first_block + blocks)
        copies = [
            pltpu.make_async_copy(
                patches[number] if part is None else patches[number].at[part], held.at[index, l], sems.at[index, l]
            )
            for l, (number, part) in enumerate(parts[index])
        ]
        spots.append((base, off, top, bottom, meets, copies))

        @pl.when(meets)
        def _():
            for copy in copies:
                copy.start()

    out_ref[...] = jnp.zeros(out_ref.shape, jnp.float32)
    per_col = probe_out.shape[3]
    for m in range(probe_out.shape[0]):
        total = sum(share[m].astype(jnp.float32) for share in shares) * factor
        probe_out[m, 0] = total[:, :per_col]
        probe_out[m, 1] = total[:, per_col:]
    lane, line = lanes(length), lines(length)
    for index, (base, off, top, bottom, meets, copies) in enumerate(spots):
        @pl.when(meets)
        def _():
            for copy in copies:
                copy.wait()
        for block in range(blocks):
            first, second = base == first_block + block, base + 1 == first_block + block
            left = jnp.where(first, off, 0)
            right = jnp.where(first, length, off)

            @pl.when(first | second)
            def _():
                cols = (lane >= left) & (lane < right)
                spot = slice(block * length, (block + 1) * length)
                for i in range(0, rows, STEP):
                    mask = cols & (line >= top - i) & (line < bottom - i)
                    at = pl.ds(i, STEP)
                    for l in range(layers):
                        for q in range(2):
                            value = held[index, l, q, at, :].astype(jnp.float32)
                            out_ref[l, q, at, spot] += jnp.where(mask, value, 0.0)


def body(object_slices, probe, measured, positions, counts):
    layers, _, tile_rows, tile_cols = object_slices.shape
    modes, _, length, _ = probe.shape
    slots = measured.shape[2]
    n_scan, n_obj = lax.axis_size("scan"), lax.axis_size("obj")
    chips = n_scan // CORES
    sizes = (n_scan, n_obj, tile_cols)
    smem = pl.BlockSpec(memory_space=pltpu.SMEM)
    vmem = pl.BlockSpec(memory_space=pltpu.VMEM)
    hbm = pl.BlockSpec(memory_space=pltpu.HBM)
    real, half = jnp.float32, jnp.bfloat16

    def call(kernel, outs, ins, scratch, name, flops, limit, *args):
        return pl.pallas_call(
            functools.partial(kernel[0], sizes, *kernel[1:]),
            out_shape=[jax.ShapeDtypeStruct(*o) for o in outs],
            in_specs=ins,
            out_specs=[vmem] * len(outs),
            scratch_shapes=scratch,
            compiler_params=pltpu.CompilerParams(vmem_limit_bytes=limit * MIB),
            cost_estimate=pl.CostEstimate(flops=flops, bytes_accessed=4 * MIB, transcendentals=0),
            name=name,
        )(*args)

    def across(block):
        return send(block, lambda s, o: (s ^ 1, o))

    def along(block, jump):
        return send(block, lambda s, o: (s + CORES * jump, o)) if jump else block

    def outward(block, sign):
        return send(block, lambda s, o: (s, o + sign))

    info = jnp.concatenate([counts[0], positions[0, 0].reshape(-1), jnp.zeros((3,), jnp.int32)])
    both = jnp.concatenate([info, send(info, lambda s, o: (s, o + 1))])
    info = lax.all_to_all(jnp.broadcast_to(both, (n_scan, 1, 16)), "scan", 0, 0, tiled=True)

    measured, info = lax.optimization_barrier((measured, info))
    second = measured[0, 0, 1]
    others = [send(second, lambda s, o, k=k: (s + k, o)) for k in range(1, n_scan)]

    patch_shape = (layers, 2, length, length)
    field_shape = (modes, 2, length, length)
    wide = [pltpu.VMEM((layers, 2, tile_rows, 2 * length), real), pltpu.SemaphoreType.DMA((layers, 2, 2))]
    (piece,) = call(
        (pick_kernel, False), [(patch_shape, half)], [smem, hbm], wide, "cut", MIB, LARGE, info, object_slices
    )
    piece = outward(piece, -1)
    (own_part,) = call(
        (pick_kernel, True), [(patch_shape, real)], [smem, hbm], wide, "own", MIB, LARGE, info, object_slices
    )
    mats, turned = call(
        (prep_kernel,),
        [((4, 2 * length, 2 * length), half), (field_shape, real)],
        [smem, vmem, vmem],
        [],
        "prep",
        MIB,
        SMALL,
        info,
        probe,
        dft_tables(length),
    )
    chunk_shape = (n_obj, chips, modes, length // n_obj, 2 * (length // n_scan))
    grad, keep, give = call(
        (pattern_kernel,),
        [(patch_shape, half), (chunk_shape, half), (chunk_shape, half)],
        [smem] + [vmem] * (5 + n_scan),
        [
            pltpu.VMEM((2 * length, modes * length), half),
            pltpu.VMEM((modes * length, 2 * length), half),
            pltpu.VMEM((modes * length, 2 * length), real),
            pltpu.VMEM(patch_shape, real),
            pltpu.VMEM(field_shape, real),
            pltpu.VMEM((length, length), measured.dtype),
        ],
        "pattern",
        3 * 2 * 2 * modes * 8 * length**3,
        SMALL,
        info,
        mats,
        fresnel_tables(length),
        turned,
        own_part,
        piece,
        measured[0, 0],
        *others,
    )

    here = [grad] + [along(grad, j) for j in range(1, chips)]
    chunks = (keep.astype(real) + across(give).astype(real)).astype(half)
    first, chunks = lax.optimization_barrier((grad, chunks))
    there = outward(first, 1)
    x_first = [outward(block[1], 1) for block in here[1:]]
    obj_first = [along(there[0], j) for j in range(1, chips)]
    held = here + [there] + x_first + obj_first
    held += [across(block) for block in held]
    kinds, parts = [], []
    for flip in range(2):
        start = flip * (len(held) // 2)
        for j in range(chips):
            kinds.append((OWN, flip, j))
            parts.append([(start + j, l) for l in range(layers)])
        for j in range(chips):
            kinds.append((PREVIOUS, flip, j))
            if j == 0:
                parts.append([(start + chips, l) for l in range(layers)])
            else:
                parts.append([(start + 2 * chips - 1 + j, None), (start + chips + j, None)])
    chunks = lax.all_to_all(chunks, "obj", 0, 0, tiled=True)
    chunks = jnp.sum(chunks.astype(real), axis=0).astype(half)
    shares = [along(chunks[j], j) for j in range(chips)]
    factor = 1.0 / math.sqrt(n_scan * n_obj * slots // 2)
    object_grad, probe_grad = call(
        (place_kernel, kinds, parts, factor),
        [
            ((layers, 2, tile_rows, tile_cols // n_scan), real),
            ((modes, 2, length // n_obj, length // n_scan), real),
        ],
        [smem] + [vmem] * chips + [hbm] * len(held),
        [
            pltpu.VMEM((2 * n_scan, layers, *patch_shape[1:]), half),
            pltpu.SemaphoreType.DMA((2 * n_scan, layers)),
        ],
        "place",
        MIB,
        LARGE,
        info,
        *shares,
        *held,
    )
    return (object_grad, probe_grad)


def solution(mesh):
    return jax.shard_map(
        body,
        mesh=mesh,
        in_specs=(
            P(None, None, "obj", None),
            P(),
            P("scan", "obj", None, None, None),
            P("scan", "obj", None, None),
            P("scan", "obj"),
        ),
        out_specs=(P(None, None, "obj", "scan"), P(None, None, "obj", "scan")),
        check_vma=False,
    )
```

```python
import functools
import math

import jax
import jax.numpy as jnp
import ml_dtypes
import numpy as np
from jax import lax
from jax.experimental import pallas as pl
from jax.experimental.pallas import tpu as pltpu
from jax.sharding import PartitionSpec as P

AXES = ("scan", "obj")
CORES = 2
MIB = 1 << 20
SMALL, MIDDLE, LARGE = 20, 48, 56


def dft_tables(length):
    index = np.arange(length)
    angles = (index[:, None] * index[None, :] % length) * (2.0 * math.pi / length)
    parts = np.stack([np.cos(angles), -np.sin(angles)]) / math.sqrt(length)
    return parts.astype(np.float32).astype(ml_dtypes.bfloat16).astype(np.float32)


def fresnel_tables(length):
    index = np.arange(length)
    freqs = np.where(index < length // 2, index, index - length)
    squares = freqs * freqs
    phases = ((squares[:, None] + squares[None, :]) % (4 * length)) * (2.0 * math.pi / (4 * length))
    return np.stack([np.cos(phases), -np.sin(phases)]).astype(np.float32)


def send(block, move):
    n_scan, n_obj = lax.axis_size("scan"), lax.axis_size("obj")
    route = []
    for s in range(n_scan):
        for o in range(n_obj):
            goal = move(s, o)
            if goal is not None:
                route.append((s * n_obj + o, goal[0] % n_scan * n_obj + goal[1] % n_obj))
    return lax.ppermute(block, AXES, route)


OWN, PREVIOUS = 0, 1


def assigned(info, tile, target, n_scan):
    def entry(a, j):
        return info[a, 0, 8 * tile + j]

    idle = entry(target, 0) == 0
    counts = [entry(a, 0) for a in range(n_scan)]
    rank = jnp.int32(0)
    for a in range(n_scan):
        rank += jnp.where((counts[a] == 0) & (a < target), 1, 0)
    source = jnp.int32(target)
    seen = jnp.int32(0)
    for a in range(n_scan):
        full = counts[a] == 2
        source = jnp.where(idle & full & (seen == rank), a, source)
        seen += jnp.where(full, 1, 0)
    slot = jnp.where(idle, 1, 0)
    return source, slot, entry(source, 1 + 2 * slot), entry(source, 2 + 2 * slot)


def column_block(col, length, tile_cols):
    base = jnp.minimum(lax.div(col, length), tile_cols // length - 2)
    return base, col - base * length


STEP = 32


def lanes(length):
    return lax.broadcasted_iota(jnp.int32, (STEP, length), 1)


def lines(length):
    return lax.broadcasted_iota(jnp.int32, (STEP, length), 0)


def mul(ar, ai, br, bi):
    return ar * br - ai * bi, ar * bi + ai * br


def cmul(ar, ai, br, bi):
    return ar * br + ai * bi, ar * bi - ai * br


def fetch_columns(object_ref, wide, sems, base, length):
    layers, _, rows, _ = wide.shape
    start = pl.multiple_of(base * length, length)
    copies = []
    for l in range(layers):
        for q in range(2):
            for h in range(2):
                at = pl.ds(h * (rows // 2), rows // 2)
                copy = pltpu.make_async_copy(
                    object_ref.at[l, q, at, pl.ds(start, 2 * length)], wide.at[l, q, at], sems.at[l, q, h]
                )
                copy.start()
                copies.append(copy)
    return copies


def pick_columns(wide, l, q, at, off, length):
    return jnp.where(lanes(length) >= off, wide[l, q, at, :length], wide[l, q, at, length:])


def pick_kernel(sizes, own, info, object_ref, out_ref, wide, sems):
    n_scan, _, tile_cols = sizes
    layers, _, rows, length = out_ref.shape
    _, _, _, col = assigned(info, OWN if own else PREVIOUS, lax.axis_index("scan"), n_scan)
    base, off = column_block(col, length, tile_cols)
    copies = fetch_columns(object_ref, wide, sems, base, length)
    for l in range(layers):
        for q in range(2):
            for i in range(0, rows, STEP):
                if i % (rows // 2) == 0:
                    copies.pop(0).wait()
                at = pl.ds(i, STEP)
                out_ref[l, q, at, :] = pick_columns(wide, l, q, at, off, length).astype(out_ref.dtype)


def prep_kernel(sizes, info, probe_ref, dft_ref, mats, p_ref):
    n_scan, _, tile_cols = sizes
    modes, _, length, _ = probe_ref.shape
    _, _, row, col = assigned(info, OWN, lax.axis_index("scan"), n_scan)
    _, off = column_block(col, length, tile_cols)
    turn = lax.rem(off, length)

    def put(k, real, imag):
        mats[k, :length, :length] = real.astype(jnp.bfloat16)
        mats[k, length:, length:] = real.astype(jnp.bfloat16)
        mats[k, :length, length:] = imag.astype(jnp.bfloat16)
        mats[k, length:, :length] = (-imag).astype(jnp.bfloat16)

    real, imag = dft_ref[0], dft_ref[1]
    put(0, pltpu.roll(real, row, 1), -pltpu.roll(imag, row, 1))
    put(1, pltpu.roll(real, turn, 0), pltpu.roll(imag, turn, 0))
    put(2, pltpu.roll(real, row, 0), pltpu.roll(imag, row, 0))
    put(3, pltpu.roll(real, turn, 1), -pltpu.roll(imag, turn, 1))
    for m in range(modes):
        for q in range(2):
            p_ref[m, q] = pltpu.roll(pltpu.roll(probe_ref[m, q], row, 0), turn, 1)


def put_v(v_ref, length, m, i, real, imag):
    spot = slice(m * length, (m + 1) * length)
    v_ref[pl.ds(i, STEP), spot] = real.astype(jnp.bfloat16)
    v_ref[pl.ds(length + i, STEP), spot] = imag.astype(jnp.bfloat16)


def get_s(s_ref, length, m, i):
    at = pl.ds(m * length + i, STEP)
    return s_ref[at, :length], s_ref[at, length:]


def transform(mats, inverse, v_ref, u_ref, s_ref):
    length = mats.shape[1] // 2
    mid = jnp.dot(mats[2 * inverse], v_ref[...], preferred_element_type=jnp.float32).astype(jnp.bfloat16)
    for m in range(v_ref.shape[1] // length):
        for q in range(2):
            u_ref[m * length : (m + 1) * length, q * length : (q + 1) * length] = mid[
                q * length : (q + 1) * length, m * length : (m + 1) * length
            ]
    s_ref[...] = jnp.dot(u_ref[...], mats[2 * inverse + 1], preferred_element_type=jnp.float32)


def propagate(product, mats, fresnel_ref, v_in, v_ref, u_ref, s_ref):
    length = mats.shape[1] // 2
    transform(mats, 0, v_in, u_ref, s_ref)
    for i in range(0, length, STEP):
        at = pl.ds(i, STEP)
        kr, ki = fresnel_ref[0, at, :], fresnel_ref[1, at, :]
        for m in range(v_ref.shape[1] // length):
            put_v(v_ref, length, m, i, *product(kr, ki, *get_s(s_ref, length, m, i)))
    transform(mats, 1, v_ref, u_ref, s_ref)


def join(own, piece, i, row):
    return jnp.where(lines(own.shape[1]) >= row - i, own, piece.astype(jnp.float32))


def pattern_kernel(sizes, *refs):
    n_scan, n_obj, tile_cols = sizes
    info, mats, fresnel_ref, p_ref, xo_ref, piece, own_ref = refs[:7]
    others = refs[7 : 6 + n_scan]
    grad_ref, keep_ref, give_ref, v_ref, u_ref, s_ref, x_ref, a_ref, meas_ref = refs[6 + n_scan :]
    modes, _, length, _ = p_ref.shape
    me = lax.axis_index("scan")
    core, chip, chips = lax.rem(me, CORES), lax.div(me, CORES), n_scan // CORES
    source, slot, row, col = assigned(info, OWN, me, n_scan)
    _, off = column_block(col, length, tile_cols)

    @pl.when(slot == 0)
    def _():
        meas_ref[...] = own_ref[0]

    for k in range(1, n_scan):
        @pl.when((slot == 1) & (source == lax.rem(me - k + n_scan, n_scan)))
        def _():
            meas_ref[...] = others[k - 1][...]

    for l in range(x_ref.shape[0]):
        for q in range(2):
            for i in range(0, length, STEP):
                at = pl.ds(i, STEP)
                x_ref[l, q, at, :] = join(xo_ref[l, q, at, :], piece[l, q, at, :], i, row)
    for i in range(0, length, STEP):
        at = pl.ds(i, STEP)
        xr, xi = x_ref[0, 0, at, :], x_ref[0, 1, at, :]
        for m in range(modes):
            put_v(v_ref, length, m, i, *mul(p_ref[m, 0, at, :], p_ref[m, 1, at, :], xr, xi))
    propagate(mul, mats, fresnel_ref, v_ref, v_ref, u_ref, s_ref)
    for i in range(0, length, STEP):
        at = pl.ds(i, STEP)
        xr, xi = x_ref[1, 0, at, :], x_ref[1, 1, at, :]
        for m in range(modes):
            ar, ai = get_s(s_ref, length, m, i)
            a_ref[m, 0, at, :] = ar
            a_ref[m, 1, at, :] = ai
            put_v(v_ref, length, m, i, *mul(ar, ai, xr, xi))
    transform(mats, 0, v_ref, u_ref, s_ref)
    for i in range(0, length, STEP):
        misfit = -meas_ref[pl.ds(i, STEP), :].astype(jnp.float32)
        for m in range(modes):
            fr, fi = get_s(s_ref, length, m, i)
            misfit += fr * fr + fi * fi
        for m in range(modes):
            fr, fi = get_s(s_ref, length, m, i)
            put_v(v_ref, length, m, i, misfit * fr, misfit * fi)
    transform(mats, 1, v_ref, u_ref, s_ref)
    for i in range(0, length, STEP):
        at = pl.ds(i, STEP)
        gr = gi = 0.0
        for m in range(modes):
            cr, ci = get_s(s_ref, length, m, i)
            dr, di = cmul(a_ref[m, 0, at, :], a_ref[m, 1, at, :], cr, ci)
            gr, gi = gr + dr, gi + di
            put_v(v_ref, length, m, i, *cmul(x_ref[1, 0, at, :], x_ref[1, 1, at, :], cr, ci))
        grad_ref[1, 0, at, :] = gr.astype(grad_ref.dtype)
        grad_ref[1, 1, at, :] = gi.astype(grad_ref.dtype)
    propagate(cmul, mats, fresnel_ref, v_ref, v_ref, u_ref, s_ref)
    for i in range(0, length, STEP):
        at = pl.ds(i, STEP)
        gr = gi = 0.0
        for m in range(modes):
            cr, ci = get_s(s_ref, length, m, i)
            dr, di = cmul(p_ref[m, 0, at, :], p_ref[m, 1, at, :], cr, ci)
            gr, gi = gr + dr, gi + di
            a_ref[m, 0, at, :], a_ref[m, 1, at, :] = cmul(x_ref[0, 0, at, :], x_ref[0, 1, at, :], cr, ci)
        grad_ref[0, 0, at, :] = gr.astype(grad_ref.dtype)
        grad_ref[0, 1, at, :] = gi.astype(grad_ref.dtype)
    row_back = lax.rem(length - row, length)
    col_back = lax.rem(2 * length - off, length)
    per_row, per_col = length // n_obj, length // n_scan
    lane = lax.broadcasted_iota(jnp.int32, (length, 128), 1)
    for m in range(modes):
        for q in range(2):
            a_ref[m, q] = pltpu.roll(pltpu.roll(a_ref[m, q], row_back, 0), col_back, 1)
        for s in range(n_scan):
            first, shift = s * per_col // 128 * 128, s * per_col % 128
            real = a_ref[m, 0, :, first : first + 128]
            imag = a_ref[m, 1, :, first : first + 128]
            real = pltpu.roll(real, (128 - shift) % 128, 1) if shift else real
            imag = pltpu.roll(imag, (per_col - shift) % 128, 1) if shift != per_col else imag
            both = jnp.where(lane < per_col, real, imag)[:, : 2 * per_col]
            apart = lax.rem(s // CORES - chip + chips, chips)
            for mine, ref in ((core, keep_ref), (1 - core, give_ref)):
                @pl.when(mine == s % CORES)
                def _():
                    for o in range(n_obj):
                        ref[apart, o, m] = both[o * per_row : (o + 1) * per_row].astype(ref.dtype)


def place_kernel(sizes, kinds, parts, factor, *refs):
    n_scan, n_obj, tile_cols = sizes
    layers = refs[-4].shape[0]
    info = refs[0]
    chunks = refs[1]
    patches = refs[2:-4]
    out_ref, probe_out, held, sems = refs[-4:]
    _, _, rows, width = out_ref.shape
    length = patches[0].shape[-1]
    me = lax.axis_index("scan")
    blocks = width // length
    first_block = me * blocks
    spots = []
    for index, (tile, flip, jump) in enumerate(kinds):
        source = lax.rem((me ^ flip) - CORES * jump + n_scan, n_scan)
        _, _, row, col = assigned(info, tile, source, n_scan)
        base, off = column_block(col, length, tile_cols)
        top, bottom = (row, rows) if tile == OWN else (0, row)
        meets = (base + 1 >= first_block) & (base < first_block + blocks)
        copies = [
            pltpu.make_async_copy(
                patches[number] if part is None else patches[number].at[part], held.at[index, l], sems.at[index, l]
            )
            for l, (number, part) in enumerate(parts[index])
        ]
        spots.append((base, off, top, bottom, meets, copies))

        @pl.when(meets)
        def _():
            for copy in copies:
                copy.start()

    out_ref[...] = jnp.zeros(out_ref.shape, jnp.float32)
    per_col = probe_out.shape[3]
    for m in range(probe_out.shape[0]):
        total = sum(chunks[o, m].astype(jnp.float32) for o in range(n_obj)) * factor
        probe_out[m, 0] = total[:, :per_col]
        probe_out[m, 1] = total[:, per_col:]
    lane, line = lanes(length), lines(length)
    for index, (base, off, top, bottom, meets, copies) in enumerate(spots):
        @pl.when(meets)
        def _():
            for copy in copies:
                copy.wait()
        for block in range(blocks):
            first, second = base == first_block + block, base + 1 == first_block + block
            left = jnp.where(first, off, 0)
            right = jnp.where(first, length, off)

            @pl.when(first | second)
            def _():
                cols = (lane >= left) & (lane < right)
                spot = slice(block * length, (block + 1) * length)
                for i in range(0, rows, STEP):
                    mask = cols & (line >= top - i) & (line < bottom - i)
                    at = pl.ds(i, STEP)
                    for l in range(layers):
                        for q in range(2):
                            value = held[index, l, q, at, :].astype(jnp.float32)
                            out_ref[l, q, at, spot] += jnp.where(mask, value, 0.0)


def body(object_slices, probe, measured, positions, counts):
    layers, _, tile_rows, tile_cols = object_slices.shape
    modes, _, length, _ = probe.shape
    slots = measured.shape[2]
    n_scan, n_obj = lax.axis_size("scan"), lax.axis_size("obj")
    chips = n_scan // CORES
    sizes = (n_scan, n_obj, tile_cols)
    smem = pl.BlockSpec(memory_space=pltpu.SMEM)
    vmem = pl.BlockSpec(memory_space=pltpu.VMEM)
    hbm = pl.BlockSpec(memory_space=pltpu.HBM)
    real, half = jnp.float32, jnp.bfloat16

    def call(kernel, outs, ins, scratch, name, flops, limit, *args):
        return pl.pallas_call(
            functools.partial(kernel[0], sizes, *kernel[1:]),
            out_shape=[jax.ShapeDtypeStruct(*o) for o in outs],
            in_specs=ins,
            out_specs=[vmem] * len(outs),
            scratch_shapes=scratch,
            compiler_params=pltpu.CompilerParams(vmem_limit_bytes=limit * MIB),
            cost_estimate=pl.CostEstimate(flops=flops, bytes_accessed=4 * MIB, transcendentals=0),
            name=name,
        )(*args)

    def across(block):
        return send(block, lambda s, o: (s ^ 1, o))

    def along(block, jump):
        return send(block, lambda s, o: (s + CORES * jump, o)) if jump else block

    def outward(block, sign):
        return send(block, lambda s, o: (s, o + sign))

    info = jnp.concatenate([counts[0], positions[0, 0].reshape(-1), jnp.zeros((3,), jnp.int32)])
    both = jnp.concatenate([info, send(info, lambda s, o: (s, o + 1))])
    info = lax.all_to_all(jnp.broadcast_to(both, (n_scan, 1, 16)), "scan", 0, 0, tiled=True)

    measured, info = lax.optimization_barrier((measured, info))
    second = measured[0, 0, 1]
    others = [send(second, lambda s, o, k=k: (s + k, o)) for k in range(1, n_scan)]

    patch_shape = (layers, 2, length, length)
    field_shape = (modes, 2, length, length)
    wide = [pltpu.VMEM((layers, 2, tile_rows, 2 * length), real), pltpu.SemaphoreType.DMA((layers, 2, 2))]
    (piece,) = call(
        (pick_kernel, False), [(patch_shape, half)], [smem, hbm], wide, "cut", MIB, LARGE, info, object_slices
    )
    piece = outward(piece, -1)
    (own_part,) = call(
        (pick_kernel, True), [(patch_shape, real)], [smem, hbm], wide, "own", MIB, MIDDLE, info, object_slices
    )
    mats, turned = call(
        (prep_kernel,),
        [((4, 2 * length, 2 * length), half), (field_shape, real)],
        [smem, vmem, vmem],
        [],
        "prep",
        MIB,
        SMALL,
        info,
        probe,
        dft_tables(length),
    )
    chunk_shape = (chips, n_obj, modes, length // n_obj, 2 * (length // n_scan))
    grad, keep, give = call(
        (pattern_kernel,),
        [(patch_shape, half), (chunk_shape, half), (chunk_shape, half)],
        [smem] + [vmem] * (5 + n_scan),
        [
            pltpu.VMEM((2 * length, modes * length), half),
            pltpu.VMEM((modes * length, 2 * length), half),
            pltpu.VMEM((modes * length, 2 * length), real),
            pltpu.VMEM(patch_shape, real),
            pltpu.VMEM(field_shape, real),
            pltpu.VMEM((length, length), measured.dtype),
        ],
        "pattern",
        3 * 2 * 2 * modes * 8 * length**3,
        SMALL,
        info,
        mats,
        fresnel_tables(length),
        turned,
        own_part,
        piece,
        measured[0, 0],
        *others,
    )

    here = [grad] + [along(grad, j) for j in range(1, chips)]
    chunks = (keep.astype(real) + across(give).astype(real)).astype(half)
    chunks = sum((along(chunks[j], j).astype(real) for j in range(1, chips)), chunks[0].astype(real)).astype(half)
    there = outward(grad, 1)
    late, chunks = lax.optimization_barrier((here[1:], chunks))
    here = here[:1] + late
    x_first = [outward(block[1], 1) for block in late]
    obj_first = [along(there[0], j) for j in range(1, chips)]
    held = here + [there] + x_first + obj_first
    held += [across(block) for block in held]
    kinds, parts = [], []
    for flip in range(2):
        start = flip * (len(held) // 2)
        for j in range(chips):
            kinds.append((OWN, flip, j))
            parts.append([(start + j, l) for l in range(layers)])
        for j in range(chips):
            kinds.append((PREVIOUS, flip, j))
            if j == 0:
                parts.append([(start + chips, l) for l in range(layers)])
            else:
                parts.append([(start + 2 * chips - 1 + j, None), (start + chips + j, None)])
    chunks = lax.all_to_all(chunks, "obj", 0, 0, tiled=True)
    factor = 1.0 / math.sqrt(n_scan * n_obj * slots // 2)
    object_grad, probe_grad = call(
        (place_kernel, kinds, parts, factor),
        [
            ((layers, 2, tile_rows, tile_cols // n_scan), real),
            ((modes, 2, length // n_obj, length // n_scan), real),
        ],
        [smem, vmem] + [hbm] * len(held),
        [
            pltpu.VMEM((2 * n_scan, layers, *patch_shape[1:]), half),
            pltpu.SemaphoreType.DMA((2 * n_scan, layers)),
        ],
        "place",
        MIB,
        LARGE,
        info,
        chunks,
        *held,
    )
    return (object_grad, probe_grad)


def solution(mesh):
    return jax.shard_map(
        body,
        mesh=mesh,
        in_specs=(
            P(None, None, "obj", None),
            P(),
            P("scan", "obj", None, None, None),
            P("scan", "obj", None, None),
            P("scan", "obj"),
        ),
        out_specs=(P(None, None, "obj", "scan"), P(None, None, "obj", "scan")),
        check_vma=False,
    )
```

```python
import functools
import math

import jax
import jax.numpy as jnp
import ml_dtypes
import numpy as np
from jax import lax
from jax.experimental import pallas as pl
from jax.experimental.pallas import tpu as pltpu
from jax.sharding import PartitionSpec as P

AXES = ("scan", "obj")
CORES = 2
MIB = 1 << 20
SMALL, MIDDLE, LARGE = 20, 48, 56


def dft_tables(length):
    index = np.arange(length)
    angles = (index[:, None] * index[None, :] % length) * (2.0 * math.pi / length)
    parts = np.stack([np.cos(angles), -np.sin(angles)]) / math.sqrt(length)
    return parts.astype(np.float32).astype(ml_dtypes.bfloat16).astype(np.float32)


def fresnel_tables(length):
    index = np.arange(length)
    freqs = np.where(index < length // 2, index, index - length)
    squares = freqs * freqs
    phases = ((squares[:, None] + squares[None, :]) % (4 * length)) * (2.0 * math.pi / (4 * length))
    return np.stack([np.cos(phases), -np.sin(phases)]).astype(np.float32)


def send(block, move):
    n_scan, n_obj = lax.axis_size("scan"), lax.axis_size("obj")
    route = []
    for s in range(n_scan):
        for o in range(n_obj):
            goal = move(s, o)
            if goal is not None:
                route.append((s * n_obj + o, goal[0] % n_scan * n_obj + goal[1] % n_obj))
    return lax.ppermute(block, AXES, route)


OWN, PREVIOUS = 0, 1


def assigned(info, tile, target, n_scan):
    def entry(a, j):
        return info[a, 0, 8 * tile + j]

    idle = entry(target, 0) == 0
    counts = [entry(a, 0) for a in range(n_scan)]
    rank = jnp.int32(0)
    for a in range(n_scan):
        rank += jnp.where((counts[a] == 0) & (a < target), 1, 0)
    source = jnp.int32(target)
    seen = jnp.int32(0)
    for a in range(n_scan):
        full = counts[a] == 2
        source = jnp.where(idle & full & (seen == rank), a, source)
        seen += jnp.where(full, 1, 0)
    slot = jnp.where(idle, 1, 0)
    return source, slot, entry(source, 1 + 2 * slot), entry(source, 2 + 2 * slot)


def column_block(col, length, tile_cols):
    base = jnp.minimum(lax.div(col, length), tile_cols // length - 2)
    return base, col - base * length


STEP = 32


def lanes(length):
    return lax.broadcasted_iota(jnp.int32, (STEP, length), 1)


def lines(length):
    return lax.broadcasted_iota(jnp.int32, (STEP, length), 0)


def mul(ar, ai, br, bi):
    return ar * br - ai * bi, ar * bi + ai * br


def cmul(ar, ai, br, bi):
    return ar * br + ai * bi, ar * bi - ai * br


def fetch_columns(object_ref, wide, sems, base, length):
    layers, _, rows, _ = wide.shape
    start = pl.multiple_of(base * length, length)
    copies = []
    for l in range(layers):
        for q in range(2):
            for h in range(2):
                at = pl.ds(h * (rows // 2), rows // 2)
                copy = pltpu.make_async_copy(
                    object_ref.at[l, q, at, pl.ds(start, 2 * length)], wide.at[l, q, at], sems.at[l, q, h]
                )
                copy.start()
                copies.append(copy)
    return copies


def pick_columns(wide, l, q, at, off, length):
    return jnp.where(lanes(length) >= off, wide[l, q, at, :length], wide[l, q, at, length:])


def pick_kernel(sizes, own, info, object_ref, out_ref, wide, sems):
    n_scan, _, tile_cols = sizes
    layers, _, rows, length = out_ref.shape
    _, _, _, col = assigned(info, OWN if own else PREVIOUS, lax.axis_index("scan"), n_scan)
    base, off = column_block(col, length, tile_cols)
    copies = fetch_columns(object_ref, wide, sems, base, length)
    for l in range(layers):
        for q in range(2):
            for i in range(0, rows, STEP):
                if i % (rows // 2) == 0:
                    copies.pop(0).wait()
                at = pl.ds(i, STEP)
                out_ref[l, q, at, :] = pick_columns(wide, l, q, at, off, length).astype(out_ref.dtype)


def prep_kernel(sizes, info, probe_ref, dft_ref, mats, p_ref):
    n_scan, _, tile_cols = sizes
    modes, _, length, _ = probe_ref.shape
    _, _, row, col = assigned(info, OWN, lax.axis_index("scan"), n_scan)
    _, off = column_block(col, length, tile_cols)
    turn = lax.rem(off, length)

    def put(k, real, imag):
        mats[k, :length, :length] = real.astype(jnp.bfloat16)
        mats[k, length:, length:] = real.astype(jnp.bfloat16)
        mats[k, :length, length:] = imag.astype(jnp.bfloat16)
        mats[k, length:, :length] = (-imag).astype(jnp.bfloat16)

    real, imag = dft_ref[0], dft_ref[1]
    put(0, pltpu.roll(real, row, 1), -pltpu.roll(imag, row, 1))
    put(1, pltpu.roll(real, turn, 0), pltpu.roll(imag, turn, 0))
    put(2, pltpu.roll(real, row, 0), pltpu.roll(imag, row, 0))
    put(3, pltpu.roll(real, turn, 1), -pltpu.roll(imag, turn, 1))
    for m in range(modes):
        for q in range(2):
            p_ref[m, q] = pltpu.roll(pltpu.roll(probe_ref[m, q], row, 0), turn, 1)


def put_v(v_ref, length, m, i, real, imag):
    spot = slice(m * length, (m + 1) * length)
    v_ref[pl.ds(i, STEP), spot] = real.astype(jnp.bfloat16)
    v_ref[pl.ds(length + i, STEP), spot] = imag.astype(jnp.bfloat16)


def get_s(s_ref, length, m, i):
    at = pl.ds(m * length + i, STEP)
    return s_ref[at, :length], s_ref[at, length:]


def transform(mats, inverse, v_ref, u_ref, s_ref):
    length = mats.shape[1] // 2
    mid = jnp.dot(mats[2 * inverse], v_ref[...], preferred_element_type=jnp.float32).astype(jnp.bfloat16)
    for m in range(v_ref.shape[1] // length):
        for q in range(2):
            u_ref[m * length : (m + 1) * length, q * length : (q + 1) * length] = mid[
                q * length : (q + 1) * length, m * length : (m + 1) * length
            ]
    s_ref[...] = jnp.dot(u_ref[...], mats[2 * inverse + 1], preferred_element_type=jnp.float32)


def propagate(product, mats, fresnel_ref, v_in, v_ref, u_ref, s_ref):
    length = mats.shape[1] // 2
    transform(mats, 0, v_in, u_ref, s_ref)
    for i in range(0, length, STEP):
        at = pl.ds(i, STEP)
        kr, ki = fresnel_ref[0, at, :], fresnel_ref[1, at, :]
        for m in range(v_ref.shape[1] // length):
            put_v(v_ref, length, m, i, *product(kr, ki, *get_s(s_ref, length, m, i)))
    transform(mats, 1, v_ref, u_ref, s_ref)


def join(own, piece, i, row):
    return jnp.where(lines(own.shape[1]) >= row - i, own, piece.astype(jnp.float32))


def pattern_kernel(sizes, *refs):
    n_scan, n_obj, tile_cols = sizes
    info, mats, fresnel_ref, p_ref, xo_ref, piece, own_ref = refs[:7]
    others = refs[7 : 6 + n_scan]
    grad_ref, keep_ref, give_ref, v_ref, u_ref, s_ref, x_ref, a_ref, meas_ref = refs[6 + n_scan :]
    modes, _, length, _ = p_ref.shape
    me = lax.axis_index("scan")
    core, chip, chips = lax.rem(me, CORES), lax.div(me, CORES), n_scan // CORES
    source, slot, row, col = assigned(info, OWN, me, n_scan)
    _, off = column_block(col, length, tile_cols)

    @pl.when(slot == 0)
    def _():
        meas_ref[...] = own_ref[0]

    for k in range(1, n_scan):
        @pl.when((slot == 1) & (source == lax.rem(me - k + n_scan, n_scan)))
        def _():
            meas_ref[...] = others[k - 1][...]

    for l in range(x_ref.shape[0]):
        for q in range(2):
            for i in range(0, length, STEP):
                at = pl.ds(i, STEP)
                x_ref[l, q, at, :] = join(xo_ref[l, q, at, :], piece[l, q, at, :], i, row)
    for i in range(0, length, STEP):
        at = pl.ds(i, STEP)
        xr, xi = x_ref[0, 0, at, :], x_ref[0, 1, at, :]
        for m in range(modes):
            put_v(v_ref, length, m, i, *mul(p_ref[m, 0, at, :], p_ref[m, 1, at, :], xr, xi))
    propagate(mul, mats, fresnel_ref, v_ref, v_ref, u_ref, s_ref)
    for i in range(0, length, STEP):
        at = pl.ds(i, STEP)
        xr, xi = x_ref[1, 0, at, :], x_ref[1, 1, at, :]
        for m in range(modes):
            ar, ai = get_s(s_ref, length, m, i)
            a_ref[m, 0, at, :] = ar
            a_ref[m, 1, at, :] = ai
            put_v(v_ref, length, m, i, *mul(ar, ai, xr, xi))
    transform(mats, 0, v_ref, u_ref, s_ref)
    for i in range(0, length, STEP):
        misfit = -meas_ref[pl.ds(i, STEP), :].astype(jnp.float32)
        for m in range(modes):
            fr, fi = get_s(s_ref, length, m, i)
            misfit += fr * fr + fi * fi
        for m in range(modes):
            fr, fi = get_s(s_ref, length, m, i)
            put_v(v_ref, length, m, i, misfit * fr, misfit * fi)
    transform(mats, 1, v_ref, u_ref, s_ref)
    for i in range(0, length, STEP):
        at = pl.ds(i, STEP)
        gr = gi = 0.0
        for m in range(modes):
            cr, ci = get_s(s_ref, length, m, i)
            dr, di = cmul(a_ref[m, 0, at, :], a_ref[m, 1, at, :], cr, ci)
            gr, gi = gr + dr, gi + di
            put_v(v_ref, length, m, i, *cmul(x_ref[1, 0, at, :], x_ref[1, 1, at, :], cr, ci))
        grad_ref[1, 0, at, :] = gr.astype(grad_ref.dtype)
        grad_ref[1, 1, at, :] = gi.astype(grad_ref.dtype)
    propagate(cmul, mats, fresnel_ref, v_ref, v_ref, u_ref, s_ref)
    for i in range(0, length, STEP):
        at = pl.ds(i, STEP)
        gr = gi = 0.0
        for m in range(modes):
            cr, ci = get_s(s_ref, length, m, i)
            dr, di = cmul(p_ref[m, 0, at, :], p_ref[m, 1, at, :], cr, ci)
            gr, gi = gr + dr, gi + di
            a_ref[m, 0, at, :], a_ref[m, 1, at, :] = cmul(x_ref[0, 0, at, :], x_ref[0, 1, at, :], cr, ci)
        grad_ref[0, 0, at, :] = gr.astype(grad_ref.dtype)
        grad_ref[0, 1, at, :] = gi.astype(grad_ref.dtype)
    row_back = lax.rem(length - row, length)
    col_back = lax.rem(2 * length - off, length)
    per_row, per_col = length // n_obj, length // n_scan
    lane = lax.broadcasted_iota(jnp.int32, (length, 128), 1)
    for m in range(modes):
        for q in range(2):
            a_ref[m, q] = pltpu.roll(pltpu.roll(a_ref[m, q], row_back, 0), col_back, 1)
        for s in range(n_scan):
            first, shift = s * per_col // 128 * 128, s * per_col % 128
            real = a_ref[m, 0, :, first : first + 128]
            imag = a_ref[m, 1, :, first : first + 128]
            real = pltpu.roll(real, (128 - shift) % 128, 1) if shift else real
            imag = pltpu.roll(imag, (per_col - shift) % 128, 1) if shift != per_col else imag
            both = jnp.where(lane < per_col, real, imag)[:, : 2 * per_col]
            apart = lax.rem(s // CORES - chip + chips, chips)
            for mine, ref in ((core, keep_ref), (1 - core, give_ref)):
                @pl.when(mine == s % CORES)
                def _():
                    for o in range(n_obj):
                        ref[apart, o, m] = both[o * per_row : (o + 1) * per_row].astype(ref.dtype)


def place_kernel(sizes, kinds, factor, *refs):
    n_scan, n_obj, tile_cols = sizes
    layers = refs[-4].shape[0]
    info = refs[0]
    chunks = refs[1]
    patches = refs[2:-4]
    out_ref, probe_out, held, sems = refs[-4:]
    _, _, rows, width = out_ref.shape
    length = patches[0].shape[-1]
    me = lax.axis_index("scan")
    blocks = width // length
    first_block = me * blocks
    spots = []
    for index, (tile, flip, jump) in enumerate(kinds):
        source = lax.rem((me ^ flip) - CORES * jump + n_scan, n_scan)
        _, _, row, col = assigned(info, tile, source, n_scan)
        base, off = column_block(col, length, tile_cols)
        top, bottom = (row, rows) if tile == OWN else (0, row)
        meets = (base + 1 >= first_block) & (base < first_block + blocks)
        copies = [
            pltpu.make_async_copy(patches[index].at[l], held.at[index, l], sems.at[index, l])
            for l in range(layers)
        ]
        spots.append((base, off, top, bottom, meets, copies))

        @pl.when(meets)
        def _():
            for copy in copies:
                copy.start()

    out_ref[...] = jnp.zeros(out_ref.shape, jnp.float32)
    per_col = probe_out.shape[3]
    for m in range(probe_out.shape[0]):
        total = sum(chunks[o, m].astype(jnp.float32) for o in range(n_obj)) * factor
        probe_out[m, 0] = total[:, :per_col]
        probe_out[m, 1] = total[:, per_col:]
    lane, line = lanes(length), lines(length)
    for index, (base, off, top, bottom, meets, copies) in enumerate(spots):
        @pl.when(meets)
        def _():
            for copy in copies:
                copy.wait()
        for block in range(blocks):
            first, second = base == first_block + block, base + 1 == first_block + block
            left = jnp.where(first, off, 0)
            right = jnp.where(first, length, off)

            @pl.when(first | second)
            def _():
                cols = (lane >= left) & (lane < right)
                spot = slice(block * length, (block + 1) * length)
                for i in range(0, rows, STEP):
                    mask = cols & (line >= top - i) & (line < bottom - i)
                    at = pl.ds(i, STEP)
                    for l in range(layers):
                        for q in range(2):
                            value = held[index, l, q, at, :].astype(jnp.float32)
                            out_ref[l, q, at, spot] += jnp.where(mask, value, 0.0)


def body(object_slices, probe, measured, positions, counts):
    layers, _, tile_rows, tile_cols = object_slices.shape
    modes, _, length, _ = probe.shape
    slots = measured.shape[2]
    n_scan, n_obj = lax.axis_size("scan"), lax.axis_size("obj")
    chips = n_scan // CORES
    sizes = (n_scan, n_obj, tile_cols)
    smem = pl.BlockSpec(memory_space=pltpu.SMEM)
    vmem = pl.BlockSpec(memory_space=pltpu.VMEM)
    hbm = pl.BlockSpec(memory_space=pltpu.HBM)
    real, half = jnp.float32, jnp.bfloat16

    def call(kernel, outs, ins, scratch, name, flops, limit, *args):
        return pl.pallas_call(
            functools.partial(kernel[0], sizes, *kernel[1:]),
            out_shape=[jax.ShapeDtypeStruct(*o) for o in outs],
            in_specs=ins,
            out_specs=[vmem] * len(outs),
            scratch_shapes=scratch,
            compiler_params=pltpu.CompilerParams(vmem_limit_bytes=limit * MIB),
            cost_estimate=pl.CostEstimate(flops=flops, bytes_accessed=4 * MIB, transcendentals=0),
            name=name,
        )(*args)

    def across(block):
        return send(block, lambda s, o: (s ^ 1, o))

    def along(block, jump):
        return send(block, lambda s, o: (s + CORES * jump, o)) if jump else block

    def outward(block, sign):
        return send(block, lambda s, o: (s, o + sign))

    info = jnp.concatenate([counts[0], positions[0, 0].reshape(-1), jnp.zeros((3,), jnp.int32)])
    both = jnp.concatenate([info, send(info, lambda s, o: (s, o + 1))])
    info = lax.all_to_all(jnp.broadcast_to(both, (n_scan, 1, 16)), "scan", 0, 0, tiled=True)

    measured, info = lax.optimization_barrier((measured, info))
    second = measured[0, 0, 1]
    others = [send(second, lambda s, o, k=k: (s + k, o)) for k in range(1, n_scan)]

    patch_shape = (layers, 2, length, length)
    field_shape = (modes, 2, length, length)
    wide = [pltpu.VMEM((layers, 2, tile_rows, 2 * length), real), pltpu.SemaphoreType.DMA((layers, 2, 2))]
    (piece,) = call(
        (pick_kernel, False), [(patch_shape, half)], [smem, hbm], wide, "cut", MIB, LARGE, info, object_slices
    )
    piece = outward(piece, -1)
    (own_part,) = call(
        (pick_kernel, True), [(patch_shape, real)], [smem, hbm], wide, "own", MIB, MIDDLE, info, object_slices
    )
    mats, turned = call(
        (prep_kernel,),
        [((4, 2 * length, 2 * length), half), (field_shape, real)],
        [smem, vmem, vmem],
        [],
        "prep",
        MIB,
        SMALL,
        info,
        probe,
        dft_tables(length),
    )
    chunk_shape = (chips, n_obj, modes, length // n_obj, 2 * (length // n_scan))
    grad, keep, give = call(
        (pattern_kernel,),
        [(patch_shape, half), (chunk_shape, half), (chunk_shape, half)],
        [smem] + [vmem] * (5 + n_scan),
        [
            pltpu.VMEM((2 * length, modes * length), half),
            pltpu.VMEM((modes * length, 2 * length), half),
            pltpu.VMEM((modes * length, 2 * length), real),
            pltpu.VMEM(patch_shape, real),
            pltpu.VMEM(field_shape, real),
            pltpu.VMEM((length, length), measured.dtype),
        ],
        "pattern",
        3 * 2 * 2 * modes * 8 * length**3,
        SMALL,
        info,
        mats,
        fresnel_tables(length),
        turned,
        own_part,
        piece,
        measured[0, 0],
        *others,
    )

    here = [along(grad, j) for j in range(1, chips)]
    there = [send(grad, lambda s, o, j=j: (s + CORES * j, o + 1)) for j in range(chips)]
    chunks = (keep.astype(real) + across(give).astype(real)).astype(half)
    chunks = sum((along(chunks[j], j).astype(real) for j in range(1, chips)), chunks[0].astype(real)).astype(half)
    here, there, _ = lax.optimization_barrier((here, there, chunks))
    chunks = lax.all_to_all(chunks, "obj", 0, 0, tiled=True)
    there, chunks = lax.optimization_barrier((there, chunks))
    held = [grad] + here + there
    held += [across(block) for block in held]
    kinds = [(tile, flip, j) for flip in range(2) for tile in (OWN, PREVIOUS) for j in range(chips)]
    factor = 1.0 / math.sqrt(n_scan * n_obj * slots // 2)
    object_grad, probe_grad = call(
        (place_kernel, kinds, factor),
        [
            ((layers, 2, tile_rows, tile_cols // n_scan), real),
            ((modes, 2, length // n_obj, length // n_scan), real),
        ],
        [smem, vmem] + [hbm] * len(held),
        [
            pltpu.VMEM((2 * n_scan, layers, *patch_shape[1:]), half),
            pltpu.SemaphoreType.DMA((2 * n_scan, layers)),
        ],
        "place",
        MIB,
        LARGE,
        info,
        chunks,
        *held,
    )
    return (object_grad, probe_grad)


def solution(mesh):
    return jax.shard_map(
        body,
        mesh=mesh,
        in_specs=(
            P(None, None, "obj", None),
            P(),
            P("scan", "obj", None, None, None),
            P("scan", "obj", None, None),
            P("scan", "obj"),
        ),
        out_specs=(P(None, None, "obj", "scan"), P(None, None, "obj", "scan")),
        check_vma=False,
    )
```

```python
import functools
import math

import jax
import jax.numpy as jnp
import ml_dtypes
import numpy as np
from jax import lax
from jax.experimental import pallas as pl
from jax.experimental.pallas import tpu as pltpu
from jax.sharding import PartitionSpec as P

AXES = ("scan", "obj")
CORES = 2
MIB = 1 << 20
SMALL, MIDDLE, LARGE = 20, 48, 56


def dft_tables(length):
    index = np.arange(length)
    angles = (index[:, None] * index[None, :] % length) * (2.0 * math.pi / length)
    parts = np.stack([np.cos(angles), -np.sin(angles)]) / math.sqrt(length)
    return parts.astype(np.float32).astype(ml_dtypes.bfloat16).astype(np.float32)


def fresnel_tables(length):
    index = np.arange(length)
    freqs = np.where(index < length // 2, index, index - length)
    squares = freqs * freqs
    phases = ((squares[:, None] + squares[None, :]) % (4 * length)) * (2.0 * math.pi / (4 * length))
    return np.stack([np.cos(phases), -np.sin(phases)]).astype(np.float32)


def send(block, move):
    n_scan, n_obj = lax.axis_size("scan"), lax.axis_size("obj")
    route = []
    for s in range(n_scan):
        for o in range(n_obj):
            goal = move(s, o)
            if goal is not None:
                route.append((s * n_obj + o, goal[0] % n_scan * n_obj + goal[1] % n_obj))
    return lax.ppermute(block, AXES, route)


OWN, PREVIOUS = 0, 1


def assigned(info, tile, target, n_scan):
    def entry(a, j):
        return info[a, 0, 8 * tile + j]

    idle = entry(target, 0) == 0
    counts = [entry(a, 0) for a in range(n_scan)]
    rank = jnp.int32(0)
    for a in range(n_scan):
        rank += jnp.where((counts[a] == 0) & (a < target), 1, 0)
    source = jnp.int32(target)
    seen = jnp.int32(0)
    for a in range(n_scan):
        full = counts[a] == 2
        source = jnp.where(idle & full & (seen == rank), a, source)
        seen += jnp.where(full, 1, 0)
    slot = jnp.where(idle, 1, 0)
    return source, slot, entry(source, 1 + 2 * slot), entry(source, 2 + 2 * slot)


def column_block(col, length, tile_cols):
    base = jnp.minimum(lax.div(col, length), tile_cols // length - 2)
    return base, col - base * length


STEP = 32


def lanes(length):
    return lax.broadcasted_iota(jnp.int32, (STEP, length), 1)


def lines(length):
    return lax.broadcasted_iota(jnp.int32, (STEP, length), 0)


def mul(ar, ai, br, bi):
    return ar * br - ai * bi, ar * bi + ai * br


def cmul(ar, ai, br, bi):
    return ar * br + ai * bi, ar * bi - ai * br


def fetch_columns(object_ref, wide, sems, base, length):
    layers, _, rows, _ = wide.shape
    start = pl.multiple_of(base * length, length)
    copies = []
    for l in range(layers):
        for q in range(2):
            for h in range(2):
                at = pl.ds(h * (rows // 2), rows // 2)
                copy = pltpu.make_async_copy(
                    object_ref.at[l, q, at, pl.ds(start, 2 * length)], wide.at[l, q, at], sems.at[l, q, h]
                )
                copy.start()
                copies.append(copy)
    return copies


def pick_columns(wide, l, q, at, off, length):
    return jnp.where(lanes(length) >= off, wide[l, q, at, :length], wide[l, q, at, length:])


def pick_kernel(sizes, own, info, object_ref, out_ref, wide, sems):
    n_scan, _, tile_cols = sizes
    layers, _, rows, length = out_ref.shape
    _, _, _, col = assigned(info, OWN if own else PREVIOUS, lax.axis_index("scan"), n_scan)
    base, off = column_block(col, length, tile_cols)
    copies = fetch_columns(object_ref, wide, sems, base, length)
    for l in range(layers):
        for q in range(2):
            for i in range(0, rows, STEP):
                if i % (rows // 2) == 0:
                    copies.pop(0).wait()
                at = pl.ds(i, STEP)
                out_ref[l, q, at, :] = pick_columns(wide, l, q, at, off, length).astype(out_ref.dtype)


def prep_kernel(sizes, info, probe_ref, dft_ref, mats, p_ref):
    n_scan, _, tile_cols = sizes
    modes, _, length, _ = probe_ref.shape
    _, _, row, col = assigned(info, OWN, lax.axis_index("scan"), n_scan)
    _, off = column_block(col, length, tile_cols)
    turn = lax.rem(off, length)

    def put(k, real, imag):
        mats[k, :length, :length] = real.astype(jnp.bfloat16)
        mats[k, length:, length:] = real.astype(jnp.bfloat16)
        mats[k, :length, length:] = imag.astype(jnp.bfloat16)
        mats[k, length:, :length] = (-imag).astype(jnp.bfloat16)

    real, imag = dft_ref[0], dft_ref[1]
    put(0, pltpu.roll(real, row, 1), -pltpu.roll(imag, row, 1))
    put(1, pltpu.roll(real, turn, 0), pltpu.roll(imag, turn, 0))
    put(2, pltpu.roll(real, row, 0), pltpu.roll(imag, row, 0))
    put(3, pltpu.roll(real, turn, 1), -pltpu.roll(imag, turn, 1))
    for m in range(modes):
        for q in range(2):
            p_ref[m, q] = pltpu.roll(pltpu.roll(probe_ref[m, q], row, 0), turn, 1)


def put_v(v_ref, length, m, i, real, imag):
    spot = slice(m * length, (m + 1) * length)
    v_ref[pl.ds(i, STEP), spot] = real.astype(jnp.bfloat16)
    v_ref[pl.ds(length + i, STEP), spot] = imag.astype(jnp.bfloat16)


def get_s(s_ref, length, m, i):
    at = pl.ds(m * length + i, STEP)
    return s_ref[at, :length], s_ref[at, length:]


def transform(mats, inverse, v_ref, u_ref, s_ref):
    length = mats.shape[1] // 2
    mid = jnp.dot(mats[2 * inverse], v_ref[...], preferred_element_type=jnp.float32).astype(jnp.bfloat16)
    for m in range(v_ref.shape[1] // length):
        for q in range(2):
            u_ref[m * length : (m + 1) * length, q * length : (q + 1) * length] = mid[
                q * length : (q + 1) * length, m * length : (m + 1) * length
            ]
    s_ref[...] = jnp.dot(u_ref[...], mats[2 * inverse + 1], preferred_element_type=jnp.float32)


def propagate(product, mats, fresnel_ref, v_in, v_ref, u_ref, s_ref):
    length = mats.shape[1] // 2
    transform(mats, 0, v_in, u_ref, s_ref)
    for i in range(0, length, STEP):
        at = pl.ds(i, STEP)
        kr, ki = fresnel_ref[0, at, :], fresnel_ref[1, at, :]
        for m in range(v_ref.shape[1] // length):
            put_v(v_ref, length, m, i, *product(kr, ki, *get_s(s_ref, length, m, i)))
    transform(mats, 1, v_ref, u_ref, s_ref)


def join(own, piece, i, row):
    return jnp.where(lines(own.shape[1]) >= row - i, own, piece.astype(jnp.float32))


def pattern_kernel(sizes, *refs):
    n_scan, n_obj, tile_cols = sizes
    info, mats, fresnel_ref, p_ref, xo_ref, piece, own_ref = refs[:7]
    others = refs[7 : 6 + n_scan]
    grad_ref, keep_ref, give_ref, v_ref, u_ref, s_ref, x_ref, a_ref, meas_ref = refs[6 + n_scan :]
    modes, _, length, _ = p_ref.shape
    me = lax.axis_index("scan")
    here = lax.axis_index("obj")
    core, chip, chips = lax.rem(me, CORES), lax.div(me, CORES), n_scan // CORES
    source, slot, row, col = assigned(info, OWN, me, n_scan)
    _, off = column_block(col, length, tile_cols)

    @pl.when(slot == 0)
    def _():
        meas_ref[...] = own_ref[0]

    for k in range(1, n_scan):
        @pl.when((slot == 1) & (source == lax.rem(me - k + n_scan, n_scan)))
        def _():
            meas_ref[...] = others[k - 1][...]

    for l in range(x_ref.shape[0]):
        for q in range(2):
            for i in range(0, length, STEP):
                at = pl.ds(i, STEP)
                x_ref[l, q, at, :] = join(xo_ref[l, q, at, :], piece[l, q, at, :], i, row)
    for i in range(0, length, STEP):
        at = pl.ds(i, STEP)
        xr, xi = x_ref[0, 0, at, :], x_ref[0, 1, at, :]
        for m in range(modes):
            put_v(v_ref, length, m, i, *mul(p_ref[m, 0, at, :], p_ref[m, 1, at, :], xr, xi))
    propagate(mul, mats, fresnel_ref, v_ref, v_ref, u_ref, s_ref)
    for i in range(0, length, STEP):
        at = pl.ds(i, STEP)
        xr, xi = x_ref[1, 0, at, :], x_ref[1, 1, at, :]
        for m in range(modes):
            ar, ai = get_s(s_ref, length, m, i)
            a_ref[m, 0, at, :] = ar
            a_ref[m, 1, at, :] = ai
            put_v(v_ref, length, m, i, *mul(ar, ai, xr, xi))
    transform(mats, 0, v_ref, u_ref, s_ref)
    for i in range(0, length, STEP):
        misfit = -meas_ref[pl.ds(i, STEP), :].astype(jnp.float32)
        for m in range(modes):
            fr, fi = get_s(s_ref, length, m, i)
            misfit += fr * fr + fi * fi
        for m in range(modes):
            fr, fi = get_s(s_ref, length, m, i)
            put_v(v_ref, length, m, i, misfit * fr, misfit * fi)
    transform(mats, 1, v_ref, u_ref, s_ref)
    for i in range(0, length, STEP):
        at = pl.ds(i, STEP)
        gr = gi = 0.0
        for m in range(modes):
            cr, ci = get_s(s_ref, length, m, i)
            dr, di = cmul(a_ref[m, 0, at, :], a_ref[m, 1, at, :], cr, ci)
            gr, gi = gr + dr, gi + di
            put_v(v_ref, length, m, i, *cmul(x_ref[1, 0, at, :], x_ref[1, 1, at, :], cr, ci))
        grad_ref[1, 0, at, :] = gr.astype(grad_ref.dtype)
        grad_ref[1, 1, at, :] = gi.astype(grad_ref.dtype)
    propagate(cmul, mats, fresnel_ref, v_ref, v_ref, u_ref, s_ref)
    for i in range(0, length, STEP):
        at = pl.ds(i, STEP)
        gr = gi = 0.0
        for m in range(modes):
            cr, ci = get_s(s_ref, length, m, i)
            dr, di = cmul(p_ref[m, 0, at, :], p_ref[m, 1, at, :], cr, ci)
            gr, gi = gr + dr, gi + di
            a_ref[m, 0, at, :], a_ref[m, 1, at, :] = cmul(x_ref[0, 0, at, :], x_ref[0, 1, at, :], cr, ci)
        grad_ref[0, 0, at, :] = gr.astype(grad_ref.dtype)
        grad_ref[0, 1, at, :] = gi.astype(grad_ref.dtype)
    row_back = lax.rem(length - row, length)
    col_back = lax.rem(2 * length - off, length)
    per_row, per_col = length // n_obj, length // n_scan
    lane = lax.broadcasted_iota(jnp.int32, (length, 128), 1)
    for m in range(modes):
        for q in range(2):
            a_ref[m, q] = pltpu.roll(pltpu.roll(a_ref[m, q], row_back, 0), col_back, 1)
        for s in range(n_scan):
            first, shift = s * per_col // 128 * 128, s * per_col % 128
            real = a_ref[m, 0, :, first : first + 128]
            imag = a_ref[m, 1, :, first : first + 128]
            real = pltpu.roll(real, (128 - shift) % 128, 1) if shift else real
            imag = pltpu.roll(imag, (per_col - shift) % 128, 1) if shift != per_col else imag
            both = jnp.where(lane < per_col, real, imag)[:, : 2 * per_col]
            apart = lax.rem(s // CORES - chip + chips, chips)
            for mine, ref in ((core, keep_ref), (1 - core, give_ref)):
                @pl.when(mine == s % CORES)
                def _():
                    for o in range(n_obj):
                        ref[apart, o ^ here, m] = both[o * per_row : (o + 1) * per_row].astype(ref.dtype)


def place_kernel(sizes, kinds, parts, factor, *refs):
    n_scan, n_obj, tile_cols = sizes
    layers = refs[-4].shape[0]
    info = refs[0]
    chunks = refs[1]
    patches = refs[2:-4]
    out_ref, probe_out, held, sems = refs[-4:]
    _, _, rows, width = out_ref.shape
    length = patches[0].shape[-1]
    me = lax.axis_index("scan")
    blocks = width // length
    first_block = me * blocks
    spots = []
    for index, (tile, flip, jump) in enumerate(kinds):
        source = lax.rem((me ^ flip) - CORES * jump + n_scan, n_scan)
        _, _, row, col = assigned(info, tile, source, n_scan)
        base, off = column_block(col, length, tile_cols)
        top, bottom = (row, rows) if tile == OWN else (0, row)
        meets = (base + 1 >= first_block) & (base < first_block + blocks)
        copies = [
            pltpu.make_async_copy(
                patches[number] if part is None else patches[number].at[part], held.at[index, l], sems.at[index, l]
            )
            for l, (number, part) in enumerate(parts[index])
        ]
        spots.append((base, off, top, bottom, meets, copies))

        @pl.when(meets)
        def _():
            for copy in copies:
                copy.start()

    out_ref[...] = jnp.zeros(out_ref.shape, jnp.float32)
    per_col = probe_out.shape[3]
    for m in range(probe_out.shape[0]):
        total = chunks[0, m].astype(jnp.float32) * factor
        probe_out[m, 0] = total[:, :per_col]
        probe_out[m, 1] = total[:, per_col:]
    lane, line = lanes(length), lines(length)
    for index, (base, off, top, bottom, meets, copies) in enumerate(spots):
        @pl.when(meets)
        def _():
            for copy in copies:
                copy.wait()
        for block in range(blocks):
            first, second = base == first_block + block, base + 1 == first_block + block
            left = jnp.where(first, off, 0)
            right = jnp.where(first, length, off)

            @pl.when(first | second)
            def _():
                cols = (lane >= left) & (lane < right)
                spot = slice(block * length, (block + 1) * length)
                for i in range(0, rows, STEP):
                    mask = cols & (line >= top - i) & (line < bottom - i)
                    at = pl.ds(i, STEP)
                    for l in range(layers):
                        for q in range(2):
                            value = held[index, l, q, at, :].astype(jnp.float32)
                            out_ref[l, q, at, spot] += jnp.where(mask, value, 0.0)


def body(object_slices, probe, measured, positions, counts):
    layers, _, tile_rows, tile_cols = object_slices.shape
    modes, _, length, _ = probe.shape
    slots = measured.shape[2]
    n_scan, n_obj = lax.axis_size("scan"), lax.axis_size("obj")
    chips = n_scan // CORES
    sizes = (n_scan, n_obj, tile_cols)
    smem = pl.BlockSpec(memory_space=pltpu.SMEM)
    vmem = pl.BlockSpec(memory_space=pltpu.VMEM)
    hbm = pl.BlockSpec(memory_space=pltpu.HBM)
    real, half = jnp.float32, jnp.bfloat16

    def call(kernel, outs, ins, scratch, name, flops, limit, *args):
        return pl.pallas_call(
            functools.partial(kernel[0], sizes, *kernel[1:]),
            out_shape=[jax.ShapeDtypeStruct(*o) for o in outs],
            in_specs=ins,
            out_specs=[vmem] * len(outs),
            scratch_shapes=scratch,
            compiler_params=pltpu.CompilerParams(vmem_limit_bytes=limit * MIB),
            cost_estimate=pl.CostEstimate(flops=flops, bytes_accessed=4 * MIB, transcendentals=0),
            name=name,
        )(*args)

    def across(block):
        return send(block, lambda s, o: (s ^ 1, o))

    def along(block, jump):
        return send(block, lambda s, o: (s + CORES * jump, o)) if jump else block

    def outward(block, sign):
        return send(block, lambda s, o: (s, o + sign))

    info = jnp.concatenate([counts[0], positions[0, 0].reshape(-1), jnp.zeros((3,), jnp.int32)])
    both = jnp.concatenate([info, send(info, lambda s, o: (s, o + 1))])
    info = lax.all_to_all(jnp.broadcast_to(both, (n_scan, 1, 16)), "scan", 0, 0, tiled=True)

    measured, info = lax.optimization_barrier((measured, info))
    second = measured[0, 0, 1]
    others = [send(second, lambda s, o, k=k: (s + k, o)) for k in range(1, n_scan)]

    patch_shape = (layers, 2, length, length)
    field_shape = (modes, 2, length, length)
    wide = [pltpu.VMEM((layers, 2, tile_rows, 2 * length), real), pltpu.SemaphoreType.DMA((layers, 2, 2))]
    (piece,) = call(
        (pick_kernel, False), [(patch_shape, half)], [smem, hbm], wide, "cut", MIB, LARGE, info, object_slices
    )
    piece = outward(piece, -1)
    (own_part,) = call(
        (pick_kernel, True), [(patch_shape, real)], [smem, hbm], wide, "own", MIB, MIDDLE, info, object_slices
    )
    mats, turned = call(
        (prep_kernel,),
        [((4, 2 * length, 2 * length), half), (field_shape, real)],
        [smem, vmem, vmem],
        [],
        "prep",
        MIB,
        SMALL,
        info,
        probe,
        dft_tables(length),
    )
    chunk_shape = (chips, n_obj, modes, length // n_obj, 2 * (length // n_scan))
    grad, keep, give = call(
        (pattern_kernel,),
        [(patch_shape, half), (chunk_shape, half), (chunk_shape, half)],
        [smem] + [vmem] * (5 + n_scan),
        [
            pltpu.VMEM((2 * length, modes * length), half),
            pltpu.VMEM((modes * length, 2 * length), half),
            pltpu.VMEM((modes * length, 2 * length), real),
            pltpu.VMEM(patch_shape, real),
            pltpu.VMEM(field_shape, real),
            pltpu.VMEM((length, length), measured.dtype),
        ],
        "pattern",
        3 * 2 * 2 * modes * 8 * length**3,
        SMALL,
        info,
        mats,
        fresnel_tables(length),
        turned,
        own_part,
        piece,
        measured[0, 0],
        *others,
    )

    def narrow(block):
        return block.astype(half)

    far = range(1, chips)
    here = [along(grad, j) for j in far]
    sums = narrow(keep.astype(real) + across(give).astype(real))
    there = outward(grad, 1)
    sums = narrow(sum((along(sums[j], j).astype(real) for j in far), sums[0].astype(real)))
    width = n_obj // 2
    while width:
        if width == n_obj // 4:
            here, there, sums = lax.optimization_barrier((here, there, sums))
        other = send(sums[width:], lambda s, o: (s, o ^ width))
        sums = narrow(sums[:width].astype(real) + other.astype(real))
        width //= 2
    x_first = [outward(block[1], 1) for block in here]
    obj_first = [along(there[0], j) for j in far]
    held = [grad] + here + [there] + x_first + obj_first
    held += [across(block) for block in held]
    kinds, parts = [], []
    for flip in range(2):
        start = flip * (len(held) // 2)
        for j in range(chips):
            kinds.append((OWN, flip, j))
            parts.append([(start + j, l) for l in range(layers)])
        for j in range(chips):
            kinds.append((PREVIOUS, flip, j))
            if j == 0:
                parts.append([(start + chips, l) for l in range(layers)])
            else:
                parts.append([(start + 2 * chips - 1 + j, None), (start + chips + j, None)])
    factor = 1.0 / math.sqrt(n_scan * n_obj * slots // 2)
    object_grad, probe_grad = call(
        (place_kernel, kinds, parts, factor),
        [
            ((layers, 2, tile_rows, tile_cols // n_scan), real),
            ((modes, 2, length // n_obj, length // n_scan), real),
        ],
        [smem, vmem] + [hbm] * len(held),
        [
            pltpu.VMEM((2 * n_scan, layers, *patch_shape[1:]), half),
            pltpu.SemaphoreType.DMA((2 * n_scan, layers)),
        ],
        "place",
        MIB,
        LARGE,
        info,
        sums,
        *held,
    )
    return (object_grad, probe_grad)


def solution(mesh):
    return jax.shard_map(
        body,
        mesh=mesh,
        in_specs=(
            P(None, None, "obj", None),
            P(),
            P("scan", "obj", None, None, None),
            P("scan", "obj", None, None),
            P("scan", "obj"),
        ),
        out_specs=(P(None, None, "obj", "scan"), P(None, None, "obj", "scan")),
        check_vma=False,
    )
```

```python
import functools
import math

import jax
import jax.numpy as jnp
import ml_dtypes
import numpy as np
from jax import lax
from jax.experimental import pallas as pl
from jax.experimental.pallas import tpu as pltpu
from jax.sharding import PartitionSpec as P

AXES = ("scan", "obj")
CORES = 2
MIB = 1 << 20
SMALL, MIDDLE, LARGE = 20, 48, 56


def dft_tables(length):
    index = np.arange(length)
    angles = (index[:, None] * index[None, :] % length) * (2.0 * math.pi / length)
    parts = np.stack([np.cos(angles), -np.sin(angles)]) / math.sqrt(length)
    return parts.astype(np.float32).astype(ml_dtypes.bfloat16).astype(np.float32)


def fresnel_tables(length):
    index = np.arange(length)
    freqs = np.where(index < length // 2, index, index - length)
    squares = freqs * freqs
    phases = ((squares[:, None] + squares[None, :]) % (4 * length)) * (2.0 * math.pi / (4 * length))
    return np.stack([np.cos(phases), -np.sin(phases)]).astype(np.float32)


def send(block, move):
    n_scan, n_obj = lax.axis_size("scan"), lax.axis_size("obj")
    route = []
    for s in range(n_scan):
        for o in range(n_obj):
            goal = move(s, o)
            if goal is not None:
                route.append((s * n_obj + o, goal[0] % n_scan * n_obj + goal[1] % n_obj))
    return lax.ppermute(block, AXES, route)


OWN, PREVIOUS = 0, 1


def assigned(info, tile, target, n_scan):
    def entry(a, j):
        return info[a, 0, 8 * tile + j]

    idle = entry(target, 0) == 0
    counts = [entry(a, 0) for a in range(n_scan)]
    rank = jnp.int32(0)
    for a in range(n_scan):
        rank += jnp.where((counts[a] == 0) & (a < target), 1, 0)
    source = jnp.int32(target)
    seen = jnp.int32(0)
    for a in range(n_scan):
        full = counts[a] == 2
        source = jnp.where(idle & full & (seen == rank), a, source)
        seen += jnp.where(full, 1, 0)
    slot = jnp.where(idle, 1, 0)
    return source, slot, entry(source, 1 + 2 * slot), entry(source, 2 + 2 * slot)


def column_block(col, length, tile_cols):
    base = jnp.minimum(lax.div(col, length), tile_cols // length - 2)
    return base, col - base * length


STEP = 32


def lanes(length):
    return lax.broadcasted_iota(jnp.int32, (STEP, length), 1)


def lines(length):
    return lax.broadcasted_iota(jnp.int32, (STEP, length), 0)


def mul(ar, ai, br, bi):
    return ar * br - ai * bi, ar * bi + ai * br


def cmul(ar, ai, br, bi):
    return ar * br + ai * bi, ar * bi - ai * br


def fetch_columns(object_ref, wide, sems, base, length):
    layers, _, rows, _ = wide.shape
    start = pl.multiple_of(base * length, length)
    copies = []
    for l in range(layers):
        for q in range(2):
            for h in range(2):
                at = pl.ds(h * (rows // 2), rows // 2)
                copy = pltpu.make_async_copy(
                    object_ref.at[l, q, at, pl.ds(start, 2 * length)], wide.at[l, q, at], sems.at[l, q, h]
                )
                copy.start()
                copies.append(copy)
    return copies


def pick_columns(wide, l, q, at, off, length):
    return jnp.where(lanes(length) >= off, wide[l, q, at, :length], wide[l, q, at, length:])


def pick_kernel(sizes, own, info, object_ref, out_ref, wide, sems):
    n_scan, _, tile_cols = sizes
    layers, _, rows, length = out_ref.shape
    _, _, _, col = assigned(info, OWN if own else PREVIOUS, lax.axis_index("scan"), n_scan)
    base, off = column_block(col, length, tile_cols)
    copies = fetch_columns(object_ref, wide, sems, base, length)
    for l in range(layers):
        for q in range(2):
            for i in range(0, rows, STEP):
                if i % (rows // 2) == 0:
                    copies.pop(0).wait()
                at = pl.ds(i, STEP)
                out_ref[l, q, at, :] = pick_columns(wide, l, q, at, off, length).astype(out_ref.dtype)


def prep_kernel(sizes, info, probe_ref, dft_ref, mats, p_ref):
    n_scan, _, tile_cols = sizes
    modes, _, length, _ = probe_ref.shape
    _, _, row, col = assigned(info, OWN, lax.axis_index("scan"), n_scan)
    _, off = column_block(col, length, tile_cols)
    turn = lax.rem(off, length)

    def put(k, real, imag):
        mats[k, :length, :length] = real.astype(jnp.bfloat16)
        mats[k, length:, length:] = real.astype(jnp.bfloat16)
        mats[k, :length, length:] = imag.astype(jnp.bfloat16)
        mats[k, length:, :length] = (-imag).astype(jnp.bfloat16)

    real, imag = dft_ref[0], dft_ref[1]
    put(0, pltpu.roll(real, row, 1), -pltpu.roll(imag, row, 1))
    put(1, pltpu.roll(real, turn, 0), pltpu.roll(imag, turn, 0))
    put(2, pltpu.roll(real, row, 0), pltpu.roll(imag, row, 0))
    put(3, pltpu.roll(real, turn, 1), -pltpu.roll(imag, turn, 1))
    for m in range(modes):
        for q in range(2):
            p_ref[m, q] = pltpu.roll(pltpu.roll(probe_ref[m, q], row, 0), turn, 1)


def put_v(v_ref, length, m, i, real, imag):
    spot = slice(m * length, (m + 1) * length)
    v_ref[pl.ds(i, STEP), spot] = real.astype(jnp.bfloat16)
    v_ref[pl.ds(length + i, STEP), spot] = imag.astype(jnp.bfloat16)


def get_s(s_ref, length, m, i):
    at = pl.ds(m * length + i, STEP)
    return s_ref[at, :length], s_ref[at, length:]


def transform(mats, inverse, v_ref, u_ref, s_ref):
    length = mats.shape[1] // 2
    mid = jnp.dot(mats[2 * inverse], v_ref[...], preferred_element_type=jnp.float32).astype(jnp.bfloat16)
    for m in range(v_ref.shape[1] // length):
        for q in range(2):
            u_ref[m * length : (m + 1) * length, q * length : (q + 1) * length] = mid[
                q * length : (q + 1) * length, m * length : (m + 1) * length
            ]
    s_ref[...] = jnp.dot(u_ref[...], mats[2 * inverse + 1], preferred_element_type=jnp.float32)


def propagate(product, mats, fresnel_ref, v_in, v_ref, u_ref, s_ref):
    length = mats.shape[1] // 2
    transform(mats, 0, v_in, u_ref, s_ref)
    for i in range(0, length, STEP):
        at = pl.ds(i, STEP)
        kr, ki = fresnel_ref[0, at, :], fresnel_ref[1, at, :]
        for m in range(v_ref.shape[1] // length):
            put_v(v_ref, length, m, i, *product(kr, ki, *get_s(s_ref, length, m, i)))
    transform(mats, 1, v_ref, u_ref, s_ref)


def join(own, piece, i, row):
    return jnp.where(lines(own.shape[1]) >= row - i, own, piece.astype(jnp.float32))


def pattern_kernel(sizes, *refs):
    n_scan, n_obj, tile_cols = sizes
    info, mats, fresnel_ref, p_ref, xo_ref, piece, own_ref = refs[:7]
    others = refs[7 : 6 + n_scan]
    grad_ref, keep_ref, give_ref, v_ref, u_ref, s_ref, x_ref, a_ref, meas_ref = refs[6 + n_scan :]
    modes, _, length, _ = p_ref.shape
    me = lax.axis_index("scan")
    core, chip, chips = lax.rem(me, CORES), lax.div(me, CORES), n_scan // CORES
    source, slot, row, col = assigned(info, OWN, me, n_scan)
    _, off = column_block(col, length, tile_cols)

    @pl.when(slot == 0)
    def _():
        meas_ref[...] = own_ref[0]

    for k in range(1, n_scan):
        @pl.when((slot == 1) & (source == lax.rem(me - k + n_scan, n_scan)))
        def _():
            meas_ref[...] = others[k - 1][...]

    for l in range(x_ref.shape[0]):
        for q in range(2):
            for i in range(0, length, STEP):
                at = pl.ds(i, STEP)
                x_ref[l, q, at, :] = join(xo_ref[l, q, at, :], piece[l, q, at, :], i, row)
    for i in range(0, length, STEP):
        at = pl.ds(i, STEP)
        xr, xi = x_ref[0, 0, at, :], x_ref[0, 1, at, :]
        for m in range(modes):
            put_v(v_ref, length, m, i, *mul(p_ref[m, 0, at, :], p_ref[m, 1, at, :], xr, xi))
    propagate(mul, mats, fresnel_ref, v_ref, v_ref, u_ref, s_ref)
    for i in range(0, length, STEP):
        at = pl.ds(i, STEP)
        xr, xi = x_ref[1, 0, at, :], x_ref[1, 1, at, :]
        for m in range(modes):
            ar, ai = get_s(s_ref, length, m, i)
            a_ref[m, 0, at, :] = ar
            a_ref[m, 1, at, :] = ai
            put_v(v_ref, length, m, i, *mul(ar, ai, xr, xi))
    transform(mats, 0, v_ref, u_ref, s_ref)
    for i in range(0, length, STEP):
        misfit = -meas_ref[pl.ds(i, STEP), :].astype(jnp.float32)
        for m in range(modes):
            fr, fi = get_s(s_ref, length, m, i)
            misfit += fr * fr + fi * fi
        for m in range(modes):
            fr, fi = get_s(s_ref, length, m, i)
            put_v(v_ref, length, m, i, misfit * fr, misfit * fi)
    transform(mats, 1, v_ref, u_ref, s_ref)
    for i in range(0, length, STEP):
        at = pl.ds(i, STEP)
        gr = gi = 0.0
        for m in range(modes):
            cr, ci = get_s(s_ref, length, m, i)
            dr, di = cmul(a_ref[m, 0, at, :], a_ref[m, 1, at, :], cr, ci)
            gr, gi = gr + dr, gi + di
            put_v(v_ref, length, m, i, *cmul(x_ref[1, 0, at, :], x_ref[1, 1, at, :], cr, ci))
        grad_ref[1, 0, at, :] = gr.astype(grad_ref.dtype)
        grad_ref[1, 1, at, :] = gi.astype(grad_ref.dtype)
    propagate(cmul, mats, fresnel_ref, v_ref, v_ref, u_ref, s_ref)
    for i in range(0, length, STEP):
        at = pl.ds(i, STEP)
        gr = gi = 0.0
        for m in range(modes):
            cr, ci = get_s(s_ref, length, m, i)
            dr, di = cmul(p_ref[m, 0, at, :], p_ref[m, 1, at, :], cr, ci)
            gr, gi = gr + dr, gi + di
            a_ref[m, 0, at, :], a_ref[m, 1, at, :] = cmul(x_ref[0, 0, at, :], x_ref[0, 1, at, :], cr, ci)
        grad_ref[0, 0, at, :] = gr.astype(grad_ref.dtype)
        grad_ref[0, 1, at, :] = gi.astype(grad_ref.dtype)
    row_back = lax.rem(length - row, length)
    col_back = lax.rem(2 * length - off, length)
    per_row, per_col = length // n_obj, length // n_scan
    lane = lax.broadcasted_iota(jnp.int32, (length, 128), 1)
    for m in range(modes):
        for q in range(2):
            a_ref[m, q] = pltpu.roll(pltpu.roll(a_ref[m, q], row_back, 0), col_back, 1)
        for s in range(n_scan):
            first, shift = s * per_col // 128 * 128, s * per_col % 128
            real = a_ref[m, 0, :, first : first + 128]
            imag = a_ref[m, 1, :, first : first + 128]
            real = pltpu.roll(real, (128 - shift) % 128, 1) if shift else real
            imag = pltpu.roll(imag, (per_col - shift) % 128, 1) if shift != per_col else imag
            both = jnp.where(lane < per_col, real, imag)[:, : 2 * per_col]
            apart = lax.rem(s // CORES - chip + chips, chips)
            for mine, ref in ((core, keep_ref), (1 - core, give_ref)):
                @pl.when(mine == s % CORES)
                def _():
                    for o in range(n_obj):
                        ref[o, apart, m] = both[o * per_row : (o + 1) * per_row].astype(ref.dtype)


def place_kernel(sizes, kinds, parts, factor, *refs):
    n_scan, _, tile_cols = sizes
    chips = n_scan // CORES
    layers = refs[-4].shape[0]
    info = refs[0]
    shares = refs[1 : 1 + chips]
    patches = refs[1 + chips : -4]
    out_ref, probe_out, held, sems = refs[-4:]
    _, _, rows, width = out_ref.shape
    length = patches[0].shape[-1]
    me = lax.axis_index("scan")
    blocks = width // length
    first_block = me * blocks
    spots = []
    for index, (tile, flip, jump) in enumerate(kinds):
        source = lax.rem((me ^ flip) - CORES * jump + n_scan, n_scan)
        _, _, row, col = assigned(info, tile, source, n_scan)
        base, off = column_block(col, length, tile_cols)
        top, bottom = (row, rows) if tile == OWN else (0, row)
        meets = (base + 1 >= first_block) & (base < first_block + blocks)
        copies = [
            pltpu.make_async_copy(
                patches[number] if part is None else patches[number].at[part], held.at[index, l], sems.at[index, l]
            )
            for l, (number, part) in enumerate(parts[index])
        ]
        spots.append((base, off, top, bottom, meets, copies))

        @pl.when(meets)
        def _():
            for copy in copies:
                copy.start()

    out_ref[...] = jnp.zeros(out_ref.shape, jnp.float32)
    per_col = probe_out.shape[3]
    for m in range(probe_out.shape[0]):
        total = sum(share[m].astype(jnp.float32) for share in shares) * factor
        probe_out[m, 0] = total[:, :per_col]
        probe_out[m, 1] = total[:, per_col:]
    lane, line = lanes(length), lines(length)
    for index, (base, off, top, bottom, meets, copies) in enumerate(spots):
        @pl.when(meets)
        def _():
            for copy in copies:
                copy.wait()
        for block in range(blocks):
            first, second = base == first_block + block, base + 1 == first_block + block
            left = jnp.where(first, off, 0)
            right = jnp.where(first, length, off)

            @pl.when(first | second)
            def _():
                cols = (lane >= left) & (lane < right)
                spot = slice(block * length, (block + 1) * length)
                for i in range(0, rows, STEP):
                    mask = cols & (line >= top - i) & (line < bottom - i)
                    at = pl.ds(i, STEP)
                    for l in range(layers):
                        for q in range(2):
                            value = held[index, l, q, at, :].astype(jnp.float32)
                            out_ref[l, q, at, spot] += jnp.where(mask, value, 0.0)


def body(object_slices, probe, measured, positions, counts):
    layers, _, tile_rows, tile_cols = object_slices.shape
    modes, _, length, _ = probe.shape
    slots = measured.shape[2]
    n_scan, n_obj = lax.axis_size("scan"), lax.axis_size("obj")
    chips = n_scan // CORES
    sizes = (n_scan, n_obj, tile_cols)
    smem = pl.BlockSpec(memory_space=pltpu.SMEM)
    vmem = pl.BlockSpec(memory_space=pltpu.VMEM)
    hbm = pl.BlockSpec(memory_space=pltpu.HBM)
    real, half = jnp.float32, jnp.bfloat16

    def call(kernel, outs, ins, scratch, name, flops, limit, *args):
        return pl.pallas_call(
            functools.partial(kernel[0], sizes, *kernel[1:]),
            out_shape=[jax.ShapeDtypeStruct(*o) for o in outs],
            in_specs=ins,
            out_specs=[vmem] * len(outs),
            scratch_shapes=scratch,
            compiler_params=pltpu.CompilerParams(vmem_limit_bytes=limit * MIB),
            cost_estimate=pl.CostEstimate(flops=flops, bytes_accessed=4 * MIB, transcendentals=0),
            name=name,
        )(*args)

    def across(block):
        return send(block, lambda s, o: (s ^ 1, o))

    def along(block, jump):
        return send(block, lambda s, o: (s + CORES * jump, o)) if jump else block

    def outward(block, sign):
        return send(block, lambda s, o: (s, o + sign))

    info = jnp.concatenate([counts[0], positions[0, 0].reshape(-1), jnp.zeros((3,), jnp.int32)])
    both = jnp.concatenate([info, send(info, lambda s, o: (s, o + 1))])
    info = lax.all_to_all(jnp.broadcast_to(both, (n_scan, 1, 16)), "scan", 0, 0, tiled=True)

    measured, info = lax.optimization_barrier((measured, info))
    second = measured[0, 0, 1]
    others = [send(second, lambda s, o, k=k: (s + k, o)) for k in range(1, n_scan)]

    patch_shape = (layers, 2, length, length)
    field_shape = (modes, 2, length, length)
    wide = [pltpu.VMEM((layers, 2, tile_rows, 2 * length), real), pltpu.SemaphoreType.DMA((layers, 2, 2))]
    (piece,) = call(
        (pick_kernel, False), [(patch_shape, half)], [smem, hbm], wide, "cut", MIB, LARGE, info, object_slices
    )
    piece = outward(piece, -1)
    (own_part,) = call(
        (pick_kernel, True), [(patch_shape, real)], [smem, hbm], wide, "own", MIB, MIDDLE, info, object_slices
    )
    mats, turned = call(
        (prep_kernel,),
        [((4, 2 * length, 2 * length), half), (field_shape, real)],
        [smem, vmem, vmem],
        [],
        "prep",
        MIB,
        SMALL,
        info,
        probe,
        dft_tables(length),
    )
    chunk_shape = (n_obj, chips, modes, length // n_obj, 2 * (length // n_scan))
    grad, keep, give = call(
        (pattern_kernel,),
        [(patch_shape, half), (chunk_shape, half), (chunk_shape, half)],
        [smem] + [vmem] * (5 + n_scan),
        [
            pltpu.VMEM((2 * length, modes * length), half),
            pltpu.VMEM((modes * length, 2 * length), half),
            pltpu.VMEM((modes * length, 2 * length), real),
            pltpu.VMEM(patch_shape, real),
            pltpu.VMEM(field_shape, real),
            pltpu.VMEM((length, length), measured.dtype),
        ],
        "pattern",
        3 * 2 * 2 * modes * 8 * length**3,
        SMALL,
        info,
        mats,
        fresnel_tables(length),
        turned,
        own_part,
        piece,
        measured[0, 0],
        *others,
    )

    here = [grad] + [along(grad, j) for j in range(1, chips)]
    chunks = (keep.astype(real) + across(give).astype(real)).astype(half)
    first, chunks = lax.optimization_barrier((grad, chunks))
    there = outward(first, 1)
    x_first = [outward(block[1], 1) for block in here[1:]]
    obj_first = [along(there[0], j) for j in range(1, chips)]
    held = here + [there] + x_first + obj_first
    held += [across(block) for block in held]
    kinds, parts = [], []
    for flip in range(2):
        start = flip * (len(held) // 2)
        for j in range(chips):
            kinds.append((OWN, flip, j))
            parts.append([(start + j, l) for l in range(layers)])
        for j in range(chips):
            kinds.append((PREVIOUS, flip, j))
            if j == 0:
                parts.append([(start + chips, l) for l in range(layers)])
            else:
                parts.append([(start + 2 * chips - 1 + j, None), (start + chips + j, None)])
    chunks = lax.all_to_all(chunks, "obj", 0, 0, tiled=True)
    chunks = jnp.sum(chunks.astype(real), axis=0).astype(half)
    shares = [along(chunks[j], j) for j in range(chips)]
    factor = 1.0 / math.sqrt(n_scan * n_obj * slots // 2)
    object_grad, probe_grad = call(
        (place_kernel, kinds, parts, factor),
        [
            ((layers, 2, tile_rows, tile_cols // n_scan), real),
            ((modes, 2, length // n_obj, length // n_scan), real),
        ],
        [smem] + [vmem] * chips + [hbm] * len(held),
        [
            pltpu.VMEM((2 * n_scan, layers, *patch_shape[1:]), half),
            pltpu.SemaphoreType.DMA((2 * n_scan, layers)),
        ],
        "place",
        MIB,
        LARGE,
        info,
        *shares,
        *held,
    )
    return (object_grad, probe_grad)


def solution(mesh):
    return jax.shard_map(
        body,
        mesh=mesh,
        in_specs=(
            P(None, None, "obj", None),
            P(),
            P("scan", "obj", None, None, None),
            P("scan", "obj", None, None),
            P("scan", "obj"),
        ),
        out_specs=(P(None, None, "obj", "scan"), P(None, None, "obj", "scan")),
        check_vma=False,
    )
```

```python
import functools
import math

import jax
import jax.numpy as jnp
import ml_dtypes
import numpy as np
from jax import lax
from jax.experimental import pallas as pl
from jax.experimental.pallas import tpu as pltpu
from jax.sharding import PartitionSpec as P

AXES = ("scan", "obj")
CORES = 2
MIB = 1 << 20
SMALL, MIDDLE, LARGE = 20, 48, 56


def dft_tables(length):
    index = np.arange(length)
    angles = (index[:, None] * index[None, :] % length) * (2.0 * math.pi / length)
    parts = np.stack([np.cos(angles), -np.sin(angles)]) / math.sqrt(length)
    return parts.astype(np.float32).astype(ml_dtypes.bfloat16).astype(np.float32)


def fresnel_tables(length):
    index = np.arange(length)
    freqs = np.where(index < length // 2, index, index - length)
    squares = freqs * freqs
    phases = ((squares[:, None] + squares[None, :]) % (4 * length)) * (2.0 * math.pi / (4 * length))
    return np.stack([np.cos(phases), -np.sin(phases)]).astype(np.float32)


def send(block, move):
    n_scan, n_obj = lax.axis_size("scan"), lax.axis_size("obj")
    route = []
    for s in range(n_scan):
        for o in range(n_obj):
            goal = move(s, o)
            if goal is not None:
                route.append((s * n_obj + o, goal[0] % n_scan * n_obj + goal[1] % n_obj))
    return lax.ppermute(block, AXES, route)


OWN, PREVIOUS = 0, 1


def assigned(info, tile, target, n_scan):
    def entry(a, j):
        return info[a, 0, 8 * tile + j]

    idle = entry(target, 0) == 0
    counts = [entry(a, 0) for a in range(n_scan)]
    rank = jnp.int32(0)
    for a in range(n_scan):
        rank += jnp.where((counts[a] == 0) & (a < target), 1, 0)
    source = jnp.int32(target)
    seen = jnp.int32(0)
    for a in range(n_scan):
        full = counts[a] == 2
        source = jnp.where(idle & full & (seen == rank), a, source)
        seen += jnp.where(full, 1, 0)
    slot = jnp.where(idle, 1, 0)
    return source, slot, entry(source, 1 + 2 * slot), entry(source, 2 + 2 * slot)


def column_block(col, length, tile_cols):
    base = jnp.minimum(lax.div(col, length), tile_cols // length - 2)
    return base, col - base * length


STEP = 32


def lanes(length):
    return lax.broadcasted_iota(jnp.int32, (STEP, length), 1)


def lines(length):
    return lax.broadcasted_iota(jnp.int32, (STEP, length), 0)


def mul(ar, ai, br, bi):
    return ar * br - ai * bi, ar * bi + ai * br


def cmul(ar, ai, br, bi):
    return ar * br + ai * bi, ar * bi - ai * br


def fetch_columns(object_ref, wide, sems, base, length):
    layers, _, rows, _ = wide.shape
    start = pl.multiple_of(base * length, length)
    copies = []
    for l in range(layers):
        for q in range(2):
            for h in range(2):
                at = pl.ds(h * (rows // 2), rows // 2)
                copy = pltpu.make_async_copy(
                    object_ref.at[l, q, at, pl.ds(start, 2 * length)], wide.at[l, q, at], sems.at[l, q, h]
                )
                copy.start()
                copies.append(copy)
    return copies


def pick_columns(wide, l, q, at, off, length):
    return jnp.where(lanes(length) >= off, wide[l, q, at, :length], wide[l, q, at, length:])


def pick_kernel(sizes, own, info, object_ref, out_ref, wide, sems):
    n_scan, _, tile_cols = sizes
    layers, _, rows, length = out_ref.shape
    _, _, _, col = assigned(info, OWN if own else PREVIOUS, lax.axis_index("scan"), n_scan)
    base, off = column_block(col, length, tile_cols)
    copies = fetch_columns(object_ref, wide, sems, base, length)
    for l in range(layers):
        for q in range(2):
            for i in range(0, rows, STEP):
                if i % (rows // 2) == 0:
                    copies.pop(0).wait()
                at = pl.ds(i, STEP)
                out_ref[l, q, at, :] = pick_columns(wide, l, q, at, off, length).astype(out_ref.dtype)


def prep_kernel(sizes, info, probe_ref, dft_ref, mats, p_ref):
    n_scan, _, tile_cols = sizes
    modes, _, length, _ = probe_ref.shape
    _, _, row, col = assigned(info, OWN, lax.axis_index("scan"), n_scan)
    _, off = column_block(col, length, tile_cols)
    turn = lax.rem(off, length)

    def put(k, real, imag):
        mats[k, :length, :length] = real.astype(jnp.bfloat16)
        mats[k, length:, length:] = real.astype(jnp.bfloat16)
        mats[k, :length, length:] = imag.astype(jnp.bfloat16)
        mats[k, length:, :length] = (-imag).astype(jnp.bfloat16)

    real, imag = dft_ref[0], dft_ref[1]
    put(0, pltpu.roll(real, row, 1), -pltpu.roll(imag, row, 1))
    put(1, pltpu.roll(real, turn, 0), pltpu.roll(imag, turn, 0))
    put(2, pltpu.roll(real, row, 0), pltpu.roll(imag, row, 0))
    put(3, pltpu.roll(real, turn, 1), -pltpu.roll(imag, turn, 1))
    for m in range(modes):
        for q in range(2):
            p_ref[m, q] = pltpu.roll(pltpu.roll(probe_ref[m, q], row, 0), turn, 1)


def put_v(v_ref, length, m, i, real, imag):
    spot = slice(m * length, (m + 1) * length)
    v_ref[pl.ds(i, STEP), spot] = real.astype(jnp.bfloat16)
    v_ref[pl.ds(length + i, STEP), spot] = imag.astype(jnp.bfloat16)


def get_s(s_ref, length, m, i):
    at = pl.ds(m * length + i, STEP)
    return s_ref[at, :length], s_ref[at, length:]


def transform(mats, inverse, v_ref, u_ref, s_ref):
    length = mats.shape[1] // 2
    mid = jnp.dot(mats[2 * inverse], v_ref[...], preferred_element_type=jnp.float32).astype(jnp.bfloat16)
    for m in range(v_ref.shape[1] // length):
        for q in range(2):
            u_ref[m * length : (m + 1) * length, q * length : (q + 1) * length] = mid[
                q * length : (q + 1) * length, m * length : (m + 1) * length
            ]
    s_ref[...] = jnp.dot(u_ref[...], mats[2 * inverse + 1], preferred_element_type=jnp.float32)


def propagate(product, mats, fresnel_ref, v_in, v_ref, u_ref, s_ref):
    length = mats.shape[1] // 2
    transform(mats, 0, v_in, u_ref, s_ref)
    for i in range(0, length, STEP):
        at = pl.ds(i, STEP)
        kr, ki = fresnel_ref[0, at, :], fresnel_ref[1, at, :]
        for m in range(v_ref.shape[1] // length):
            put_v(v_ref, length, m, i, *product(kr, ki, *get_s(s_ref, length, m, i)))
    transform(mats, 1, v_ref, u_ref, s_ref)


def join(own, piece, i, row):
    return jnp.where(lines(own.shape[1]) >= row - i, own, piece.astype(jnp.float32))


def pattern_kernel(sizes, *refs):
    n_scan, n_obj, tile_cols = sizes
    info, mats, fresnel_ref, p_ref, xo_ref, piece, own_ref = refs[:7]
    others = refs[7 : 6 + n_scan]
    grad_ref, keep_ref, give_ref, v_ref, u_ref, s_ref, x_ref, a_ref, meas_ref = refs[6 + n_scan :]
    modes, _, length, _ = p_ref.shape
    me = lax.axis_index("scan")
    core, chip, chips = lax.rem(me, CORES), lax.div(me, CORES), n_scan // CORES
    source, slot, row, col = assigned(info, OWN, me, n_scan)
    _, off = column_block(col, length, tile_cols)

    @pl.when(slot == 0)
    def _():
        meas_ref[...] = own_ref[0]

    for k in range(1, n_scan):
        @pl.when((slot == 1) & (source == lax.rem(me - k + n_scan, n_scan)))
        def _():
            meas_ref[...] = others[k - 1][...]

    for l in range(x_ref.shape[0]):
        for q in range(2):
            for i in range(0, length, STEP):
                at = pl.ds(i, STEP)
                x_ref[l, q, at, :] = join(xo_ref[l, q, at, :], piece[l, q, at, :], i, row)
    for i in range(0, length, STEP):
        at = pl.ds(i, STEP)
        xr, xi = x_ref[0, 0, at, :], x_ref[0, 1, at, :]
        for m in range(modes):
            put_v(v_ref, length, m, i, *mul(p_ref[m, 0, at, :], p_ref[m, 1, at, :], xr, xi))
    propagate(mul, mats, fresnel_ref, v_ref, v_ref, u_ref, s_ref)
    for i in range(0, length, STEP):
        at = pl.ds(i, STEP)
        xr, xi = x_ref[1, 0, at, :], x_ref[1, 1, at, :]
        for m in range(modes):
            ar, ai = get_s(s_ref, length, m, i)
            a_ref[m, 0, at, :] = ar
            a_ref[m, 1, at, :] = ai
            put_v(v_ref, length, m, i, *mul(ar, ai, xr, xi))
    transform(mats, 0, v_ref, u_ref, s_ref)
    for i in range(0, length, STEP):
        misfit = -meas_ref[pl.ds(i, STEP), :].astype(jnp.float32)
        for m in range(modes):
            fr, fi = get_s(s_ref, length, m, i)
            misfit += fr * fr + fi * fi
        for m in range(modes):
            fr, fi = get_s(s_ref, length, m, i)
            put_v(v_ref, length, m, i, misfit * fr, misfit * fi)
    transform(mats, 1, v_ref, u_ref, s_ref)
    for i in range(0, length, STEP):
        at = pl.ds(i, STEP)
        gr = gi = 0.0
        for m in range(modes):
            cr, ci = get_s(s_ref, length, m, i)
            dr, di = cmul(a_ref[m, 0, at, :], a_ref[m, 1, at, :], cr, ci)
            gr, gi = gr + dr, gi + di
            put_v(v_ref, length, m, i, *cmul(x_ref[1, 0, at, :], x_ref[1, 1, at, :], cr, ci))
        grad_ref[1, 0, at, :] = gr.astype(grad_ref.dtype)
        grad_ref[1, 1, at, :] = gi.astype(grad_ref.dtype)
    propagate(cmul, mats, fresnel_ref, v_ref, v_ref, u_ref, s_ref)
    for i in range(0, length, STEP):
        at = pl.ds(i, STEP)
        gr = gi = 0.0
        for m in range(modes):
            cr, ci = get_s(s_ref, length, m, i)
            dr, di = cmul(p_ref[m, 0, at, :], p_ref[m, 1, at, :], cr, ci)
            gr, gi = gr + dr, gi + di
            a_ref[m, 0, at, :], a_ref[m, 1, at, :] = cmul(x_ref[0, 0, at, :], x_ref[0, 1, at, :], cr, ci)
        grad_ref[0, 0, at, :] = gr.astype(grad_ref.dtype)
        grad_ref[0, 1, at, :] = gi.astype(grad_ref.dtype)
    row_back = lax.rem(length - row, length)
    col_back = lax.rem(2 * length - off, length)
    per_row, per_col = length // n_obj, length // n_scan
    lane = lax.broadcasted_iota(jnp.int32, (length, 128), 1)
    for m in range(modes):
        for q in range(2):
            a_ref[m, q] = pltpu.roll(pltpu.roll(a_ref[m, q], row_back, 0), col_back, 1)
        for s in range(n_scan):
            first, shift = s * per_col // 128 * 128, s * per_col % 128
            real = a_ref[m, 0, :, first : first + 128]
            imag = a_ref[m, 1, :, first : first + 128]
            real = pltpu.roll(real, (128 - shift) % 128, 1) if shift else real
            imag = pltpu.roll(imag, (per_col - shift) % 128, 1) if shift != per_col else imag
            both = jnp.where(lane < per_col, real, imag)[:, : 2 * per_col]
            apart = lax.rem(s // CORES - chip + chips, chips)
            for mine, ref in ((core, keep_ref), (1 - core, give_ref)):
                @pl.when(mine == s % CORES)
                def _():
                    for o in range(n_obj):
                        ref[o, apart, m] = both[o * per_row : (o + 1) * per_row].astype(ref.dtype)


def place_kernel(sizes, kinds, parts, factor, *refs):
    n_scan, _, tile_cols = sizes
    chips = n_scan // CORES
    layers = refs[-4].shape[0]
    info = refs[0]
    shares = refs[1 : 1 + chips]
    patches = refs[1 + chips : -4]
    out_ref, probe_out, held, sems = refs[-4:]
    _, _, rows, width = out_ref.shape
    length = patches[0].shape[-1]
    me = lax.axis_index("scan")
    blocks = width // length
    first_block = me * blocks
    spots = []
    for index, (tile, flip, jump) in enumerate(kinds):
        source = lax.rem((me ^ flip) - CORES * jump + n_scan, n_scan)
        _, _, row, col = assigned(info, tile, source, n_scan)
        base, off = column_block(col, length, tile_cols)
        top, bottom = (row, rows) if tile == OWN else (0, row)
        meets = (base + 1 >= first_block) & (base < first_block + blocks)
        copies = [
            pltpu.make_async_copy(
                patches[number] if part is None else patches[number].at[part], held.at[index, l], sems.at[index, l]
            )
            for l, (number, part) in enumerate(parts[index])
        ]
        spots.append((base, off, top, bottom, meets, copies))

        @pl.when(meets)
        def _():
            for copy in copies:
                copy.start()

    out_ref[...] = jnp.zeros(out_ref.shape, jnp.float32)
    per_col = probe_out.shape[3]
    for m in range(probe_out.shape[0]):
        total = sum(share[m].astype(jnp.float32) for share in shares) * factor
        probe_out[m, 0] = total[:, :per_col]
        probe_out[m, 1] = total[:, per_col:]
    lane, line = lanes(length), lines(length)
    for index, (base, off, top, bottom, meets, copies) in enumerate(spots):
        @pl.when(meets)
        def _():
            for copy in copies:
                copy.wait()
        for block in range(blocks):
            first, second = base == first_block + block, base + 1 == first_block + block
            left = jnp.where(first, off, 0)
            right = jnp.where(first, length, off)

            @pl.when(first | second)
            def _():
                cols = (lane >= left) & (lane < right)
                spot = slice(block * length, (block + 1) * length)
                for i in range(0, rows, STEP):
                    mask = cols & (line >= top - i) & (line < bottom - i)
                    at = pl.ds(i, STEP)
                    for l in range(layers):
                        for q in range(2):
                            value = held[index, l, q, at, :].astype(jnp.float32)
                            out_ref[l, q, at, spot] += jnp.where(mask, value, 0.0)


def body(object_slices, probe, measured, positions, counts):
    layers, _, tile_rows, tile_cols = object_slices.shape
    modes, _, length, _ = probe.shape
    slots = measured.shape[2]
    n_scan, n_obj = lax.axis_size("scan"), lax.axis_size("obj")
    chips = n_scan // CORES
    sizes = (n_scan, n_obj, tile_cols)
    smem = pl.BlockSpec(memory_space=pltpu.SMEM)
    vmem = pl.BlockSpec(memory_space=pltpu.VMEM)
    hbm = pl.BlockSpec(memory_space=pltpu.HBM)
    real, half = jnp.float32, jnp.bfloat16

    def call(kernel, outs, ins, scratch, name, flops, limit, *args):
        return pl.pallas_call(
            functools.partial(kernel[0], sizes, *kernel[1:]),
            out_shape=[jax.ShapeDtypeStruct(*o) for o in outs],
            in_specs=ins,
            out_specs=[vmem] * len(outs),
            scratch_shapes=scratch,
            compiler_params=pltpu.CompilerParams(vmem_limit_bytes=limit * MIB),
            cost_estimate=pl.CostEstimate(flops=flops, bytes_accessed=4 * MIB, transcendentals=0),
            name=name,
        )(*args)

    def across(block):
        return send(block, lambda s, o: (s ^ 1, o))

    def along(block, jump):
        return send(block, lambda s, o: (s + CORES * jump, o)) if jump else block

    def outward(block, sign):
        return send(block, lambda s, o: (s, o + sign))

    info = jnp.concatenate([counts[0], positions[0, 0].reshape(-1), jnp.zeros((3,), jnp.int32)])
    both = jnp.concatenate([info, send(info, lambda s, o: (s, o + 1))])
    info = lax.all_to_all(jnp.broadcast_to(both, (n_scan, 1, 16)), "scan", 0, 0, tiled=True)

    measured, info = lax.optimization_barrier((measured, info))
    second = measured[0, 0, 1]
    others = [send(second, lambda s, o, k=k: (s + k, o)) for k in range(1, n_scan)]

    patch_shape = (layers, 2, length, length)
    field_shape = (modes, 2, length, length)
    wide = [pltpu.VMEM((layers, 2, tile_rows, 2 * length), real), pltpu.SemaphoreType.DMA((layers, 2, 2))]
    (piece,) = call(
        (pick_kernel, False), [(patch_shape, half)], [smem, hbm], wide, "cut", MIB, LARGE, info, object_slices
    )
    piece = outward(piece, -1)
    (own_part,) = call(
        (pick_kernel, True), [(patch_shape, real)], [smem, hbm], wide, "own", MIB, MIDDLE, info, object_slices
    )
    mats, turned = call(
        (prep_kernel,),
        [((4, 2 * length, 2 * length), half), (field_shape, real)],
        [smem, vmem, vmem],
        [],
        "prep",
        MIB,
        SMALL,
        info,
        probe,
        dft_tables(length),
    )
    chunk_shape = (n_obj, chips, modes, length // n_obj, 2 * (length // n_scan))
    grad, keep, give = call(
        (pattern_kernel,),
        [(patch_shape, half), (chunk_shape, half), (chunk_shape, half)],
        [smem] + [vmem] * (5 + n_scan),
        [
            pltpu.VMEM((2 * length, modes * length), half),
            pltpu.VMEM((modes * length, 2 * length), half),
            pltpu.VMEM((modes * length, 2 * length), real),
            pltpu.VMEM(patch_shape, real),
            pltpu.VMEM(field_shape, real),
            pltpu.VMEM((length, length), measured.dtype),
        ],
        "pattern",
        3 * 2 * 2 * modes * 8 * length**3,
        SMALL,
        info,
        mats,
        fresnel_tables(length),
        turned,
        own_part,
        piece,
        measured[0, 0],
        *others,
    )

    there = outward(grad, 1)
    chunks = (keep.astype(real) + across(give).astype(real)).astype(half)
    first, chunks = lax.optimization_barrier((grad, chunks))
    here = [grad] + [along(first, j) for j in range(1, chips)]
    x_first = [outward(block[1], 1) for block in here[1:]]
    obj_first = [along(there[0], j) for j in range(1, chips)]
    held = here + [there] + x_first + obj_first
    held += [across(block) for block in held]
    kinds, parts = [], []
    for flip in range(2):
        start = flip * (len(held) // 2)
        for j in range(chips):
            kinds.append((OWN, flip, j))
            parts.append([(start + j, l) for l in range(layers)])
        for j in range(chips):
            kinds.append((PREVIOUS, flip, j))
            if j == 0:
                parts.append([(start + chips, l) for l in range(layers)])
            else:
                parts.append([(start + 2 * chips - 1 + j, None), (start + chips + j, None)])
    chunks = lax.all_to_all(chunks, "obj", 0, 0, tiled=True)
    chunks = jnp.sum(chunks.astype(real), axis=0).astype(half)
    shares = [along(chunks[j], j) for j in range(chips)]
    factor = 1.0 / math.sqrt(n_scan * n_obj * slots // 2)
    object_grad, probe_grad = call(
        (place_kernel, kinds, parts, factor),
        [
            ((layers, 2, tile_rows, tile_cols // n_scan), real),
            ((modes, 2, length // n_obj, length // n_scan), real),
        ],
        [smem] + [vmem] * chips + [hbm] * len(held),
        [
            pltpu.VMEM((2 * n_scan, layers, *patch_shape[1:]), half),
            pltpu.SemaphoreType.DMA((2 * n_scan, layers)),
        ],
        "place",
        MIB,
        LARGE,
        info,
        *shares,
        *held,
    )
    return (object_grad, probe_grad)


def solution(mesh):
    return jax.shard_map(
        body,
        mesh=mesh,
        in_specs=(
            P(None, None, "obj", None),
            P(),
            P("scan", "obj", None, None, None),
            P("scan", "obj", None, None),
            P("scan", "obj"),
        ),
        out_specs=(P(None, None, "obj", "scan"), P(None, None, "obj", "scan")),
        check_vma=False,
    )
```

```python
import functools
import math

import jax
import jax.numpy as jnp
import ml_dtypes
import numpy as np
from jax import lax
from jax.experimental import pallas as pl
from jax.experimental.pallas import tpu as pltpu
from jax.sharding import PartitionSpec as P

AXES = ("scan", "obj")
CORES = 2
MIB = 1 << 20
SMALL, MIDDLE, LARGE = 20, 48, 56


def dft_tables(length):
    index = np.arange(length)
    angles = (index[:, None] * index[None, :] % length) * (2.0 * math.pi / length)
    parts = np.stack([np.cos(angles), -np.sin(angles)]) / math.sqrt(length)
    return parts.astype(np.float32).astype(ml_dtypes.bfloat16).astype(np.float32)


def fresnel_tables(length):
    index = np.arange(length)
    freqs = np.where(index < length // 2, index, index - length)
    squares = freqs * freqs
    phases = ((squares[:, None] + squares[None, :]) % (4 * length)) * (2.0 * math.pi / (4 * length))
    return np.stack([np.cos(phases), -np.sin(phases)]).astype(np.float32)


def send(block, move):
    n_scan, n_obj = lax.axis_size("scan"), lax.axis_size("obj")
    route = []
    for s in range(n_scan):
        for o in range(n_obj):
            goal = move(s, o)
            if goal is not None:
                route.append((s * n_obj + o, goal[0] % n_scan * n_obj + goal[1] % n_obj))
    return lax.ppermute(block, AXES, route)


OWN, PREVIOUS = 0, 1


def assigned(info, tile, target, n_scan):
    def entry(a, j):
        return info[a, 0, 8 * tile + j]

    idle = entry(target, 0) == 0
    counts = [entry(a, 0) for a in range(n_scan)]
    rank = jnp.int32(0)
    for a in range(n_scan):
        rank += jnp.where((counts[a] == 0) & (a < target), 1, 0)
    source = jnp.int32(target)
    seen = jnp.int32(0)
    for a in range(n_scan):
        full = counts[a] == 2
        source = jnp.where(idle & full & (seen == rank), a, source)
        seen += jnp.where(full, 1, 0)
    slot = jnp.where(idle, 1, 0)
    return source, slot, entry(source, 1 + 2 * slot), entry(source, 2 + 2 * slot)


def column_block(col, length, tile_cols):
    base = jnp.minimum(lax.div(col, length), tile_cols // length - 2)
    return base, col - base * length


STEP = 32


def lanes(length):
    return lax.broadcasted_iota(jnp.int32, (STEP, length), 1)


def lines(length):
    return lax.broadcasted_iota(jnp.int32, (STEP, length), 0)


def mul(ar, ai, br, bi):
    return ar * br - ai * bi, ar * bi + ai * br


def cmul(ar, ai, br, bi):
    return ar * br + ai * bi, ar * bi - ai * br


def fetch_columns(object_ref, wide, sems, base, length):
    layers, _, rows, _ = wide.shape
    start = pl.multiple_of(base * length, length)
    copies = []
    for l in range(layers):
        for q in range(2):
            for h in range(2):
                at = pl.ds(h * (rows // 2), rows // 2)
                copy = pltpu.make_async_copy(
                    object_ref.at[l, q, at, pl.ds(start, 2 * length)], wide.at[l, q, at], sems.at[l, q, h]
                )
                copy.start()
                copies.append(copy)
    return copies


def pick_columns(wide, l, q, at, off, length):
    return jnp.where(lanes(length) >= off, wide[l, q, at, :length], wide[l, q, at, length:])


def pick_kernel(sizes, own, info, object_ref, out_ref, wide, sems):
    n_scan, _, tile_cols = sizes
    layers, _, rows, length = out_ref.shape
    _, _, _, col = assigned(info, OWN if own else PREVIOUS, lax.axis_index("scan"), n_scan)
    base, off = column_block(col, length, tile_cols)
    copies = fetch_columns(object_ref, wide, sems, base, length)
    for l in range(layers):
        for q in range(2):
            for i in range(0, rows, STEP):
                if i % (rows // 2) == 0:
                    copies.pop(0).wait()
                at = pl.ds(i, STEP)
                out_ref[l, q, at, :] = pick_columns(wide, l, q, at, off, length).astype(out_ref.dtype)


def prep_kernel(sizes, info, probe_ref, dft_ref, mats, p_ref):
    n_scan, _, tile_cols = sizes
    modes, _, length, _ = probe_ref.shape
    _, _, row, col = assigned(info, OWN, lax.axis_index("scan"), n_scan)
    _, off = column_block(col, length, tile_cols)
    turn = lax.rem(off, length)

    def put(k, real, imag):
        mats[k, :length, :length] = real.astype(jnp.bfloat16)
        mats[k, length:, length:] = real.astype(jnp.bfloat16)
        mats[k, :length, length:] = imag.astype(jnp.bfloat16)
        mats[k, length:, :length] = (-imag).astype(jnp.bfloat16)

    real, imag = dft_ref[0], dft_ref[1]
    put(0, pltpu.roll(real, row, 1), -pltpu.roll(imag, row, 1))
    put(1, pltpu.roll(real, turn, 0), pltpu.roll(imag, turn, 0))
    put(2, pltpu.roll(real, row, 0), pltpu.roll(imag, row, 0))
    put(3, pltpu.roll(real, turn, 1), -pltpu.roll(imag, turn, 1))
    for m in range(modes):
        for q in range(2):
            p_ref[m, q] = pltpu.roll(pltpu.roll(probe_ref[m, q], row, 0), turn, 1)


def put_v(v_ref, length, m, i, real, imag):
    spot = slice(m * length, (m + 1) * length)
    v_ref[pl.ds(i, STEP), spot] = real.astype(jnp.bfloat16)
    v_ref[pl.ds(length + i, STEP), spot] = imag.astype(jnp.bfloat16)


def get_s(s_ref, length, m, i):
    at = pl.ds(m * length + i, STEP)
    return s_ref[at, :length], s_ref[at, length:]


def transform(mats, inverse, v_ref, u_ref, s_ref):
    length = mats.shape[1] // 2
    mid = jnp.dot(mats[2 * inverse], v_ref[...], preferred_element_type=jnp.float32).astype(jnp.bfloat16)
    for m in range(v_ref.shape[1] // length):
        for q in range(2):
            u_ref[m * length : (m + 1) * length, q * length : (q + 1) * length] = mid[
                q * length : (q + 1) * length, m * length : (m + 1) * length
            ]
    s_ref[...] = jnp.dot(u_ref[...], mats[2 * inverse + 1], preferred_element_type=jnp.float32)


def propagate(product, mats, fresnel_ref, v_in, v_ref, u_ref, s_ref):
    length = mats.shape[1] // 2
    transform(mats, 0, v_in, u_ref, s_ref)
    for i in range(0, length, STEP):
        at = pl.ds(i, STEP)
        kr, ki = fresnel_ref[0, at, :], fresnel_ref[1, at, :]
        for m in range(v_ref.shape[1] // length):
            put_v(v_ref, length, m, i, *product(kr, ki, *get_s(s_ref, length, m, i)))
    transform(mats, 1, v_ref, u_ref, s_ref)


def join(own, piece, i, row):
    return jnp.where(lines(own.shape[1]) >= row - i, own, piece.astype(jnp.float32))


def pattern_kernel(sizes, *refs):
    n_scan, n_obj, tile_cols = sizes
    info, mats, fresnel_ref, p_ref, xo_ref, piece, own_ref = refs[:7]
    others = refs[7 : 6 + n_scan]
    grad_ref, keep_ref, give_ref, v_ref, u_ref, s_ref, x_ref, a_ref, meas_ref = refs[6 + n_scan :]
    modes, _, length, _ = p_ref.shape
    me = lax.axis_index("scan")
    core, chip, chips = lax.rem(me, CORES), lax.div(me, CORES), n_scan // CORES
    source, slot, row, col = assigned(info, OWN, me, n_scan)
    _, off = column_block(col, length, tile_cols)

    @pl.when(slot == 0)
    def _():
        meas_ref[...] = own_ref[0]

    for k in range(1, n_scan):
        @pl.when((slot == 1) & (source == lax.rem(me - k + n_scan, n_scan)))
        def _():
            meas_ref[...] = others[k - 1][...]

    for l in range(x_ref.shape[0]):
        for q in range(2):
            for i in range(0, length, STEP):
                at = pl.ds(i, STEP)
                x_ref[l, q, at, :] = join(xo_ref[l, q, at, :], piece[l, q, at, :], i, row)
    for i in range(0, length, STEP):
        at = pl.ds(i, STEP)
        xr, xi = x_ref[0, 0, at, :], x_ref[0, 1, at, :]
        for m in range(modes):
            put_v(v_ref, length, m, i, *mul(p_ref[m, 0, at, :], p_ref[m, 1, at, :], xr, xi))
    propagate(mul, mats, fresnel_ref, v_ref, v_ref, u_ref, s_ref)
    for i in range(0, length, STEP):
        at = pl.ds(i, STEP)
        xr, xi = x_ref[1, 0, at, :], x_ref[1, 1, at, :]
        for m in range(modes):
            ar, ai = get_s(s_ref, length, m, i)
            a_ref[m, 0, at, :] = ar
            a_ref[m, 1, at, :] = ai
            put_v(v_ref, length, m, i, *mul(ar, ai, xr, xi))
    transform(mats, 0, v_ref, u_ref, s_ref)
    for i in range(0, length, STEP):
        misfit = -meas_ref[pl.ds(i, STEP), :].astype(jnp.float32)
        for m in range(modes):
            fr, fi = get_s(s_ref, length, m, i)
            misfit += fr * fr + fi * fi
        for m in range(modes):
            fr, fi = get_s(s_ref, length, m, i)
            put_v(v_ref, length, m, i, misfit * fr, misfit * fi)
    transform(mats, 1, v_ref, u_ref, s_ref)
    for i in range(0, length, STEP):
        at = pl.ds(i, STEP)
        gr = gi = 0.0
        for m in range(modes):
            cr, ci = get_s(s_ref, length, m, i)
            dr, di = cmul(a_ref[m, 0, at, :], a_ref[m, 1, at, :], cr, ci)
            gr, gi = gr + dr, gi + di
            put_v(v_ref, length, m, i, *cmul(x_ref[1, 0, at, :], x_ref[1, 1, at, :], cr, ci))
        grad_ref[1, 0, at, :] = gr.astype(grad_ref.dtype)
        grad_ref[1, 1, at, :] = gi.astype(grad_ref.dtype)
    propagate(cmul, mats, fresnel_ref, v_ref, v_ref, u_ref, s_ref)
    for i in range(0, length, STEP):
        at = pl.ds(i, STEP)
        gr = gi = 0.0
        for m in range(modes):
            cr, ci = get_s(s_ref, length, m, i)
            dr, di = cmul(p_ref[m, 0, at, :], p_ref[m, 1, at, :], cr, ci)
            gr, gi = gr + dr, gi + di
            a_ref[m, 0, at, :], a_ref[m, 1, at, :] = cmul(x_ref[0, 0, at, :], x_ref[0, 1, at, :], cr, ci)
        grad_ref[0, 0, at, :] = gr.astype(grad_ref.dtype)
        grad_ref[0, 1, at, :] = gi.astype(grad_ref.dtype)
    row_back = lax.rem(length - row, length)
    col_back = lax.rem(2 * length - off, length)
    per_row, per_col = length // n_obj, length // n_scan
    lane = lax.broadcasted_iota(jnp.int32, (length, 128), 1)
    for m in range(modes):
        for q in range(2):
            a_ref[m, q] = pltpu.roll(pltpu.roll(a_ref[m, q], row_back, 0), col_back, 1)
        for s in range(n_scan):
            first, shift = s * per_col // 128 * 128, s * per_col % 128
            real = a_ref[m, 0, :, first : first + 128]
            imag = a_ref[m, 1, :, first : first + 128]
            real = pltpu.roll(real, (128 - shift) % 128, 1) if shift else real
            imag = pltpu.roll(imag, (per_col - shift) % 128, 1) if shift != per_col else imag
            both = jnp.where(lane < per_col, real, imag)[:, : 2 * per_col]
            apart = lax.rem(s // CORES - chip + chips, chips)
            for mine, ref in ((core, keep_ref), (1 - core, give_ref)):
                @pl.when(mine == s % CORES)
                def _():
                    for o in range(n_obj):
                        ref[o, apart, m] = both[o * per_row : (o + 1) * per_row].astype(ref.dtype)


def place_kernel(sizes, kinds, parts, factor, *refs):
    n_scan, _, tile_cols = sizes
    chips = n_scan // CORES
    layers = refs[-4].shape[0]
    info = refs[0]
    shares = refs[1 : 1 + chips]
    patches = refs[1 + chips : -4]
    out_ref, probe_out, held, sems = refs[-4:]
    _, _, rows, width = out_ref.shape
    length = patches[0].shape[-1]
    me = lax.axis_index("scan")
    blocks = width // length
    first_block = me * blocks
    spots = []
    for index, (tile, flip, jump) in enumerate(kinds):
        source = lax.rem((me ^ flip) - CORES * jump + n_scan, n_scan)
        _, _, row, col = assigned(info, tile, source, n_scan)
        base, off = column_block(col, length, tile_cols)
        top, bottom = (row, rows) if tile == OWN else (0, row)
        meets = (base + 1 >= first_block) & (base < first_block + blocks)
        copies = [
            pltpu.make_async_copy(
                patches[number] if part is None else patches[number].at[part], held.at[index, l], sems.at[index, l]
            )
            for l, (number, part) in enumerate(parts[index])
        ]
        spots.append((base, off, top, bottom, meets, copies))

        @pl.when(meets)
        def _():
            for copy in copies:
                copy.start()

    out_ref[...] = jnp.zeros(out_ref.shape, jnp.float32)
    per_col = probe_out.shape[3]
    for m in range(probe_out.shape[0]):
        total = sum(share[m].astype(jnp.float32) for share in shares) * factor
        probe_out[m, 0] = total[:, :per_col]
        probe_out[m, 1] = total[:, per_col:]
    lane, line = lanes(length), lines(length)
    for index, (base, off, top, bottom, meets, copies) in enumerate(spots):
        @pl.when(meets)
        def _():
            for copy in copies:
                copy.wait()
        for block in range(blocks):
            first, second = base == first_block + block, base + 1 == first_block + block
            left = jnp.where(first, off, 0)
            right = jnp.where(first, length, off)

            @pl.when(first | second)
            def _():
                cols = (lane >= left) & (lane < right)
                spot = slice(block * length, (block + 1) * length)
                for i in range(0, rows, STEP):
                    mask = cols & (line >= top - i) & (line < bottom - i)
                    at = pl.ds(i, STEP)
                    for l in range(layers):
                        for q in range(2):
                            value = held[index, l, q, at, :].astype(jnp.float32)
                            out_ref[l, q, at, spot] += jnp.where(mask, value, 0.0)


def body(object_slices, probe, measured, positions, counts):
    layers, _, tile_rows, tile_cols = object_slices.shape
    modes, _, length, _ = probe.shape
    slots = measured.shape[2]
    n_scan, n_obj = lax.axis_size("scan"), lax.axis_size("obj")
    chips = n_scan // CORES
    sizes = (n_scan, n_obj, tile_cols)
    smem = pl.BlockSpec(memory_space=pltpu.SMEM)
    vmem = pl.BlockSpec(memory_space=pltpu.VMEM)
    hbm = pl.BlockSpec(memory_space=pltpu.HBM)
    real, half = jnp.float32, jnp.bfloat16

    def call(kernel, outs, ins, scratch, name, flops, limit, *args):
        return pl.pallas_call(
            functools.partial(kernel[0], sizes, *kernel[1:]),
            out_shape=[jax.ShapeDtypeStruct(*o) for o in outs],
            in_specs=ins,
            out_specs=[vmem] * len(outs),
            scratch_shapes=scratch,
            compiler_params=pltpu.CompilerParams(vmem_limit_bytes=limit * MIB),
            cost_estimate=pl.CostEstimate(flops=flops, bytes_accessed=4 * MIB, transcendentals=0),
            name=name,
        )(*args)

    def across(block):
        return send(block, lambda s, o: (s ^ 1, o))

    def along(block, jump):
        return send(block, lambda s, o: (s + CORES * jump, o)) if jump else block

    def outward(block, sign):
        return send(block, lambda s, o: (s, o + sign))

    info = jnp.concatenate([counts[0], positions[0, 0].reshape(-1), jnp.zeros((3,), jnp.int32)])
    both = jnp.concatenate([info, send(info, lambda s, o: (s, o + 1))])
    info = lax.all_to_all(jnp.broadcast_to(both, (n_scan, 1, 16)), "scan", 0, 0, tiled=True)

    measured, info = lax.optimization_barrier((measured, info))
    second = measured[0, 0, 1]
    others = [send(second, lambda s, o, k=k: (s + k, o)) for k in range(1, n_scan)]

    patch_shape = (layers, 2, length, length)
    field_shape = (modes, 2, length, length)
    wide = [pltpu.VMEM((layers, 2, tile_rows, 2 * length), real), pltpu.SemaphoreType.DMA((layers, 2, 2))]
    (piece,) = call(
        (pick_kernel, False), [(patch_shape, half)], [smem, hbm], wide, "cut", MIB, LARGE, info, object_slices
    )
    piece = outward(piece, -1)
    (own_part,) = call(
        (pick_kernel, True), [(patch_shape, real)], [smem, hbm], wide, "own", MIB, MIDDLE, info, object_slices
    )
    mats, turned = call(
        (prep_kernel,),
        [((4, 2 * length, 2 * length), half), (field_shape, real)],
        [smem, vmem, vmem],
        [],
        "prep",
        MIB,
        SMALL,
        info,
        probe,
        dft_tables(length),
    )
    chunk_shape = (n_obj, chips, modes, length // n_obj, 2 * (length // n_scan))
    grad, keep, give = call(
        (pattern_kernel,),
        [(patch_shape, half), (chunk_shape, half), (chunk_shape, half)],
        [smem] + [vmem] * (5 + n_scan),
        [
            pltpu.VMEM((2 * length, modes * length), half),
            pltpu.VMEM((modes * length, 2 * length), half),
            pltpu.VMEM((modes * length, 2 * length), real),
            pltpu.VMEM(patch_shape, real),
            pltpu.VMEM(field_shape, real),
            pltpu.VMEM((length, length), measured.dtype),
        ],
        "pattern",
        3 * 2 * 2 * modes * 8 * length**3,
        SMALL,
        info,
        mats,
        fresnel_tables(length),
        turned,
        own_part,
        piece,
        measured[0, 0],
        *others,
    )

    there = outward(grad, 1)
    chunks = (keep.astype(real) + across(give).astype(real)).astype(half)
    first, chunks = lax.optimization_barrier((grad, chunks))
    here = [grad] + [along(first, j) for j in range(1, chips)]
    x_first = [outward(block[1], 1) for block in here[1:]]
    obj_first = [along(there[0], j) for j in range(1, chips)]
    held = here + [there] + x_first + obj_first
    held += [across(block) for block in held]
    kinds, parts = [], []
    for flip in range(2):
        start = flip * (len(held) // 2)
        for j in range(chips):
            kinds.append((OWN, flip, j))
            parts.append([(start + j, l) for l in range(layers)])
        for j in range(chips):
            kinds.append((PREVIOUS, flip, j))
            if j == 0:
                parts.append([(start + chips, l) for l in range(layers)])
            else:
                parts.append([(start + 2 * chips - 1 + j, None), (start + chips + j, None)])
    chunks = lax.all_to_all(chunks, "obj", 0, 0, tiled=True)
    chunks = jnp.sum(chunks.astype(real), axis=0).astype(half)
    shares = [along(chunks[j], j) for j in range(chips)]
    factor = 1.0 / math.sqrt(n_scan * n_obj * slots // 2)
    object_grad, probe_grad = call(
        (place_kernel, kinds, parts, factor),
        [
            ((layers, 2, tile_rows, tile_cols // n_scan), real),
            ((modes, 2, length // n_obj, length // n_scan), real),
        ],
        [smem] + [vmem] * chips + [hbm] * len(held),
        [
            pltpu.VMEM((2 * n_scan, layers, *patch_shape[1:]), half),
            pltpu.SemaphoreType.DMA((2 * n_scan, layers)),
        ],
        "place",
        MIB,
        MIDDLE,
        info,
        *shares,
        *held,
    )
    return (object_grad, probe_grad)


def solution(mesh):
    return jax.shard_map(
        body,
        mesh=mesh,
        in_specs=(
            P(None, None, "obj", None),
            P(),
            P("scan", "obj", None, None, None),
            P("scan", "obj", None, None),
            P("scan", "obj"),
        ),
        out_specs=(P(None, None, "obj", "scan"), P(None, None, "obj", "scan")),
        check_vma=False,
    )
```
